32 devices in a mesh: dp: 8 (over y, x, core), seq: 4 (over z).
Axes of the slice: x: 2, y: 2, z: 4, core: 2. Of those that a mesh axis runs over, the one named last changes fastest.
Arguments:
- tokens: bfloat16 [8, 1024, 1152], P('dp', 'seq'), may hold values from -38 to 38
- doc_ids: int32 [8, 1024], P('dp', 'seq'), may hold values from 0 to 33, as said below
- token_expert: int32 [8, 1024, 1], P('dp', 'seq'), may hold values from 0 to 1; in each aligned block of 256 rows (0 to 255, 256 to 511, ..., all dimensions but the last counted through in order) at most 160 rows name the same one
- out_grad: bfloat16 [8, 1024, 1152], P('dp', 'seq'), may hold values from -38 to 38
- norm_gains: bfloat16 [2, 1152], P(None, 'dp'), may hold values from 0.5 to 1.5
- in_proj: bfloat16 [1152, 4608], P(None, ('dp', 'seq')), may hold values from -0.1875 to 0.1875
- conv_weight: bfloat16 [4, 2304], P(None, ('dp', 'seq')), may hold values from -3 to 3
- conv_bias: bfloat16 [2304], P(('dp', 'seq')), may hold values from -1 to 1
- select_proj: bfloat16 [2304, 104], P(('dp', 'seq')), may hold values from -0.125 to 0.125
- step_proj: bfloat16 [72, 2304], P(None, ('dp', 'seq')), may hold values from -0.75 to 0.75
- step_bias: bfloat16 [2304], P(('dp', 'seq')), may hold values from -7 to -2
- decay_log: bfloat16 [2304, 16], P(('dp', 'seq')), may hold values from -1.59375 to 0.69921875
- skip_gain: bfloat16 [2304], P(('dp', 'seq')), may hold values from 0.25 to 1
- out_proj: bfloat16 [2304, 1152], P(('dp', 'seq')), may hold values from -1 to 1
- router: bfloat16 [1152, 2], P('dp'), may hold values from -0.125 to 0.125
- expert_up: bfloat16 [2, 1152, 3072], P(None, None, ('dp', 'seq')), may hold values from -0.1875 to 0.1875
- expert_down: bfloat16 [2, 3072, 1152], P(None, ('dp', 'seq')), may hold values from -0.4375 to 0.4375
Outputs:
- layer_out: bfloat16 [8, 1024, 1152], P('dp', 'seq')
- tokens_grad: bfloat16 [8, 1024, 1152], P('dp', 'seq')
- gains_grad: float32 [2, 1152], P(None, 'dp')
- in_proj_grad: float32 [1152, 4608], P(None, ('dp', 'seq'))
- conv_weight_grad: float32 [4, 2304], P(None, ('dp', 'seq'))
- conv_bias_grad: float32 [2304], P(('dp', 'seq'))
- select_proj_grad: float32 [2304, 104], P(('dp', 'seq'))
- step_proj_grad: float32 [72, 2304], P(None, ('dp', 'seq'))
- step_bias_grad: float32 [2304], P(('dp', 'seq'))
- decay_log_grad: float32 [2304, 16], P(('dp', 'seq'))
- skip_gain_grad: float32 [2304], P(('dp', 'seq'))
- out_proj_grad: float32 [2304, 1152], P(('dp', 'seq'))
- router_grad: float32 [1152, 2], P('dp')
- expert_up_grad: float32 [2, 1152, 3072], P(None, None, ('dp', 'seq'))
- expert_down_grad: float32 [2, 3072, 1152], P(None, ('dp', 'seq'))
- stats: float32 [3], replicated
The draws below stay inside these ranges and needn't reach their ends.
Inputs may be any that keep to these rules, and one draw needn't show every extreme that they name: `doc_ids`: each packed row starts at document 0, and its numbers never fall and rise by at most one from one position to the next. `token_expert`: of the 256 tokens of one device at most 160 name the same expert, and in every draw the tokens of some device name one expert exactly 160 times.
All inputs are finite; a program needn't handle non-finite values.
Results may differ from the reference program's by a relative error of at most 0.012.
The reference program's roundings to bfloat16 on the way count: a program that leaves them out, or rounds other values in their place, can miss the bound.
Values may be sent and summed in bfloat16 or wider, within the bound.
No kernel may reach another device: no remote copies, remote signals or barrier semaphores. Data moves between devices by JAX's collectives and lax.ppermute only.
A program may use at most 384 MiB of HBM per device.

```python
import math
import jax
import jax.numpy as jnp
import numpy as np
from jax import lax

MODEL_WIDTH = 1152
DI = 2304
R = 72
NS = 16
KC = 4
FF = 3072
EXPERT_COUNT = 2
DEVICE_TOKENS = 256
EXPERT_SLOTS = 160
PACKED_ROWS = 8
ROW_LENGTH = 1024


def ramp_draw(key, salt):
    key = jax.random.fold_in(key, salt)
    first_moment = jax.random.fold_in(key, 0)
    token_position = jnp.arange(PACKED_ROWS * ROW_LENGTH, dtype=jnp.float32).reshape(PACKED_ROWS, ROW_LENGTH, 1)
    position_ramp = 1.0 + 2.0 * token_position / (PACKED_ROWS * ROW_LENGTH - 1)
    base_offset = jnp.clip(jax.random.normal(first_moment, (PACKED_ROWS, ROW_LENGTH, MODEL_WIDTH), jnp.float32), -6.0, 6.0)
    values = base_offset * position_ramp
    return values.astype(jnp.bfloat16)


def draw_tokens(key, part):
    return ramp_draw(key, 11)


def draw_out_grad(key, part):
    return ramp_draw(key, 23)


def draw_doc_ids(key, part):
    key = jax.random.fold_in(key, 37)
    key_start, ending_key, break_key, key_row = jax.random.split(key, 4)
    limit = DEVICE_TOKENS // 8 + 1
    full_row = jax.random.randint(key_row, (), 0, PACKED_ROWS)
    is_full = (jnp.arange(PACKED_ROWS, dtype=jnp.int32) == full_row)[:, None]
    begin = jax.random.randint(key_start, (PACKED_ROWS, 1), 0, DEVICE_TOKENS // 2)
    begin = jnp.where(is_full, DEVICE_TOKENS // 2 - 1, begin)
    finish_index = jax.random.randint(ending_key, (PACKED_ROWS, 1), ROW_LENGTH - DEVICE_TOKENS // 2, ROW_LENGTH + 1)
    token_position = jnp.arange(ROW_LENGTH, dtype=jnp.int32)[None, :]
    document_breaks = jax.random.randint(break_key, (PACKED_ROWS, ROW_LENGTH), 0, 8) == 0
    outside = (token_position < begin) | (token_position > finish_index)
    forced = is_full & (token_position <= limit)
    flags = (token_position == 0) | (token_position == begin) | (token_position == finish_index) | document_breaks & outside | forced
    numbers = jnp.cumsum(flags.astype(jnp.int32), axis=1) - 1
    return jnp.minimum(numbers, limit).astype(jnp.int32)


def level_of(key, extent, pieces, least, largest):
    def one(axis_at, parts):
        heights = jax.random.uniform(jax.random.fold_in(jax.random.fold_in(key, 6), axis_at), (parts,), jnp.float32, least / len(pieces), largest / len(pieces))
        return jnp.repeat(jnp.exp(heights), extent[axis_at] // parts).reshape((-1,) + (1,) * (len(extent) - axis_at - 1))

    loudness = one(*pieces[0])
    for cut in pieces[1:]:
        loudness = loudness * one(*cut)
    return loudness


def shared_out(key, own, number, rows, amount, top, most, skew):
    ranking = jax.random.permutation(key, amount)
    heavy_load, usual = shares(amount, rows * top, most, skew, True), shares(amount, rows * top, most, skew, False)
    places = jnp.arange(amount)

    def named(tallies, rotation):
        used = int((tallies > 0).sum())
        fixed = max(1, used // 4)
        moved = fixed + (places - fixed + rotation * (used - fixed)) % max(1, amount - fixed)
        return jnp.zeros((amount,), jnp.int32).at[ranking[jnp.where(places < fixed, places, moved)]].set(jnp.asarray(tallies, jnp.int32))

    tallies = jnp.where(number % 4 == 0, named(heavy_load, number // 4), named(usual, number - number // 4 - 1))
    mixed = jax.random.permutation(jax.random.fold_in(own, 3), amount)
    source_of, sink = mixed[0:amount // 2 * 2:2], mixed[1:amount // 2 * 2:2]
    room = jnp.minimum(tallies[source_of] - 1, most - tallies[sink]) // 2
    room = jnp.where((source_of == ranking[0]) | (sink == ranking[0]) | (tallies[sink] == 0), 0, jnp.maximum(room, 0))
    moved = jax.random.randint(jax.random.fold_in(own, 4), (amount // 2,), 0, 1 << 20) % (room + 1)
    tallies = tallies.at[source_of].add(-moved).at[sink].add(moved)
    items = jnp.searchsorted(jnp.cumsum(tallies), jnp.arange(rows * top), side="right").astype(jnp.int32)
    grid = items.reshape(top, rows).T
    grid = grid[jax.random.permutation(jax.random.fold_in(own, 1), rows)]
    rotation = jax.random.randint(jax.random.fold_in(own, 2), (rows, 1), 0, top)
    return jnp.take_along_axis(grid, (jnp.arange(top)[None, :] + rotation) % top, axis=1)


def shares(amount, total, bound, slope, full):
    weights = [(1 << 20) // math.isqrt(rank ** slope) + 1 for rank in range(1, amount + 1)]
    largest = bound if full else min(bound, max(-(-total // amount), total * weights[0] // sum(weights)))
    least = 1 if total - largest >= amount - 1 else 0
    given, surplus = [largest] + [least] * (amount - 1), total - largest - least * (amount - 1)
    while surplus > 0:
        movable = [i for i in range(1, amount) if given[i] < largest] or [i for i in range(1, amount) if given[i] < bound]
        pool, left = sum([weights[i] for i in movable]), surplus
        for i in movable:
            extra = min(bound - given[i], max(1, left * weights[i] // pool), surplus)
            given[i] = given[i] + extra
            surplus = surplus - extra
    return np.array(given)


def noise(own_key, dims, deviation, reach, shards=(), held_as=jnp.bfloat16):
    values = deviation * jax.random.normal(own_key, dims, jnp.float32)
    if shards:
        values = values * level_of(own_key, dims, shards, -0.22, 0.18)
    return jnp.clip(values, -reach, reach).astype(held_as)


def setup_inputs(seed: int = 0) -> dict:
    splits = jax.random.split(jax.random.key(seed), 18)
    tokens = draw_tokens(jax.random.fold_in(splits[17], 71), 0)
    doc_ids = draw_doc_ids(jax.random.fold_in(splits[17], 71), 0)
    token_expert_keys = jax.random.split(jax.random.fold_in(splits[2], 1), PACKED_ROWS * ROW_LENGTH // DEVICE_TOKENS)
    token_expert_turns = jax.random.permutation(jax.random.fold_in(splits[2], 3), PACKED_ROWS * ROW_LENGTH // DEVICE_TOKENS)
    token_expert = jax.vmap(lambda own, number: shared_out(jax.random.fold_in(splits[2], 2), own, number, DEVICE_TOKENS, EXPERT_COUNT, 1, EXPERT_SLOTS, 1))(token_expert_keys, token_expert_turns).reshape((PACKED_ROWS, ROW_LENGTH, 1))
    out_grad = draw_out_grad(jax.random.fold_in(splits[17], 71), 0)
    norm_gains = jnp.clip(1.0 + 0.1 * jax.random.normal(splits[4], (2, MODEL_WIDTH), jnp.float32), 0.5, 1.5).astype(jnp.bfloat16)
    in_proj = noise(splits[5], (MODEL_WIDTH, 2 * DI), MODEL_WIDTH ** -0.5, 0.1875, ((1, 32),))
    conv_weight = noise(splits[6], (KC, DI), 0.5, 3.0, ((1, 32),))
    conv_bias = noise(splits[7], (DI,), 0.2, 1.0, ((0, 32),))
    select_proj = noise(splits[8], (DI, R + 2 * NS), DI ** -0.5, 0.125, ((0, 32),))
    step_proj = noise(splits[9], (R, DI), R ** -0.5, 0.75, ((1, 32),))
    step_bias = jnp.clip(-7.0 + 5.0 * jax.random.uniform(splits[10], (DI,), jnp.float32) ** level_of(splits[10], (DI,), ((0, 32),), -0.2, 0.2), -7.0, -2.0).astype(jnp.bfloat16)
    decay_log = jnp.clip(-1.59375 + 2.2929688 * jax.random.uniform(splits[11], (DI, NS), jnp.float32) ** level_of(splits[11], (DI, NS), ((0, 32),), -0.2, 0.2), -1.59375, 0.69921875).astype(jnp.bfloat16)
    skip_gain = jnp.clip(0.25 + 0.75 * jax.random.uniform(splits[12], (DI,), jnp.float32) ** level_of(splits[12], (DI,), ((0, 32),), -0.2, 0.2), 0.25, 1.0).astype(jnp.bfloat16)
    out_proj = noise(splits[13], (DI, MODEL_WIDTH), (DI // 64) ** -0.5, 1.0, ((0, 32),))
    router = noise(splits[14], (MODEL_WIDTH, EXPERT_COUNT), (2 * MODEL_WIDTH) ** -0.5, 0.125, ((0, 8),))
    expert_up = noise(splits[15], (EXPERT_COUNT, MODEL_WIDTH, FF), MODEL_WIDTH ** -0.5, 0.1875, ((2, 32),))
    expert_down = noise(splits[16], (EXPERT_COUNT, FF, MODEL_WIDTH), (FF // 16) ** -0.5, 0.4375, ((1, 32),))
    return {"tokens": tokens, "doc_ids": doc_ids, "token_expert": token_expert, "out_grad": out_grad, "norm_gains": norm_gains, "in_proj": in_proj, "conv_weight": conv_weight, "conv_bias": conv_bias, "select_proj": select_proj, "step_proj": step_proj, "step_bias": step_bias, "decay_log": decay_log, "skip_gain": skip_gain, "out_proj": out_proj, "router": router, "expert_up": expert_up, "expert_down": expert_down}


EPS = 1e-05

@jax.custom_vjp
def low(v):
    return lax.optimization_barrier(v.astype(jnp.bfloat16)).astype(jnp.float32)

@jax.custom_vjp
def low_back(v):
    return v

def low_keep(v):
    return (low(v), None)

def low_pass(kept, grad):
    return (grad,)

def back_keep(v):
    return (v, None)

def back_low(kept, grad):
    return (low(grad),)
low.defvjp(low_keep, low_pass)
low_back.defvjp(back_keep, back_low)

def product(left, right):
    return jnp.dot(left, right, precision=lax.Precision.HIGHEST, preferred_element_type=jnp.float32)

def scan_block(state, part, decay_rate):

    def advance(state, item):
        delta_t, inner_t, select_in, select_out, kept_t = item
        state = kept_t * jnp.exp(delta_t[:, None] * decay_rate) * state + (delta_t * inner_t)[:, None] * select_in[None, :]
        return (state, lax.optimization_barrier(jnp.sum(state * select_out[None, :], 1)))
    return lax.scan(advance, state, part)

def row_forward(stream, doc_row, route_row, weights):
    gains, in_proj, conv_weight, conv_bias, select_proj, step_proj, step_bias, decay_log, skip_gain, out_proj, router, expert_up, expert_down = weights
    length = stream.shape[0]
    inv_first = lax.rsqrt(lax.optimization_barrier(jnp.mean(stream * stream, -1, keepdims=True)) + EPS)
    normed = low(stream * inv_first * gains[0])
    proj = low_back(low(product(normed, in_proj)))
    front = proj[:, :DI]
    gate_half = proj[:, DI:]
    pad_ids = jnp.concatenate([jnp.full((KC - 1,), -1, jnp.int32), doc_row.astype(jnp.int32)])
    pad_rows = jnp.concatenate([jnp.zeros((KC - 1, DI), front.dtype), front])
    conv_sum = conv_bias[None, :]
    for k in range(KC):
        match = (pad_ids[k:k + length] == doc_row)[:, None]
        conv_sum = conv_sum + conv_weight[k][None, :] * jnp.where(match, pad_rows[k:k + length], 0.0)
    inner = low(jax.nn.silu(conv_sum))
    select = low_back(product(inner, select_proj))
    steps_low = low(select[:, :R])
    in_select = select[:, R:R + NS]
    out_select = select[:, R + NS:]
    step_pre = low_back(product(steps_low, step_proj))
    delta = jax.nn.softplus(step_pre + step_bias[None, :])
    decay_rate = -jnp.exp(decay_log)
    kept = (pad_ids[KC - 2:KC - 2 + length] == doc_row).astype(front.dtype)
    block = math.gcd(length, 64)
    blocked = tuple((member.reshape((length // block, block) + member.shape[1:]) for member in (delta, inner, in_select, out_select, kept)))
    runner = jax.checkpoint(scan_block)
    _, outputs = lax.scan(lambda state, part: runner(state, part, decay_rate), jnp.zeros((DI, NS), front.dtype), blocked)
    scanned = outputs.reshape(length, DI) + skip_gain[None, :] * inner
    gated = low(scanned * jax.nn.silu(gate_half))
    mixed = low_back(product(gated, out_proj))
    resid = stream + mixed
    inv_second = lax.rsqrt(lax.optimization_barrier(jnp.mean(resid * resid, -1, keepdims=True)) + EPS)
    normed_moe = low(resid * inv_second * gains[1])
    logits = product(normed_moe, router)
    probs = jax.nn.softmax(logits, -1)
    route_hot = (route_row[:, None] == jnp.arange(EXPERT_COUNT)[None, :]).astype(front.dtype)
    chosen = lax.optimization_barrier(jnp.sum(probs * route_hot, 1))
    returned = jnp.zeros_like(stream)
    for expert in range(EXPERT_COUNT):
        hidden = low_back(product(normed_moe, expert_up[expert]))
        active = low(jax.nn.gelu(hidden, approximate=False))
        result = low_back(product(active, expert_down[expert]))
        returned = returned + route_hot[:, expert:expert + 1] * result
    branch = chosen[:, None] * returned
    layer = resid + branch
    squared_values = jnp.stack([jnp.sum(resid * resid), jnp.sum(mixed * mixed), jnp.sum(branch * branch)])
    return (layer, squared_values)

def reference(tokens, doc_ids, token_expert, out_grad, norm_gains, in_proj, conv_weight, conv_bias, select_proj, step_proj, step_bias, decay_log, skip_gain, out_proj, router, expert_up, expert_down):
    weights = tuple((member.astype(jnp.float32) for member in (norm_gains, in_proj, conv_weight, conv_bias, select_proj, step_proj, step_bias, decay_log, skip_gain, out_proj, router, expert_up, expert_down)))
    streams = tokens.astype(jnp.float32)
    routes = token_expert[:, :, 0]

    def whole(streams, weights):

        def per_row(item):
            stream, doc_row, route_row = item
            return row_forward(stream, doc_row, route_row, weights)
        layers, squared_values = lax.map(jax.checkpoint(per_row), (streams, doc_ids, routes))
        return (layers, lax.optimization_barrier(jnp.sum(squared_values, 0)))
    layers, pullback, squared_values = jax.vjp(whole, streams, weights, has_aux=True)
    stream_grad, weight_grads = pullback(out_grad.astype(jnp.float32))
    stats = jnp.sqrt(squared_values / (PACKED_ROWS * ROW_LENGTH * MODEL_WIDTH))
    return (layers.astype(jnp.bfloat16), stream_grad.astype(jnp.bfloat16), weight_grads[0], weight_grads[1], weight_grads[2], weight_grads[3], weight_grads[4], weight_grads[5], weight_grads[6], weight_grads[7], weight_grads[8], weight_grads[9], weight_grads[10], weight_grads[11], weight_grads[12], stats)
```

```python
import functools, math
import jax
import jax.numpy as jnp
from jax import lax
from jax.experimental import pallas as pl
from jax.experimental.pallas import tpu as pltpu
from jax.sharding import PartitionSpec as P

NS = 16
SEG = 8
LANE = 128
FAR = 1e30


def spread_columns(wide, columns):
    for n in range(NS):
        wide[n] = jnp.broadcast_to(columns[:, n : n + 1], wide.shape[1:])


def rows_of(i):
    return pl.ds(pl.multiple_of(i * SEG, SEG), SEG)


def rate_rows(rate):
    return [jnp.broadcast_to(rate[n : n + 1, :], (SEG, rate.shape[1])) for n in range(NS)]


def tiled_lanes(block, width):
    return block if width == LANE else jnp.concatenate([block] * (width // LANE), 1)


def prefix_pairs(decay, value, reverse):
    place = lax.broadcasted_iota(jnp.int32, decay.shape, 0)

    def shifted(array, by, fill):
        if reverse:
            return jnp.where(place < SEG - by, pltpu.roll(array, SEG - by, 0), fill)
        return jnp.where(place >= by, pltpu.roll(array, by, 0), fill)

    for by in (1, 2, 4):
        value = decay * shifted(value, by, 0.0) + value
        decay = decay * shifted(decay, by, 1.0)
    last = slice(0, 1) if reverse else slice(SEG - 1, SEG)
    return shifted(decay, 1, 1.0), shifted(value, 1, 0.0), decay[last], value[last]


def ends_kernel(
    reverse, delta, driven, kept, select, rate, pre_decay, pre_value, all_decay, all_value, wide
):
    @pl.when(pl.program_id(0) == 0)
    def _():
        spread_columns(wide, select)

    width = delta.shape[1]
    length = delta.shape[0] // SEG
    rates = rate_rows(rate)
    zero = jnp.zeros((SEG, width), jnp.float32)

    def step(k, carry):
        total, states = carry
        i = length - 1 - k if reverse else k
        rows = rows_of(i)
        reach = jnp.where(tiled_lanes(kept[rows, :], width) > 0, delta[rows, :], FAR)
        drive = driven[rows, :]
        new = []
        for n in range(NS):
            factor = jnp.exp2(reach * rates[n])
            term = drive * tiled_lanes(wide[n, rows, :], width)
            new.append(factor * (states[n] + term) if reverse else factor * states[n] + term)
        return total + reach, tuple(new)

    total, states = lax.fori_loop(0, length, step, (zero, (zero,) * NS))
    for n in range(NS):
        before_decay, before_value, whole_decay, whole_value = prefix_pairs(
            jnp.exp2(total * rates[n]), states[n], reverse
        )
        pre_decay[n] = before_decay
        pre_value[n] = before_value
        all_decay[n : n + 1, :] = whole_decay
        all_value[n : n + 1, :] = whole_value


def output_kernel(
    delta, driven, inner, gate, kept, in_select, out_select, rate, skip, pre_decay, pre_value,
    entry, scanned, gated, wide_in, wide_out,
):
    @pl.when(pl.program_id(0) == 0)
    def _():
        spread_columns(wide_in, in_select)
        spread_columns(wide_out, out_select)

    width = delta.shape[1]
    length = delta.shape[0] // SEG
    rates = rate_rows(rate)
    start = tuple(pre_decay[n] * entry[n : n + 1, :] + pre_value[n] for n in range(NS))

    def step(i, states):
        rows = rows_of(i)
        reach = jnp.where(tiled_lanes(kept[rows, :], width) > 0, delta[rows, :], FAR)
        drive = driven[rows, :]
        new, parts = [], [0.0] * 4
        for n in range(NS):
            state = jnp.exp2(reach * rates[n]) * states[n] + drive * tiled_lanes(
                wide_in[n, rows, :], width
            )
            parts[n % 4] = parts[n % 4] + state * tiled_lanes(wide_out[n, rows, :], width)
            new.append(state)
        scanned[rows, :] = (parts[0] + parts[1]) + (parts[2] + parts[3])
        return tuple(new)

    lax.fori_loop(0, length, step, start)
    value = scanned[...] + skip[...] * inner[...].astype(jnp.float32)
    scanned[...] = value
    half = gate[...].astype(jnp.float32)
    gated[...] = (value * (half * jax.nn.sigmoid(half))).astype(jnp.bfloat16)


def adjoint_kernel(
    delta, driven, inner, grad, kept, in_select, out_select, rate, pre_decay, pre_value, entry,
    post_decay, post_value, exit_, inner_grad, delta_grad, rate_sum, in_grad, out_grad,
    states, wide_in, wide_out, in_total, out_total,
):
    j = pl.program_id(0)

    @pl.when(j == 0)
    def _():
        spread_columns(wide_in, in_select)
        spread_columns(wide_out, out_select)
        in_total[...] = jnp.zeros_like(in_total)
        out_total[...] = jnp.zeros_like(out_total)

    width = delta.shape[1]
    length = delta.shape[0] // SEG
    rates = rate_rows(rate)
    start = tuple(pre_decay[n] * entry[n : n + 1, :] + pre_value[n] for n in range(NS))

    def folded(value):
        return sum(value[:, k : k + LANE] for k in range(0, width, LANE))

    def advance(i, carry):
        rows = rows_of(i)
        reach = jnp.where(tiled_lanes(kept[rows, :], width) > 0, delta[rows, :], FAR)
        drive, grad_t = driven[rows, :], grad[rows, :]
        new = []
        for n in range(NS):
            states[i, n] = carry[n]
            state = jnp.exp2(reach * rates[n]) * carry[n] + drive * tiled_lanes(
                wide_in[n, rows, :], width
            )
            out_total[n, rows, :] = out_total[n, rows, :] + folded(grad_t * state)
            new.append(state)
        return tuple(new)

    lax.fori_loop(0, length, advance, start)
    back = tuple(post_decay[n] * exit_[n : n + 1, :] + post_value[n] for n in range(NS))
    zero = jnp.zeros((SEG, width), jnp.float32)

    def retreat(k, carry):
        backs, sums = carry
        i = length - 1 - k
        rows = rows_of(i)
        step_t = delta[rows, :]
        reach = jnp.where(tiled_lanes(kept[rows, :], width) > 0, step_t, FAR)
        drive, grad_t = driven[rows, :], grad[rows, :]
        new_backs, new_sums = [], []
        weighted, slope = [0.0] * 2, [0.0] * 2
        for n in range(NS):
            adjoint = grad_t * tiled_lanes(wide_out[n, rows, :], width) + backs[n]
            passed = jnp.exp2(reach * rates[n]) * adjoint
            through = passed * states[i, n]
            weighted[n % 2] = weighted[n % 2] + adjoint * tiled_lanes(wide_in[n, rows, :], width)
            slope[n % 2] = slope[n % 2] + through * rates[n]
            in_total[n, rows, :] = in_total[n, rows, :] + folded(adjoint * drive)
            new_backs.append(passed)
            new_sums.append(sums[n] + through * step_t)
        all_weighted = weighted[0] + weighted[1]
        inner_grad[rows, :] = all_weighted * step_t
        delta_grad[rows, :] = all_weighted * inner[rows, :] + (slope[0] + slope[1]) * math.log(2.0)
        return tuple(new_backs), tuple(new_sums)

    _, sums = lax.fori_loop(0, length, retreat, (back, (zero,) * NS))
    for n in range(NS):
        rate_sum[n : n + 1, :] = jnp.sum(sums[n], 0, keepdims=True)

    @pl.when(j == pl.num_programs(0) - 1)
    def _():
        place = lax.broadcasted_iota(jnp.int32, in_grad.shape, 1)
        for total, result in ((in_total, in_grad), (out_total, out_grad)):
            value = jnp.zeros(result.shape, jnp.float32)
            for n in range(NS):
                column = jnp.sum(total[n], 1, keepdims=True)
                value = jnp.where(place == n, column, value)
            result[...] = value


def column_specs(rows, width):
    return (
        pl.BlockSpec((rows, width), lambda j: (0, j)),
        pl.BlockSpec((rows, LANE), lambda j: (0, 0)),
        pl.BlockSpec((rows, NS), lambda j: (0, 0)),
        pl.BlockSpec((NS, width), lambda j: (0, j)),
        pl.BlockSpec((NS, SEG, width), lambda j: (0, 0, j)),
        pl.BlockSpec((1, width), lambda j: (0, j)),
    )


def params(mib):
    return pltpu.CompilerParams(
        dimension_semantics=("arbitrary",), vmem_limit_bytes=mib * 2**20
    )


def segment_ends(delta, driven, kept, select, rate, reverse, width=LANE):
    rows, channels = delta.shape
    block, flag, columns, state, segments, _ = column_specs(rows, width)
    return pl.pallas_call(
        functools.partial(ends_kernel, reverse),
        grid=(channels // width,),
        in_specs=[block, block, flag, columns, state],
        out_specs=[segments, segments, state, state],
        out_shape=[jax.ShapeDtypeStruct((NS, SEG, channels), jnp.float32)] * 2
        + [jax.ShapeDtypeStruct((NS, channels), jnp.float32)] * 2,
        scratch_shapes=[pltpu.VMEM((NS, rows, LANE), jnp.float32)],
        compiler_params=params(24),
    )(delta, driven, kept, select, rate)


def scan_output(
    delta, driven, inner, gate, kept, in_select, out_select, rate, skip, pre, entry, width=LANE
):
    rows, channels = delta.shape
    block, flag, columns, state, segments, line = column_specs(rows, width)
    wide = pltpu.VMEM((NS, rows, LANE), jnp.float32)
    return pl.pallas_call(
        output_kernel,
        grid=(channels // width,),
        in_specs=[block] * 4 + [flag, columns, columns, state, line, segments, segments, state],
        out_specs=[block, block],
        out_shape=[
            jax.ShapeDtypeStruct((rows, channels), jnp.float32),
            jax.ShapeDtypeStruct((rows, channels), jnp.bfloat16),
        ],
        scratch_shapes=[wide, wide],
        compiler_params=params(24),
    )(delta, driven, inner, gate, kept, in_select, out_select, rate, skip, *pre, entry)


def scan_adjoint(
    delta, driven, inner, grad, kept, in_select, out_select, rate, pre, entry, post, exit_,
    width=LANE,
):
    rows, channels = delta.shape
    block, flag, columns, state, segments, _ = column_specs(rows, width)
    wide = pltpu.VMEM((NS, rows, LANE), jnp.float32)
    return pl.pallas_call(
        adjoint_kernel,
        grid=(channels // width,),
        in_specs=[block] * 4
        + [flag, columns, columns, state, segments, segments, state, segments, segments, state],
        out_specs=[block, block, state, columns, columns],
        out_shape=[jax.ShapeDtypeStruct((rows, channels), jnp.float32)] * 2
        + [jax.ShapeDtypeStruct((NS, channels), jnp.float32)]
        + [jax.ShapeDtypeStruct((rows, NS), jnp.float32)] * 2,
        scratch_shapes=[
            pltpu.VMEM((rows // SEG, NS, SEG, width), jnp.float32),
            wide, wide, wide, wide,
        ],
        compiler_params=params(32),
    )(
        delta, driven, inner, grad, kept, in_select, out_select, rate, *pre, entry, *post, exit_
    )


MODEL_WIDTH = 1152
DI = 2304
R = 72
KC = 4
EXPERT_COUNT = 2
EPS = 1e-05
REACH = KC - 1
BOTH = ("dp", "seq")
HIGHEST = lax.Precision.HIGHEST
F32 = jnp.float32
BF16 = jnp.bfloat16


def passed_along(array, axis, by):
    size = lax.axis_size(axis)
    pairs = [(i, i + by) for i in range(size) if 0 <= i + by < size]
    return lax.ppermute(array, axis, pairs)


def interleave(array):
    split = array.reshape((SEG, array.shape[0] // SEG) + array.shape[1:])
    return split.swapaxes(0, 1).reshape(array.shape)


def in_order(array):
    split = array.reshape((array.shape[0] // SEG, SEG) + array.shape[1:])
    return split.swapaxes(0, 1).reshape(array.shape)


def with_earlier(array, earlier):
    last = array[array.shape[0] - REACH * SEG :].reshape((REACH, SEG) + array.shape[1:])
    front = jnp.concatenate([earlier[:, None], last[:, : SEG - 1]], 1)
    return jnp.concatenate([front.reshape((REACH * SEG,) + array.shape[1:]), array])


def entering(decay, value, reverse):
    size, mine = lax.axis_size("seq"), lax.axis_index("seq")
    gathered = lax.all_gather(jnp.stack([decay, value]).astype(BF16), "seq").astype(F32)
    state = jnp.zeros_like(value)
    for k in range(size):
        at = size - 1 - k if reverse else k
        reached = at > mine if reverse else at < mine
        state = jnp.where(reached, gathered[at, 0] * state + gathered[at, 1], state)
    return state


def silu_slope(value):
    logistic = jax.nn.sigmoid(value)
    return logistic * (1.0 + value * (1.0 - logistic))


def gelu_slope(value):
    return 0.5 * (1.0 + lax.erf(value / math.sqrt(2.0))) + value * jnp.exp(
        -0.5 * value * value
    ) / math.sqrt(2.0 * math.pi)


def dot(left, right, contract, precision=None):
    return lax.dot_general(
        left, right, (contract, ((), ())), precision=precision, preferred_element_type=F32
    )


def gathered(shard):
    return lax.all_gather(shard, BOTH, axis=0, tiled=True)


def scattered(whole):
    return lax.psum_scatter(whole.astype(BF16), BOTH, scatter_dimension=0, tiled=True).astype(F32)


def per_device(
    tokens,
    doc_ids,
    token_expert,
    out_grad,
    norm_gains,
    in_proj,
    conv_weight,
    conv_bias,
    select_proj,
    step_proj,
    step_bias,
    decay_log,
    skip_gain,
    out_proj,
    router,
    expert_up,
    expert_down,
):
    rows = tokens.shape[1]
    slots_per = 5 * rows // (4 * EXPERT_COUNT)
    slots = EXPERT_COUNT * slots_per
    wide = DI // 6

    prior_tokens = passed_along(tokens[0, rows - REACH :], "seq", 1)
    prior_doc = passed_along(doc_ids[0, rows - REACH :], "seq", 1)
    lines = lax.all_gather(jnp.concatenate([norm_gains, router.T]), "dp", axis=1, tiled=True)
    gains_all = lines[:2].astype(F32)
    router_all = lines[2:].astype(F32)

    in_full = gathered(in_proj.T)
    small = jnp.concatenate(
        [
            select_proj,
            step_proj.T,
            decay_log,
            conv_weight.T,
            conv_bias[:, None],
            step_bias[:, None],
            skip_gain[:, None],
        ],
        1,
    )
    small_full = gathered(small)
    select_full = small_full[:, : R + 2 * NS]
    step_full = small_full[:, R + 2 * NS : 2 * R + 2 * NS]
    line_full = small_full[:, 2 * R + 2 * NS :].astype(F32).T
    decay_rate = -jnp.exp(line_full[:NS])
    conv_taps = line_full[NS : NS + KC]
    bias_conv, bias_step, skip_wide = (line_full[NS + KC + k][None] for k in range(3))
    out_full = gathered(out_proj)
    up_full = [gathered(expert_up[e].T) for e in range(EXPERT_COUNT)]
    down_full = [gathered(expert_down[e]) for e in range(EXPERT_COUNT)]

    mine = interleave(tokens[0])
    doc_row = interleave(doc_ids[0])
    route = interleave(token_expert[0, :, 0])
    out_cot = interleave(out_grad[0]).astype(F32)

    extended = jnp.concatenate([mine, prior_tokens, jnp.zeros_like(mine[: SEG - REACH])])
    stream_ext = extended.astype(F32)
    inv_ext = lax.rsqrt(jnp.mean(stream_ext * stream_ext, -1, keepdims=True) + EPS)
    hat_ext = stream_ext * inv_ext
    normed_ext = (hat_ext * gains_all[0]).astype(BF16)
    stream, inv_first, hat_first, normed = (
        a[:rows] for a in (stream_ext, inv_ext, hat_ext, normed_ext)
    )
    proj_ext = dot(normed_ext, in_full, ((1,), (1,))).astype(BF16)
    front = proj_ext[:rows, :DI]
    gate = proj_ext[:rows, DI:]
    ext_ids = with_earlier(doc_row, prior_doc)
    ext_rows = with_earlier(front.astype(F32), proj_ext[rows : rows + REACH, :DI].astype(F32))
    masks = [(ext_ids[k * SEG : k * SEG + rows] == doc_row)[:, None] for k in range(KC)]
    taps = [jnp.where(masks[k], ext_rows[k * SEG : k * SEG + rows], 0.0) for k in range(KC)]
    conv_sum = bias_conv
    for k in range(KC):
        conv_sum = conv_sum + conv_taps[k][None] * taps[k]
    inner = jax.nn.silu(conv_sum).astype(BF16)
    inner_wide = inner.astype(F32)
    select = dot(inner, select_full, ((1,), (0,)))
    steps_low = select[:, :R].astype(BF16)
    in_select = select[:, R : R + NS]
    out_select = select[:, R + NS :]
    step_pre = dot(steps_low, step_full, ((1,), (1,))) + bias_step
    delta = jax.nn.softplus(step_pre)
    driven = delta * inner_wide
    kept = jnp.broadcast_to(masks[REACH - 1].astype(F32), (rows, LANE))
    rate = decay_rate * math.log2(math.e)

    *pre, all_decay, all_state = segment_ends(delta, driven, kept, in_select, rate, False, wide)
    state_in = entering(all_decay, all_state, False)
    scanned, gated = scan_output(
        delta, driven, inner, gate, kept, in_select, out_select, rate, skip_wide, pre, state_in, wide
    )
    mixed = dot(gated, out_full, ((1,), (0,)))
    resid = stream + mixed
    inv_second = lax.rsqrt(jnp.mean(resid * resid, -1, keepdims=True) + EPS)
    hat_second = resid * inv_second
    normed_moe = (hat_second * gains_all[1]).astype(BF16)
    normed_wide = normed_moe.astype(F32)
    logits = dot(normed_wide, router_all, ((1,), (1,)), HIGHEST)
    probs = jax.nn.softmax(logits, -1)
    route_hot = route[:, None] == jnp.arange(EXPERT_COUNT, dtype=jnp.int32)[None, :]
    hot_wide = route_hot.astype(F32)
    chosen = jnp.sum(probs * hot_wide, 1, keepdims=True)
    place = jnp.arange(rows, dtype=jnp.int32)
    lower = (place[:, None] >= place[None, :]).astype(BF16)
    rank_in = dot(lower, route_hot.astype(BF16), ((1,), (0,))) - 1.0
    slot = jnp.sum(rank_in * hot_wide, 1).astype(jnp.int32)
    target = route * slots_per + slot
    pick = (jnp.arange(slots, dtype=jnp.int32)[:, None] == target[None, :]).astype(BF16)

    def to_slots(values):
        placed = dot(pick, values, ((1,), (0,))).astype(BF16)
        return [placed[e * slots_per : (e + 1) * slots_per] for e in range(EXPERT_COUNT)]

    def from_slots(parts):
        return dot(pick.astype(F32), jnp.concatenate(parts), ((0,), (0,)), HIGHEST)

    buffers = to_slots(normed_moe)
    hidden = [dot(buffers[e], up_full[e], ((1,), (1,))) for e in range(EXPERT_COUNT)]
    active = [jax.nn.gelu(h, approximate=False).astype(BF16) for h in hidden]
    returned = from_slots(
        [dot(active[e], down_full[e], ((1,), (0,))) for e in range(EXPERT_COUNT)]
    )
    branch = chosen * returned
    layer_out = (resid + branch).astype(BF16)
    squared_values = jnp.stack(
        [jnp.sum(resid * resid), jnp.sum(mixed * mixed), jnp.sum(branch * branch)]
    )
    chosen_grad = jnp.sum(out_cot * returned, 1, keepdims=True)
    returned_grad = to_slots((chosen * out_cot).astype(BF16))
    grad_down = [dot(active[e], returned_grad[e], ((0,), (0,))) for e in range(EXPERT_COUNT)]
    active_grad = [
        dot(returned_grad[e], down_full[e], ((1,), (1,))) for e in range(EXPERT_COUNT)
    ]
    hidden_grad = [
        (active_grad[e] * gelu_slope(hidden[e])).astype(BF16) for e in range(EXPERT_COUNT)
    ]
    grad_up = [dot(hidden_grad[e], buffers[e], ((0,), (0,))) for e in range(EXPERT_COUNT)]
    expert_sums = [scattered(g) for g in (*grad_down, *grad_up)]
    buffer_grad = from_slots(
        [dot(hidden_grad[e], up_full[e], ((1,), (0,))) for e in range(EXPERT_COUNT)]
    )
    logit_grad = chosen_grad * chosen * (hot_wide - probs)
    grad_router = dot(logit_grad, normed_wide, ((0,), (0,)), HIGHEST)
    moe_grad = buffer_grad + dot(logit_grad, router_all, ((1,), (0,)), HIGHEST)
    second_gain_grad = jnp.sum(moe_grad * hat_second, 0)
    scaled_second = moe_grad * gains_all[1]
    resid_grad = out_cot + inv_second * (
        scaled_second - hat_second * jnp.mean(scaled_second * hat_second, -1, keepdims=True)
    )
    mixed_grad = resid_grad.astype(BF16)
    grad_out = dot(gated, mixed_grad, ((0,), (0,)))
    out_sum = scattered(grad_out)
    gated_grad = dot(mixed_grad, out_full, ((1,), (1,)))
    gate_half = gate.astype(F32)
    scan_grad = gated_grad * jax.nn.silu(gate_half)
    gate_grad = gated_grad * scanned * silu_slope(gate_half)
    grad_skip = jnp.sum(scan_grad * inner_wide, 0)
    *post, back_decay, back_adjoint = segment_ends(
        delta, scan_grad, kept, out_select, rate, True, wide
    )
    adjoint_in = entering(back_decay, back_adjoint, True)
    inner_scan_grad, delta_grad, rate_sum, in_select_grad, out_select_grad = scan_adjoint(
        delta, driven, inner_wide, scan_grad, kept, in_select, out_select, rate, pre, state_in,
        post, adjoint_in, wide,
    )
    grad_decay = rate_sum * decay_rate
    pre_grad = delta_grad * jax.nn.sigmoid(step_pre)
    grad_step_bias = jnp.sum(pre_grad, 0)
    pre_low = pre_grad.astype(BF16)
    grad_step = dot(pre_low, steps_low, ((0,), (0,)))
    steps_grad = dot(pre_low, step_full, ((1,), (0,)))
    select_low = jnp.concatenate([steps_grad, in_select_grad, out_select_grad], 1).astype(BF16)
    grad_select = dot(inner, select_low, ((0,), (0,)))
    inner_grad = (
        scan_grad * skip_wide + inner_scan_grad + dot(select_low, select_full, ((1,), (1,)))
    )
    conv_back = inner_grad * silu_slope(conv_sum)
    grad_lines = jnp.concatenate(
        [
            grad_decay,
            jnp.stack(
                [jnp.sum(conv_back * taps[k], 0) for k in range(KC)]
                + [jnp.sum(conv_back, 0), grad_step_bias, grad_skip]
            ),
        ]
    )
    ext_grad = sum(
        jnp.pad(
            jnp.where(masks[k], conv_back * conv_taps[k][None], 0.0),
            ((k * SEG, (REACH - k) * SEG), (0, 0)),
        )
        for k in range(KC)
    )
    early = ext_grad[: REACH * SEG].reshape(REACH, SEG, DI)
    incoming = passed_along(early[:, 0], "seq", -1)
    tail = jnp.concatenate([early[:, 1:], incoming[:, None]], 1).reshape(REACH * SEG, DI)
    front_grad = ext_grad[REACH * SEG :] + jnp.pad(tail, ((rows - REACH * SEG, 0), (0, 0)))
    proj_grad = jnp.concatenate([front_grad, gate_grad], 1).astype(BF16)
    grad_in = dot(proj_grad, normed, ((0,), (0,)))
    in_sum = scattered(grad_in)
    normed_grad = dot(proj_grad, in_full, ((1,), (0,)))
    first_gain_grad = jnp.sum(normed_grad * hat_first, 0)
    scaled_first = normed_grad * gains_all[0]
    stream_grad = resid_grad + inv_first * (
        scaled_first - hat_first * jnp.mean(scaled_first * hat_first, -1, keepdims=True)
    )

    parts = lax.axis_size("dp")
    repeats = lax.axis_size("seq")
    grad_small = jnp.concatenate([grad_select, grad_step, grad_lines.T], 1)
    columns = grad_small.shape[1]
    unit = DI // (parts * repeats)
    shared = jnp.concatenate([first_gain_grad[None], second_gain_grad[None], grad_router])
    width = MODEL_WIDTH // parts
    shared = shared.reshape(4, parts, width).swapaxes(0, 1).reshape(parts, 1, 4 * width)
    extra = -(-4 * width // unit)
    shared = jnp.pad(shared, ((0, 0), (0, 0), (0, extra * unit - 4 * width)))
    shared = jnp.broadcast_to(shared, (parts, repeats, extra * unit)).reshape(DI, extra)
    small_sum = lax.psum_scatter(
        jnp.concatenate([grad_small, shared], 1), BOTH, scatter_dimension=0, tiled=True
    )
    shared_sum = small_sum[:, columns:].reshape(extra * unit)[: 4 * width].reshape(4, width)
    at = R + 2 * NS
    square_total = lax.psum(squared_values, BOTH)
    stats = jnp.sqrt(square_total / (rows * parts * repeats * MODEL_WIDTH))
    line_sum = small_sum[:, at + R : columns]
    return (
        in_order(layer_out)[None],
        in_order(stream_grad.astype(BF16))[None],
        shared_sum[:2],
        in_sum.T,
        line_sum[:, NS : NS + KC].T,
        line_sum[:, NS + KC],
        small_sum[:, :at],
        small_sum[:, at : at + R].T,
        line_sum[:, NS + KC + 1],
        line_sum[:, :NS],
        line_sum[:, NS + KC + 2],
        out_sum,
        shared_sum[2:].T,
        jnp.stack([s.T for s in expert_sums[EXPERT_COUNT:]]),
        jnp.stack(expert_sums[:EXPERT_COUNT]),
        stats,
    )


def solution(mesh):
    return jax.shard_map(
        per_device,
        mesh=mesh,
        in_specs=(
            P("dp", "seq", None),
            P("dp", "seq"),
            P("dp", "seq", None),
            P("dp", "seq", None),
            P(None, "dp"),
            P(None, ("dp", "seq")),
            P(None, ("dp", "seq")),
            P(("dp", "seq")),
            P(("dp", "seq"), None),
            P(None, ("dp", "seq")),
            P(("dp", "seq")),
            P(("dp", "seq"), None),
            P(("dp", "seq")),
            P(("dp", "seq"), None),
            P("dp", None),
            P(None, None, ("dp", "seq")),
            P(None, ("dp", "seq"), None),
        ),
        out_specs=(
            P("dp", "seq", None),
            P("dp", "seq", None),
            P(None, "dp"),
            P(None, ("dp", "seq")),
            P(None, ("dp", "seq")),
            P(("dp", "seq")),
            P(("dp", "seq"), None),
            P(None, ("dp", "seq")),
            P(("dp", "seq")),
            P(("dp", "seq"), None),
            P(("dp", "seq")),
            P(("dp", "seq"), None),
            P("dp", None),
            P(None, None, ("dp", "seq")),
            P(None, ("dp", "seq"), None),
            P(),
        ),
        check_vma=False,
    )
```

```python
import functools, math
import jax
import jax.numpy as jnp
from jax import lax
from jax.experimental import pallas as pl
from jax.experimental.pallas import tpu as pltpu
from jax.sharding import PartitionSpec as P

NS = 16
SEG = 8
LANE = 128
FAR = 1e30


def spread_columns(wide, columns):
    for n in range(NS):
        wide[n] = jnp.broadcast_to(columns[:, n : n + 1], wide.shape[1:])


def rows_of(i):
    return pl.ds(pl.multiple_of(i * SEG, SEG), SEG)


def rate_rows(rate):
    return [jnp.broadcast_to(rate[n : n + 1, :], (SEG, rate.shape[1])) for n in range(NS)]


def tiled_lanes(block, width):
    return block if width == LANE else jnp.concatenate([block] * (width // LANE), 1)


def prefix_pairs(decay, value, reverse):
    place = lax.broadcasted_iota(jnp.int32, decay.shape, 0)

    def shifted(array, by, fill):
        if reverse:
            return jnp.where(place < SEG - by, pltpu.roll(array, SEG - by, 0), fill)
        return jnp.where(place >= by, pltpu.roll(array, by, 0), fill)

    for by in (1, 2, 4):
        value = decay * shifted(value, by, 0.0) + value
        decay = decay * shifted(decay, by, 1.0)
    last = slice(0, 1) if reverse else slice(SEG - 1, SEG)
    return shifted(decay, 1, 1.0), shifted(value, 1, 0.0), decay[last], value[last]


def ends_kernel(
    reverse, delta, driven, kept, select, rate, pre_decay, pre_value, all_decay, all_value, wide
):
    @pl.when(pl.program_id(0) == 0)
    def _():
        spread_columns(wide, select)

    width = delta.shape[1]
    length = delta.shape[0] // SEG
    rates = rate_rows(rate)
    zero = jnp.zeros((SEG, width), jnp.float32)

    def step(k, carry):
        total, states = carry
        i = length - 1 - k if reverse else k
        rows = rows_of(i)
        reach = jnp.where(tiled_lanes(kept[rows, :], width) > 0, delta[rows, :], FAR)
        drive = driven[rows, :]
        new = []
        for n in range(NS):
            factor = jnp.exp2(reach * rates[n])
            term = drive * tiled_lanes(wide[n, rows, :], width)
            new.append(factor * (states[n] + term) if reverse else factor * states[n] + term)
        return total + reach, tuple(new)

    total, states = lax.fori_loop(0, length, step, (zero, (zero,) * NS))
    for n in range(NS):
        before_decay, before_value, whole_decay, whole_value = prefix_pairs(
            jnp.exp2(total * rates[n]), states[n], reverse
        )
        pre_decay[n] = before_decay
        pre_value[n] = before_value
        all_decay[n : n + 1, :] = whole_decay
        all_value[n : n + 1, :] = whole_value


def output_kernel(
    delta, driven, inner, gate, kept, in_select, out_select, rate, skip, pre_decay, pre_value,
    entry, scanned, gated, wide_in, wide_out,
):
    @pl.when(pl.program_id(0) == 0)
    def _():
        spread_columns(wide_in, in_select)
        spread_columns(wide_out, out_select)

    width = delta.shape[1]
    length = delta.shape[0] // SEG
    rates = rate_rows(rate)
    start = tuple(pre_decay[n] * entry[n : n + 1, :] + pre_value[n] for n in range(NS))

    def step(i, states):
        rows = rows_of(i)
        reach = jnp.where(tiled_lanes(kept[rows, :], width) > 0, delta[rows, :], FAR)
        drive = driven[rows, :]
        new, parts = [], [0.0] * 4
        for n in range(NS):
            state = jnp.exp2(reach * rates[n]) * states[n] + drive * tiled_lanes(
                wide_in[n, rows, :], width
            )
            parts[n % 4] = parts[n % 4] + state * tiled_lanes(wide_out[n, rows, :], width)
            new.append(state)
        scanned[rows, :] = (parts[0] + parts[1]) + (parts[2] + parts[3])
        return tuple(new)

    lax.fori_loop(0, length, step, start)
    value = scanned[...] + skip[...] * inner[...].astype(jnp.float32)
    scanned[...] = value
    half = gate[...].astype(jnp.float32)
    gated[...] = (value * (half * jax.nn.sigmoid(half))).astype(jnp.bfloat16)


def adjoint_kernel(
    delta, driven, inner, grad, step_pre, kept, in_select, out_select, rate, skip, pre_decay,
    pre_value, entry, post_decay, post_value, exit_, pre_low, inner_part, rate_sum, step_sum,
    skip_sum, in_grad, out_grad, states, wide_in, wide_out, in_total, out_total, inner_grad,
    delta_grad,
):
    j = pl.program_id(0)

    @pl.when(j == 0)
    def _():
        spread_columns(wide_in, in_select)
        spread_columns(wide_out, out_select)
        in_total[...] = jnp.zeros_like(in_total)
        out_total[...] = jnp.zeros_like(out_total)

    width = delta.shape[1]
    length = delta.shape[0] // SEG
    rates = rate_rows(rate)
    start = tuple(pre_decay[n] * entry[n : n + 1, :] + pre_value[n] for n in range(NS))

    def folded(value):
        return sum(value[:, k : k + LANE] for k in range(0, width, LANE))

    def advance(i, carry):
        rows = rows_of(i)
        reach = jnp.where(tiled_lanes(kept[rows, :], width) > 0, delta[rows, :], FAR)
        drive, grad_t = driven[rows, :], grad[rows, :]
        new = []
        for n in range(NS):
            states[i, n] = carry[n]
            state = jnp.exp2(reach * rates[n]) * carry[n] + drive * tiled_lanes(
                wide_in[n, rows, :], width
            )
            out_total[n, rows, :] = out_total[n, rows, :] + folded(grad_t * state)
            new.append(state)
        return tuple(new)

    lax.fori_loop(0, length, advance, start)
    back = tuple(post_decay[n] * exit_[n : n + 1, :] + post_value[n] for n in range(NS))
    zero = jnp.zeros((SEG, width), jnp.float32)

    def retreat(k, carry):
        backs, sums = carry
        i = length - 1 - k
        rows = rows_of(i)
        step_t = delta[rows, :]
        reach = jnp.where(tiled_lanes(kept[rows, :], width) > 0, step_t, FAR)
        drive, grad_t = driven[rows, :], grad[rows, :]
        new_backs, new_sums = [], []
        weighted, slope = [0.0] * 2, [0.0] * 2
        for n in range(NS):
            adjoint = grad_t * tiled_lanes(wide_out[n, rows, :], width) + backs[n]
            passed = jnp.exp2(reach * rates[n]) * adjoint
            through = passed * states[i, n]
            weighted[n % 2] = weighted[n % 2] + adjoint * tiled_lanes(wide_in[n, rows, :], width)
            slope[n % 2] = slope[n % 2] + through * rates[n]
            in_total[n, rows, :] = in_total[n, rows, :] + folded(adjoint * drive)
            new_backs.append(passed)
            new_sums.append(sums[n] + through * step_t)
        inner_grad[rows, :] = weighted[0] + weighted[1]
        delta_grad[rows, :] = slope[0] + slope[1]
        return tuple(new_backs), tuple(new_sums)

    _, sums = lax.fori_loop(0, length, retreat, (back, (zero,) * NS))
    for n in range(NS):
        rate_sum[n : n + 1, :] = jnp.sum(sums[n], 0, keepdims=True)
    weighted, value, grads = inner_grad[...], inner[...].astype(jnp.float32), grad[...]
    slope = weighted * value + delta_grad[...] * math.log(2.0)
    pre = slope * jax.nn.sigmoid(step_pre[...])
    pre_low[...] = pre.astype(jnp.bfloat16)
    step_sum[...] = jnp.sum(pre, 0, keepdims=True)
    skip_sum[...] = jnp.sum(grads * value, 0, keepdims=True)
    inner_part[...] = grads * skip[...] + weighted * delta[...]

    @pl.when(j == pl.num_programs(0) - 1)
    def _():
        place = lax.broadcasted_iota(jnp.int32, in_grad.shape, 1)
        for total, result in ((in_total, in_grad), (out_total, out_grad)):
            value = jnp.zeros(result.shape, jnp.float32)
            for n in range(NS):
                column = jnp.sum(total[n], 1, keepdims=True)
                value = jnp.where(place == n, column, value)
            result[...] = value


def earlier_rows(ext, front, rows):
    own = front[0:rows, :].astype(jnp.float32)
    halo = front[rows : rows + SEG, :].astype(jnp.float32)
    place = lax.broadcasted_iota(jnp.int32, (SEG, own.shape[1]), 0)
    for b in range(3):
        at = rows - (3 - b) * SEG
        group = pltpu.roll(own[at : at + SEG], 1, 0)
        ext[b * SEG : (b + 1) * SEG, :] = jnp.where(place == 0, halo[b : b + 1], group)
    ext[3 * SEG :, :] = own


def masked_tap(ext, same, k, rows, width):
    tap = ext[k * SEG : k * SEG + rows, :]
    return tap if k == 3 else tap * tiled_lanes(same[k], width)


def conv_kernel(front, same, taps, bias, conv_sum, inner, ext):
    rows, width = conv_sum.shape
    earlier_rows(ext, front, rows)
    total = jnp.broadcast_to(bias[...], (rows, width))
    for k in range(4):
        total = total + taps[k : k + 1, :] * masked_tap(ext, same, k, rows, width)
    conv_sum[...] = total
    inner[...] = (total * jax.nn.sigmoid(total)).astype(jnp.bfloat16)


def conv_back_kernel(
    front, same, taps, conv_sum, inner_part, select_low, select, front_grad, early, sums, ext
):
    rows, width = conv_sum.shape
    total = conv_sum[...]
    logistic = jax.nn.sigmoid(total)
    back = lax.dot_general(
        select_low[...], select[...], (((1,), (1,)), ((), ())), preferred_element_type=jnp.float32
    )
    back = (inner_part[...] + back) * (logistic * (1.0 + total * (1.0 - logistic)))
    earlier_rows(ext, front, rows)
    for k in range(4):
        sums[k : k + 1, :] = jnp.sum(back * masked_tap(ext, same, k, rows, width), 0, keepdims=True)
    sums[4:5, :] = jnp.sum(back, 0, keepdims=True)
    sums[5:8, :] = jnp.zeros((3, width), jnp.float32)
    ext[0 : 3 * SEG, :] = jnp.zeros((3 * SEG, width), jnp.float32)
    ext[3 * SEG :, :] = back * taps[3:4, :]
    for k in range(3):
        part = back * taps[k : k + 1, :] * tiled_lanes(same[k], width)
        ext[k * SEG : k * SEG + rows, :] = ext[k * SEG : k * SEG + rows, :] + part
    place = lax.broadcasted_iota(jnp.int32, (SEG, width), 0)
    early[...] = ext[0 : 3 * SEG, :]
    for b in range(3):
        at = rows + b * SEG
        later = pltpu.roll(ext[b * SEG : (b + 1) * SEG, :], SEG - 1, 0)
        ext[at : at + SEG, :] = ext[at : at + SEG, :] + jnp.where(place < SEG - 1, later, 0.0)
    front_grad[...] = ext[3 * SEG :, :]


def expert_kernel(
    buffer, grads, up, down, returned, buffer_grad, up_left, up_right, down_left, down_right
):
    def product(left, right, contract):
        return lax.dot_general(
            left, right, (contract, ((), ())), preferred_element_type=jnp.float32
        )

    @pl.when(pl.program_id(0) == 0)
    def _():
        returned[...] = jnp.zeros_like(returned)
        buffer_grad[...] = jnp.zeros_like(buffer_grad)

    values, cot = buffer[...], grads[...]
    hidden = product(values, up[...], ((1,), (1,)))
    below = 0.5 * (1.0 + lax.erf(hidden * math.sqrt(0.5)))
    density = jnp.exp(-0.5 * hidden * hidden) * (1.0 / math.sqrt(2.0 * math.pi))
    active = (hidden * below).astype(jnp.bfloat16)
    active_grad = product(cot, down[...], ((1,), (1,)))
    hidden_grad = (active_grad * (below + hidden * density)).astype(jnp.bfloat16)
    returned[...] += product(active, down[...], ((1,), (0,)))
    buffer_grad[...] += product(hidden_grad, up[...], ((1,), (0,)))
    cut = up_left.shape[1]
    down_grad = product(active, cot, ((0,), (0,))).astype(jnp.bfloat16)
    down_left[...] = down_grad[:, :cut]
    down_right[...] = down_grad[:, cut:]
    up_grad = product(hidden_grad, values, ((0,), (0,))).astype(jnp.bfloat16)
    up_left[...] = up_grad[:, :cut]
    up_right[...] = up_grad[:, cut:]


def column_specs(rows, width):
    return (
        pl.BlockSpec((rows, width), lambda j: (0, j)),
        pl.BlockSpec((rows, LANE), lambda j: (0, 0)),
        pl.BlockSpec((rows, NS), lambda j: (0, 0)),
        pl.BlockSpec((NS, width), lambda j: (0, j)),
        pl.BlockSpec((NS, SEG, width), lambda j: (0, 0, j)),
        pl.BlockSpec((1, width), lambda j: (0, j)),
    )


def params(mib):
    return pltpu.CompilerParams(
        dimension_semantics=("arbitrary",), vmem_limit_bytes=mib * 2**20
    )


def cost(rows, channels, passes):
    return pl.CostEstimate(
        flops=0, bytes_accessed=int(rows * channels * passes), transcendentals=0
    )


def segment_ends(delta, driven, kept, select, rate, reverse, width=LANE):
    rows, channels = delta.shape
    block, flag, columns, state, segments, _ = column_specs(rows, width)
    return pl.pallas_call(
        functools.partial(ends_kernel, reverse),
        grid=(channels // width,),
        in_specs=[block, block, flag, columns, state],
        out_specs=[segments, segments, state, state],
        out_shape=[jax.ShapeDtypeStruct((NS, SEG, channels), jnp.float32)] * 2
        + [jax.ShapeDtypeStruct((NS, channels), jnp.float32)] * 2,
        scratch_shapes=[pltpu.VMEM((NS, rows, LANE), jnp.float32)],
        compiler_params=params(24),
        cost_estimate=cost(rows, channels, 75),
    )(delta, driven, kept, select, rate)


def scan_output(
    delta, driven, inner, gate, kept, in_select, out_select, rate, skip, pre, entry, width=LANE
):
    rows, channels = delta.shape
    block, flag, columns, state, segments, line = column_specs(rows, width)
    wide = pltpu.VMEM((NS, rows, LANE), jnp.float32)
    return pl.pallas_call(
        output_kernel,
        grid=(channels // width,),
        in_specs=[block] * 4 + [flag, columns, columns, state, line, segments, segments, state],
        out_specs=[block, block],
        out_shape=[
            jax.ShapeDtypeStruct((rows, channels), jnp.float32),
            jax.ShapeDtypeStruct((rows, channels), jnp.bfloat16),
        ],
        scratch_shapes=[wide, wide],
        compiler_params=params(24),
        cost_estimate=cost(rows, channels, 95),
    )(delta, driven, inner, gate, kept, in_select, out_select, rate, skip, *pre, entry)


def scan_adjoint(
    delta, driven, inner, grad, step_pre, kept, in_select, out_select, rate, skip, pre, entry,
    post, exit_, width=LANE,
):
    rows, channels = delta.shape
    block, flag, columns, state, segments, line = column_specs(rows, width)
    wide = pltpu.VMEM((NS, rows, LANE), jnp.float32)
    whole = pltpu.VMEM((rows, width), jnp.float32)
    return pl.pallas_call(
        adjoint_kernel,
        grid=(channels // width,),
        in_specs=[block] * 5
        + [flag, columns, columns, state, line]
        + [segments, segments, state, segments, segments, state],
        out_specs=[block, block, state, line, line, columns, columns],
        out_shape=[
            jax.ShapeDtypeStruct((rows, channels), jnp.bfloat16),
            jax.ShapeDtypeStruct((rows, channels), jnp.float32),
            jax.ShapeDtypeStruct((NS, channels), jnp.float32),
        ]
        + [jax.ShapeDtypeStruct((1, channels), jnp.float32)] * 2
        + [jax.ShapeDtypeStruct((rows, NS), jnp.float32)] * 2,
        scratch_shapes=[
            pltpu.VMEM((rows // SEG, NS, SEG, width), jnp.float32),
            wide, wide, wide, wide, whole, whole,
        ],
        compiler_params=params(40),
        cost_estimate=cost(rows, channels, 280),
    )(
        delta, driven, inner, grad, step_pre, kept, in_select, out_select, rate, skip, *pre, entry,
        *post, exit_,
    )


def conv_specs(rows, width):
    return (
        pl.BlockSpec((rows + SEG, width), lambda j: (0, j)),
        pl.BlockSpec((3, rows, LANE), lambda j: (0, 0, 0)),
        pl.BlockSpec((4, width), lambda j: (0, j)),
        pl.BlockSpec((rows, width), lambda j: (0, j)),
    )


def convolved(front, same, taps, bias, width):
    rows, channels = front.shape[0] - SEG, front.shape[1]
    ahead, flags, weights, block = conv_specs(rows, width)
    return pl.pallas_call(
        conv_kernel,
        grid=(channels // width,),
        in_specs=[ahead, flags, weights, pl.BlockSpec((1, width), lambda j: (0, j))],
        out_specs=[block, block],
        out_shape=[
            jax.ShapeDtypeStruct((rows, channels), jnp.float32),
            jax.ShapeDtypeStruct((rows, channels), jnp.bfloat16),
        ],
        scratch_shapes=[pltpu.VMEM((rows + 3 * SEG, width), jnp.float32)],
        compiler_params=params(24),
        cost_estimate=cost(rows, channels, 25),
    )(front, same, taps, bias)


def convolved_back(front, same, taps, conv_sum, inner_part, select_low, select, width):
    rows, channels = conv_sum.shape
    ahead, flags, weights, block = conv_specs(rows, width)
    inputs = select.shape[1]
    return pl.pallas_call(
        conv_back_kernel,
        grid=(channels // width,),
        in_specs=[
            ahead,
            flags,
            weights,
            block,
            block,
            pl.BlockSpec((rows, inputs), lambda j: (0, 0)),
            pl.BlockSpec((width, inputs), lambda j: (j, 0)),
        ],
        out_specs=[
            block,
            pl.BlockSpec((3 * SEG, width), lambda j: (0, j)),
            pl.BlockSpec((SEG, width), lambda j: (0, j)),
        ],
        out_shape=[
            jax.ShapeDtypeStruct((rows, channels), jnp.float32),
            jax.ShapeDtypeStruct((3 * SEG, channels), jnp.float32),
            jax.ShapeDtypeStruct((SEG, channels), jnp.float32),
        ],
        scratch_shapes=[pltpu.VMEM((rows + 3 * SEG, width), jnp.float32)],
        compiler_params=params(24),
        cost_estimate=cost(rows, channels, 40),
    )(front, same, taps, conv_sum, inner_part, select_low, select)


def expert_pass(buffer, grads, up, down, tile):
    slots, width = buffer.shape
    units = up.shape[0]
    whole = pl.BlockSpec((slots, width), lambda j: (0, 0))
    strip = pl.BlockSpec((tile, width), lambda j: (j, 0))
    cut = cut_of(width)
    sizes = [cut, width - cut] * 2
    return pl.pallas_call(
        expert_kernel,
        grid=(units // tile,),
        in_specs=[whole, whole, strip, strip],
        out_specs=[whole, whole] + [pl.BlockSpec((tile, n), lambda j: (j, 0)) for n in sizes],
        out_shape=[jax.ShapeDtypeStruct((slots, width), jnp.float32)] * 2
        + [jax.ShapeDtypeStruct((units, n), jnp.bfloat16) for n in sizes],
        compiler_params=params(40),
        cost_estimate=pl.CostEstimate(
            flops=12 * slots * width * units, bytes_accessed=8 * units * width, transcendentals=0
        ),
    )(buffer, grads, up, down)


MODEL_WIDTH = 1152
DI = 2304
R = 72
KC = 4
EXPERT_COUNT = 2
EPS = 1e-05
REACH = KC - 1
BOTH = ("dp", "seq")
HIGHEST = lax.Precision.HIGHEST
F32 = jnp.float32
BF16 = jnp.bfloat16


def passed_along(array, axis, by):
    size = lax.axis_size(axis)
    pairs = [(i, i + by) for i in range(size) if 0 <= i + by < size]
    return lax.ppermute(array, axis, pairs)


def interleave(array):
    split = array.reshape((SEG, array.shape[0] // SEG) + array.shape[1:])
    return split.swapaxes(0, 1).reshape(array.shape)


def in_order(array):
    split = array.reshape((array.shape[0] // SEG, SEG) + array.shape[1:])
    return split.swapaxes(0, 1).reshape(array.shape)


def with_earlier(array, earlier):
    last = array[array.shape[0] - REACH * SEG :].reshape((REACH, SEG) + array.shape[1:])
    front = jnp.concatenate([earlier[:, None], last[:, : SEG - 1]], 1)
    return jnp.concatenate([front.reshape((REACH * SEG,) + array.shape[1:]), array])


def entering(decay, value, reverse):
    pair = jnp.stack([decay, value]).astype(BF16)
    state = jnp.zeros_like(value)
    for k in range(lax.axis_size("seq") - 1, 0, -1):
        part = passed_along(pair, "seq", -k if reverse else k).astype(F32)
        state = part[0] * state + part[1]
    return state


def silu_slope(value):
    logistic = jax.nn.sigmoid(value)
    return logistic * (1.0 + value * (1.0 - logistic))


def gelu_slope(value):
    return 0.5 * (1.0 + lax.erf(value / math.sqrt(2.0))) + value * jnp.exp(
        -0.5 * value * value
    ) / math.sqrt(2.0 * math.pi)


def dot(left, right, contract, precision=None):
    return lax.dot_general(
        left, right, (contract, ((), ())), precision=precision, preferred_element_type=F32
    )


def sides():
    return math.isqrt(lax.axis_size("dp") // 2)


def moved(array, axis, by=1):
    if axis == "z":
        size = lax.axis_size("seq")
        return lax.ppermute(array, "seq", [(i, (i + by) % size) for i in range(size)])
    side = sides()
    stride, size = {"core": (1, 2), "x": (2, side), "y": (2 * side, side)}[axis]
    pairs = []
    for i in range(lax.axis_size("dp")):
        at = i // stride % size
        pairs.append((i, i + stride * ((at + by) % size - at)))
    return lax.ppermute(array, "dp", pairs)


def size_of(axis):
    return lax.axis_size("seq") if axis == "z" else 2 if axis == "core" else sides()


def ring_gather(block, axis):
    pieces = [block]
    for _ in range(size_of(axis) - 1):
        pieces.append(moved(pieces[-1], axis))
    if axis == "z":
        whole = jnp.zeros((len(pieces),) + block.shape, block.dtype)
        for k, piece in enumerate(pieces):
            whole = lax.dynamic_update_index_in_dim(whole, piece, depth_of(k), 0)
        return whole
    return jnp.stack(pieces)


def depth_of(k):
    size = lax.axis_size("seq")
    return lax.rem(lax.axis_index("seq") + size - k, size)


def added(left, right):
    return (left.astype(F32) + right.astype(F32)).astype(BF16)


def ring_scatter(parts, axis):
    if axis == "z":
        size = size_of(axis)
        parts = [lax.dynamic_index_in_dim(parts, depth_of(k), 0, False) for k in range(size)]
    total = parts[-1]
    for k in range(size_of(axis) - 2, -1, -1):
        total = added(parts[k], moved(total, axis, -1))
    return total


def cut_of(columns):
    return (columns // LANE + 1) // 2 * LANE


def after(value, *others):
    if not others:
        return value
    return lax.optimization_barrier((value, *others))[0]


def plane_gather(block, waits=((), (), ())):
    cut = cut_of(block.shape[1])
    pieces = ring_gather(after(block, *waits[0]), "z")
    first = after(pieces, *waits[1])
    left = after(ring_gather(first[..., :cut], "x"), *waits[2])
    right = after(ring_gather(first[..., cut:], "y"), *waits[2])
    left, right = ring_gather(left, "y"), ring_gather(right, "x")
    return jnp.concatenate([left, right.swapaxes(0, 1)], -1), pieces, (left, right)


def plane_scatter(left, right, waits=((), ())):
    left = after(ring_scatter(left, "y"), *waits[0])
    right = after(ring_scatter(right.swapaxes(0, 1), "x"), *waits[0])
    left, right = ring_scatter(left, "x"), ring_scatter(right, "y")
    return ring_scatter(after(jnp.concatenate([left, right], -1), *waits[1]), "z")


def by_place(pieces, axis):
    size = size_of(axis)
    mine = lax.axis_index("dp") // (2 * sides())
    order = []
    for j in range(size):
        piece = pieces[size - 1]
        for k in range(size - 1):
            piece = jnp.where(lax.rem(mine - j + size, size) == k, pieces[k], piece)
        order.append(piece)
    return order


def unit_blocks(whole, inverse=False):
    side = sides()
    dp = lax.axis_index("dp")
    at_x, at_core = lax.rem(dp // 2, side), lax.rem(dp, 2)
    parts = whole.reshape((side // 2, side, 2, -1) + whole.shape[1:])
    if inverse:
        parts = whole.reshape((2, side // 2, side, -1) + whole.shape[1:]).transpose(1, 2, 0, 3, 4)
    rows = []
    for k in range(side):
        piece = lax.dynamic_index_in_dim(parts, lax.rem(at_x - k + side, side), 1, False)
        pair = [piece[:, 0], piece[:, 1]]
        rows.append([jnp.where(at_core == 0, pair[c], pair[1 - c]) for c in range(2)])
    if inverse:
        return jnp.stack([jnp.stack(r, 1) for r in rows], 1).reshape(whole.shape)
    return [jnp.stack([r[c] for r in rows], 1).reshape((-1,) + whole.shape[1:]) for c in range(2)]


def unit_gather(block):
    return unit_blocks(lax.all_gather(block, BOTH, axis=0, tiled=True))


def unit_scatter(grads):
    whole = unit_blocks(jnp.concatenate(grads), True)
    return lax.psum_scatter(whole, BOTH, scatter_dimension=0, tiled=True).astype(F32)


def everywhere(array):
    for axis in ("dp", "seq"):
        size = lax.axis_size(axis)
        bit = 1
        while bit < size:
            array = array + lax.ppermute(array, axis, [(i, i ^ bit) for i in range(size)])
            bit *= 2
    return array


def per_device(
    tokens,
    doc_ids,
    token_expert,
    out_grad,
    norm_gains,
    in_proj,
    conv_weight,
    conv_bias,
    select_proj,
    step_proj,
    step_bias,
    decay_log,
    skip_gain,
    out_proj,
    router,
    expert_up,
    expert_down,
):
    rows = tokens.shape[1]
    slots_per = 5 * rows // (4 * EXPERT_COUNT)
    slots = EXPERT_COUNT * slots_per
    half = DI // 2
    wide = half // 3
    core = lax.rem(lax.axis_index("dp"), 2)
    side, depth = sides(), lax.axis_size("seq")
    both = range(2)

    prior_tokens = passed_along(tokens[0, rows - REACH :], "seq", 1)
    prior_doc = passed_along(doc_ids[0, rows - REACH :], "seq", 1)
    lines = lax.all_gather(jnp.concatenate([norm_gains, router.T]), "dp", axis=1, tiled=True)
    gains_all = lines[:2].astype(F32)
    router_all = lines[2:].astype(F32)

    small = jnp.concatenate(
        [
            select_proj,
            step_proj.T,
            decay_log,
            conv_weight.T,
            conv_bias[:, None],
            step_bias[:, None],
            skip_gain[:, None],
        ],
        1,
    )
    columns = small.shape[1]
    spare = -columns % LANE

    def expert_block(shards):
        own = jnp.where(core == 0, shards[0], shards[1])
        other = jnp.where(core == 0, shards[1], shards[0])
        return jnp.concatenate([own, moved(other, "core")])

    in_near, in_z, _ = plane_gather(in_proj.T)
    in_near = in_near.reshape(DI, MODEL_WIDTH)
    in_full = (in_near, moved(in_near, "core"))
    small_full = unit_gather(jnp.pad(small, ((0, 0), (0, spare))))
    out_full = unit_gather(out_proj)
    up_block = expert_block(expert_up.swapaxes(1, 2))
    down_block = expert_block(expert_down)

    at = R + 2 * NS
    select_full = [w[:, :at] for w in small_full]
    step_full = [w[:, at : at + R] for w in small_full]
    line_full = [w[:, at + R : columns].astype(F32).T for w in small_full]
    decay_rate = [-jnp.exp(w[:NS]) for w in line_full]
    conv_taps = [w[NS : NS + KC] for w in line_full]
    bias_conv, bias_step, skip_wide = (
        [w[NS + KC + k][None] for w in line_full] for k in range(3)
    )

    mine = interleave(tokens[0])
    doc_row = interleave(doc_ids[0])
    route = interleave(token_expert[0, :, 0])
    out_cot = interleave(out_grad[0]).astype(F32)

    extended = jnp.concatenate([mine, prior_tokens, jnp.zeros_like(mine[: SEG - REACH])])
    stream_ext = extended.astype(F32)
    inv_ext = lax.rsqrt(jnp.mean(stream_ext * stream_ext, -1, keepdims=True) + EPS)
    hat_ext = stream_ext * inv_ext
    normed_ext = (hat_ext * gains_all[0]).astype(BF16)
    stream, inv_first, hat_first, normed = (
        a[:rows] for a in (stream_ext, inv_ext, hat_ext, normed_ext)
    )
    ext_ids = with_earlier(doc_row, prior_doc)
    same = jnp.stack(
        [(ext_ids[k * SEG : k * SEG + rows] == doc_row).astype(F32) for k in range(REACH)]
    )
    same = jnp.broadcast_to(same[:, :, None], (REACH, rows, LANE))
    kept = same[REACH - 1]

    strip = DI // side
    front, gate, conv_sum, inner = [], [], [], []
    for h in both:
        proj = dot(normed_ext, in_full[h], ((1,), (1,))).astype(BF16)
        parts = by_place([proj[:, k * strip : (k + 1) * strip] for k in range(side)], "y")
        front.append(jnp.concatenate(parts[: side // 2], 1))
        gate.append(jnp.concatenate(parts[side // 2 :], 1)[:rows])
        made = convolved(front[h], same, conv_taps[h], bias_conv[h], wide)
        conv_sum.append(made[0])
        inner.append(made[1])
    select = sum(dot(inner[h], select_full[h], ((1,), (0,))) for h in both)
    steps_low = select[:, :R].astype(BF16)
    in_select = select[:, R : R + NS]
    out_select = select[:, R + NS :]
    step_pre = [dot(steps_low, step_full[h], ((1,), (1,))) + bias_step[h] for h in both]
    delta = [jax.nn.softplus(p) for p in step_pre]
    driven = [d * x.astype(F32) for d, x in zip(delta, inner)]
    rate = [r * math.log2(math.e) for r in decay_rate]

    up_full, up_z, up_side = plane_gather(
        up_block, ((in_z,), (in_near,), tuple(x[:SEG] for x in inner))
    )
    pre, state_in, marks = [], [], []
    for h in both:
        *ends, all_decay, all_state = segment_ends(
            delta[h], driven[h], kept, in_select, rate[h], False, wide
        )
        marks.append(all_decay)
        pre.append(ends)
        state_in.append(entering(all_decay, all_state, False))
    scanned, gated = zip(
        *(
            scan_output(
                delta[h], driven[h], inner[h], gate[h], kept, in_select, out_select, rate[h],
                skip_wide[h], pre[h], state_in[h], wide,
            )
            for h in both
        )
    )
    down_full, _, _ = plane_gather(
        down_block, ((up_z,), tuple(marks), tuple(g[:SEG] for g in gated))
    )
    up_full, down_full = (w.reshape(-1, MODEL_WIDTH) for w in (up_full, down_full))
    mixed = sum(dot(gated[h], out_full[h], ((1,), (0,))) for h in both)
    resid = stream + mixed
    inv_second = lax.rsqrt(jnp.mean(resid * resid, -1, keepdims=True) + EPS)
    hat_second = resid * inv_second
    normed_moe = (hat_second * gains_all[1]).astype(BF16)
    normed_wide = normed_moe.astype(F32)
    logits = dot(normed_wide, router_all, ((1,), (1,)), HIGHEST)
    probs = jax.nn.softmax(logits, -1)
    route_hot = route[:, None] == jnp.arange(EXPERT_COUNT, dtype=jnp.int32)[None, :]
    hot_wide = route_hot.astype(F32)
    chosen = jnp.sum(probs * hot_wide, 1, keepdims=True)
    place = jnp.arange(rows, dtype=jnp.int32)
    lower = (place[:, None] >= place[None, :]).astype(BF16)
    rank_in = dot(lower, route_hot.astype(BF16), ((1,), (0,))) - 1.0
    slot = jnp.sum(rank_in * hot_wide, 1).astype(jnp.int32)
    target = jnp.where(route == core, 0, slots_per) + slot
    pick = (jnp.arange(slots, dtype=jnp.int32)[:, None] == target[None, :]).astype(BF16)
    returned_grad = (chosen * out_cot).astype(BF16)
    placed = dot(pick, jnp.concatenate([normed_moe, returned_grad], 1), ((1,), (0,))).astype(BF16)
    placed = jnp.concatenate([placed[:slots_per], moved(placed[slots_per:], "core")])
    buffer, grad_slots = placed[:, :MODEL_WIDTH], placed[:, MODEL_WIDTH:]

    def from_slots(parts):
        parts = jnp.concatenate([parts[:slots_per], moved(parts[slots_per:], "core")])
        return dot(pick.astype(F32), parts, ((0,), (0,)), HIGHEST)

    def expert_scatter(left, right, waits):
        left, right = (g.reshape(side, side, depth, -1, g.shape[1]) for g in (left, right))
        own, other = jnp.split(plane_scatter(left, right, waits), 2)
        other = moved(other, "core")
        pair = jnp.where(core == 0, own, other), jnp.where(core == 0, other, own)
        return jnp.stack(pair).astype(F32)

    returned, buffer_grad, *expert_grads = expert_pass(
        buffer, grad_slots, up_full, down_full, up_full.shape[0] // 12
    )
    returned = from_slots(returned)
    buffer_grad = from_slots(buffer_grad)
    branch = chosen * returned
    layer_out = (resid + branch).astype(BF16)
    squared_values = jnp.stack(
        [jnp.sum(resid * resid), jnp.sum(mixed * mixed), jnp.sum(branch * branch)]
    )
    chosen_grad = jnp.sum(out_cot * returned, 1, keepdims=True)
    logit_grad = chosen_grad * chosen * (hot_wide - probs)
    grad_router = dot(logit_grad, normed_wide, ((0,), (0,)), HIGHEST)
    moe_grad = buffer_grad + dot(logit_grad, router_all, ((1,), (0,)), HIGHEST)
    second_gain_grad = jnp.sum(moe_grad * hat_second, 0)
    scaled_second = moe_grad * gains_all[1]
    resid_grad = out_cot + inv_second * (
        scaled_second - hat_second * jnp.mean(scaled_second * hat_second, -1, keepdims=True)
    )
    mixed_grad = resid_grad.astype(BF16)
    gated_grad = [dot(mixed_grad, out_full[h], ((1,), (1,))) for h in both]
    gates = [g.astype(F32) for g in gate]
    scan_grad = [gated_grad[h] * jax.nn.silu(gates[h]) for h in both]
    gate_grad = [(gated_grad[h] * scanned[h] * silu_slope(gates[h])).astype(BF16) for h in both]
    post, adjoint_in = [], []
    for h in both:
        *ends, all_decay, all_adjoint = segment_ends(
            delta[h], scan_grad[h], kept, out_select, rate[h], True, wide
        )
        post.append(ends)
        marks.append(all_decay)
        adjoint_in.append(entering(all_decay, all_adjoint, True))
    out_sum = unit_scatter(
        [dot(gated[h], mixed_grad, ((0,), (0,))).astype(BF16) for h in both]
    )
    pre_low, inner_part, rate_sum, step_sum, skip_sum, in_grad, out_grads = zip(
        *(
            scan_adjoint(
                delta[h], driven[h], inner[h], scan_grad[h], step_pre[h], kept, in_select,
                out_select, rate[h], skip_wide[h], pre[h], state_in[h], post[h], adjoint_in[h],
                wide,
            )
            for h in both
        )
    )
    down_sum = expert_scatter(
        *expert_grads[2:], (tuple(marks[2:]), (step_sum[0],))
    )
    up_sum = expert_scatter(*expert_grads[:2], ((step_sum[0],), (step_sum[1],)))
    steps_grad = sum(dot(pre_low[h], step_full[h], ((1,), (0,))) for h in both)
    select_low = jnp.concatenate(
        [steps_grad, in_grad[0] + in_grad[1], out_grads[0] + out_grads[1]], 1
    ).astype(BF16)
    front_grad, early, tap_sums = zip(
        *(
            convolved_back(
                front[h], same, conv_taps[h], conv_sum[h], inner_part[h], select_low,
                select_full[h], wide,
            )
            for h in both
        )
    )
    grad_small = []
    for h in both:
        lines = [rate_sum[h] * decay_rate[h], tap_sums[h][: KC + 1], step_sum[h], skip_sum[h]]
        grad_small.append(
            jnp.concatenate(
                [
                    dot(inner[h], select_low, ((0,), (0,))),
                    dot(pre_low[h], steps_low, ((0,), (0,))),
                    jnp.concatenate(lines).T,
                    jnp.zeros((half, spare), F32),
                ],
                1,
            ).astype(BF16)
        )
    proj_grad = []
    for h in both:
        incoming = passed_along(early[h].reshape(REACH, SEG, half)[:, 0], "seq", -1)
        tail = jnp.pad(incoming[:, None], ((0, 0), (SEG - 1, 0), (0, 0)))
        tail = jnp.pad(tail.reshape(REACH * SEG, half), ((rows - REACH * SEG, 0), (0, 0)))
        whole = jnp.concatenate([(front_grad[h] + tail).astype(BF16), gate_grad[h]], 1)
        parts = [whole[:, k * strip : (k + 1) * strip] for k in range(side)]
        proj_grad.append(jnp.concatenate(by_place(parts, "y"), 1))
    grad_in = [dot(proj_grad[h], normed, ((0,), (0,))).astype(BF16) for h in (1, 0)]
    in_plane = added(grad_in[1], moved(grad_in[0], "core"))
    in_plane = in_plane.reshape(side, side, depth, -1, MODEL_WIDTH)
    cut = cut_of(MODEL_WIDTH)
    in_sum = plane_scatter(in_plane[..., :cut], in_plane[..., cut:]).astype(F32)
    small_sum = unit_scatter(grad_small)
    normed_grad = sum(dot(proj_grad[h], in_full[h], ((1,), (0,))) for h in both)
    first_gain_grad = jnp.sum(normed_grad * hat_first, 0)
    scaled_first = normed_grad * gains_all[0]
    stream_grad = resid_grad + inv_first * (
        scaled_first - hat_first * jnp.mean(scaled_first * hat_first, -1, keepdims=True)
    )

    line_sum = small_sum[:, at + R :]
    squares = jnp.zeros((1, MODEL_WIDTH), F32).at[0, :3].set(squared_values)
    early_sum = everywhere(jnp.concatenate([second_gain_grad[None], grad_router, squares]))
    late_sum = everywhere(first_gain_grad[None])
    parts = lax.axis_size("dp")
    width = MODEL_WIDTH // parts
    shared = lax.dynamic_slice_in_dim(
        jnp.concatenate([late_sum, early_sum[:3]]), lax.axis_index("dp") * width, width, 1
    )
    stats = jnp.sqrt(early_sum[3, :3] / (rows * parts * depth * MODEL_WIDTH))
    return (
        in_order(layer_out)[None],
        in_order(stream_grad.astype(BF16))[None],
        shared[:2],
        in_sum.T,
        line_sum[:, NS : NS + KC].T,
        line_sum[:, NS + KC],
        small_sum[:, :at],
        small_sum[:, at : at + R].T,
        line_sum[:, NS + KC + 1],
        line_sum[:, :NS],
        line_sum[:, NS + KC + 2],
        out_sum,
        shared[2:].T,
        up_sum.swapaxes(1, 2),
        down_sum,
        stats,
    )


def solution(mesh):
    return jax.shard_map(
        per_device,
        mesh=mesh,
        in_specs=(
            P("dp", "seq", None),
            P("dp", "seq"),
            P("dp", "seq", None),
            P("dp", "seq", None),
            P(None, "dp"),
            P(None, ("dp", "seq")),
            P(None, ("dp", "seq")),
            P(("dp", "seq")),
            P(("dp", "seq"), None),
            P(None, ("dp", "seq")),
            P(("dp", "seq")),
            P(("dp", "seq"), None),
            P(("dp", "seq")),
            P(("dp", "seq"), None),
            P("dp", None),
            P(None, None, ("dp", "seq")),
            P(None, ("dp", "seq"), None),
        ),
        out_specs=(
            P("dp", "seq", None),
            P("dp", "seq", None),
            P(None, "dp"),
            P(None, ("dp", "seq")),
            P(None, ("dp", "seq")),
            P(("dp", "seq")),
            P(("dp", "seq"), None),
            P(None, ("dp", "seq")),
            P(("dp", "seq")),
            P(("dp", "seq"), None),
            P(("dp", "seq")),
            P(("dp", "seq"), None),
            P("dp", None),
            P(None, None, ("dp", "seq")),
            P(None, ("dp", "seq"), None),
            P(),
        ),
        check_vma=False,
    )
```

```python
import functools, math
import jax
import jax.numpy as jnp
from jax import lax
from jax.experimental import pallas as pl
from jax.experimental.pallas import tpu as pltpu
from jax.sharding import PartitionSpec as P

NS = 16
SEG = 8
LANE = 128
FAR = 1e30


def spread_columns(wide, columns):
    for n in range(NS):
        wide[n] = jnp.broadcast_to(columns[:, n : n + 1], wide.shape[1:])


def rows_of(i):
    return pl.ds(pl.multiple_of(i * SEG, SEG), SEG)


def rate_rows(rate):
    return [jnp.broadcast_to(rate[n : n + 1, :], (SEG, rate.shape[1])) for n in range(NS)]


def tiled_lanes(block, width):
    return block if width == LANE else jnp.concatenate([block] * (width // LANE), 1)


def prefix_pairs(decay, value, reverse):
    place = lax.broadcasted_iota(jnp.int32, decay.shape, 0)

    def shifted(array, by, fill):
        if reverse:
            return jnp.where(place < SEG - by, pltpu.roll(array, SEG - by, 0), fill)
        return jnp.where(place >= by, pltpu.roll(array, by, 0), fill)

    for by in (1, 2, 4):
        value = decay * shifted(value, by, 0.0) + value
        decay = decay * shifted(decay, by, 1.0)
    last = slice(0, 1) if reverse else slice(SEG - 1, SEG)
    return shifted(decay, 1, 1.0), shifted(value, 1, 0.0), decay[last], value[last]


def ends_kernel(
    reverse, delta, driven, kept, select, rate, pre_decay, pre_value, all_decay, all_value, wide
):
    @pl.when(pl.program_id(0) == 0)
    def _():
        spread_columns(wide, select)

    width = delta.shape[1]
    length = delta.shape[0] // SEG
    rates = rate_rows(rate)
    zero = jnp.zeros((SEG, width), jnp.float32)

    def step(k, carry):
        total, states = carry
        i = length - 1 - k if reverse else k
        rows = rows_of(i)
        reach = jnp.where(tiled_lanes(kept[rows, :], width) > 0, delta[rows, :], FAR)
        drive = driven[rows, :]
        new = []
        for n in range(NS):
            factor = jnp.exp2(reach * rates[n])
            term = drive * tiled_lanes(wide[n, rows, :], width)
            new.append(factor * (states[n] + term) if reverse else factor * states[n] + term)
        return total + reach, tuple(new)

    total, states = lax.fori_loop(0, length, step, (zero, (zero,) * NS))
    for n in range(NS):
        before_decay, before_value, whole_decay, whole_value = prefix_pairs(
            jnp.exp2(total * rates[n]), states[n], reverse
        )
        pre_decay[n] = before_decay
        pre_value[n] = before_value
        all_decay[n : n + 1, :] = whole_decay
        all_value[n : n + 1, :] = whole_value


def output_kernel(
    delta, driven, inner, gate, kept, in_select, out_select, rate, skip, pre_decay, pre_value,
    entry, scanned, gated, wide_in, wide_out,
):
    @pl.when(pl.program_id(0) == 0)
    def _():
        spread_columns(wide_in, in_select)
        spread_columns(wide_out, out_select)

    width = delta.shape[1]
    length = delta.shape[0] // SEG
    rates = rate_rows(rate)
    start = tuple(pre_decay[n] * entry[n : n + 1, :] + pre_value[n] for n in range(NS))

    def step(i, states):
        rows = rows_of(i)
        reach = jnp.where(tiled_lanes(kept[rows, :], width) > 0, delta[rows, :], FAR)
        drive = driven[rows, :]
        new, parts = [], [0.0] * 4
        for n in range(NS):
            state = jnp.exp2(reach * rates[n]) * states[n] + drive * tiled_lanes(
                wide_in[n, rows, :], width
            )
            parts[n % 4] = parts[n % 4] + state * tiled_lanes(wide_out[n, rows, :], width)
            new.append(state)
        scanned[rows, :] = (parts[0] + parts[1]) + (parts[2] + parts[3])
        return tuple(new)

    lax.fori_loop(0, length, step, start)
    value = scanned[...] + skip[...] * inner[...].astype(jnp.float32)
    scanned[...] = value
    half = gate[...].astype(jnp.float32)
    gated[...] = (value * (half * jax.nn.sigmoid(half))).astype(jnp.bfloat16)


def adjoint_kernel(
    delta, driven, inner, grad, step_pre, kept, in_select, out_select, rate, skip, pre_decay,
    pre_value, entry, post_decay, post_value, exit_, pre_low, inner_part, rate_sum, step_sum,
    skip_sum, in_grad, out_grad, states, wide_in, wide_out, in_total, out_total, inner_grad,
    delta_grad,
):
    j = pl.program_id(0)

    @pl.when(j == 0)
    def _():
        spread_columns(wide_in, in_select)
        spread_columns(wide_out, out_select)
        in_total[...] = jnp.zeros_like(in_total)
        out_total[...] = jnp.zeros_like(out_total)

    width = delta.shape[1]
    length = delta.shape[0] // SEG
    rates = rate_rows(rate)
    start = tuple(pre_decay[n] * entry[n : n + 1, :] + pre_value[n] for n in range(NS))

    def folded(value):
        return sum(value[:, k : k + LANE] for k in range(0, width, LANE))

    def advance(i, carry):
        rows = rows_of(i)
        reach = jnp.where(tiled_lanes(kept[rows, :], width) > 0, delta[rows, :], FAR)
        drive, grad_t = driven[rows, :], grad[rows, :]
        new = []
        for n in range(NS):
            states[i, n] = carry[n]
            state = jnp.exp2(reach * rates[n]) * carry[n] + drive * tiled_lanes(
                wide_in[n, rows, :], width
            )
            out_total[n, rows, :] = out_total[n, rows, :] + folded(grad_t * state)
            new.append(state)
        return tuple(new)

    lax.fori_loop(0, length, advance, start)
    back = tuple(post_decay[n] * exit_[n : n + 1, :] + post_value[n] for n in range(NS))
    zero = jnp.zeros((SEG, width), jnp.float32)

    def retreat(k, carry):
        backs, sums = carry
        i = length - 1 - k
        rows = rows_of(i)
        step_t = delta[rows, :]
        reach = jnp.where(tiled_lanes(kept[rows, :], width) > 0, step_t, FAR)
        drive, grad_t = driven[rows, :], grad[rows, :]
        new_backs, new_sums = [], []
        weighted, slope = [0.0] * 2, [0.0] * 2
        for n in range(NS):
            adjoint = grad_t * tiled_lanes(wide_out[n, rows, :], width) + backs[n]
            passed = jnp.exp2(reach * rates[n]) * adjoint
            through = passed * states[i, n]
            weighted[n % 2] = weighted[n % 2] + adjoint * tiled_lanes(wide_in[n, rows, :], width)
            slope[n % 2] = slope[n % 2] + through * rates[n]
            in_total[n, rows, :] = in_total[n, rows, :] + folded(adjoint * drive)
            new_backs.append(passed)
            new_sums.append(sums[n] + through * step_t)
        inner_grad[rows, :] = weighted[0] + weighted[1]
        delta_grad[rows, :] = slope[0] + slope[1]
        return tuple(new_backs), tuple(new_sums)

    _, sums = lax.fori_loop(0, length, retreat, (back, (zero,) * NS))
    for n in range(NS):
        rate_sum[n : n + 1, :] = jnp.sum(sums[n], 0, keepdims=True)
    weighted, value, grads = inner_grad[...], inner[...].astype(jnp.float32), grad[...]
    slope = weighted * value + delta_grad[...] * math.log(2.0)
    pre = slope * jax.nn.sigmoid(step_pre[...])
    pre_low[...] = pre.astype(jnp.bfloat16)
    step_sum[...] = jnp.sum(pre, 0, keepdims=True)
    skip_sum[...] = jnp.sum(grads * value, 0, keepdims=True)
    inner_part[...] = grads * skip[...] + weighted * delta[...]

    @pl.when(j == pl.num_programs(0) - 1)
    def _():
        place = lax.broadcasted_iota(jnp.int32, in_grad.shape, 1)
        for total, result in ((in_total, in_grad), (out_total, out_grad)):
            value = jnp.zeros(result.shape, jnp.float32)
            for n in range(NS):
                column = jnp.sum(total[n], 1, keepdims=True)
                value = jnp.where(place == n, column, value)
            result[...] = value


def earlier_rows(ext, front, rows):
    own = front[0:rows, :].astype(jnp.float32)
    halo = front[rows : rows + SEG, :].astype(jnp.float32)
    place = lax.broadcasted_iota(jnp.int32, (SEG, own.shape[1]), 0)
    for b in range(3):
        at = rows - (3 - b) * SEG
        group = pltpu.roll(own[at : at + SEG], 1, 0)
        ext[b * SEG : (b + 1) * SEG, :] = jnp.where(place == 0, halo[b : b + 1], group)
    ext[3 * SEG :, :] = own


def masked_tap(ext, same, k, rows, width):
    tap = ext[k * SEG : k * SEG + rows, :]
    return tap if k == 3 else tap * tiled_lanes(same[k], width)


def conv_kernel(front, same, taps, bias, conv_sum, inner, ext):
    rows, width = conv_sum.shape
    earlier_rows(ext, front, rows)
    total = jnp.broadcast_to(bias[...], (rows, width))
    for k in range(4):
        total = total + taps[k : k + 1, :] * masked_tap(ext, same, k, rows, width)
    conv_sum[...] = total
    inner[...] = (total * jax.nn.sigmoid(total)).astype(jnp.bfloat16)


def conv_back_kernel(
    front, same, taps, conv_sum, inner_part, select_low, select, front_grad, early, sums, ext
):
    rows, width = conv_sum.shape
    total = conv_sum[...]
    logistic = jax.nn.sigmoid(total)
    back = lax.dot_general(
        select_low[...], select[...], (((1,), (1,)), ((), ())), preferred_element_type=jnp.float32
    )
    back = (inner_part[...] + back) * (logistic * (1.0 + total * (1.0 - logistic)))
    earlier_rows(ext, front, rows)
    for k in range(4):
        sums[k : k + 1, :] = jnp.sum(back * masked_tap(ext, same, k, rows, width), 0, keepdims=True)
    sums[4:5, :] = jnp.sum(back, 0, keepdims=True)
    sums[5:8, :] = jnp.zeros((3, width), jnp.float32)
    ext[0 : 3 * SEG, :] = jnp.zeros((3 * SEG, width), jnp.float32)
    ext[3 * SEG :, :] = back * taps[3:4, :]
    for k in range(3):
        part = back * taps[k : k + 1, :] * tiled_lanes(same[k], width)
        ext[k * SEG : k * SEG + rows, :] = ext[k * SEG : k * SEG + rows, :] + part
    place = lax.broadcasted_iota(jnp.int32, (SEG, width), 0)
    early[...] = ext[0 : 3 * SEG, :]
    for b in range(3):
        at = rows + b * SEG
        later = pltpu.roll(ext[b * SEG : (b + 1) * SEG, :], SEG - 1, 0)
        ext[at : at + SEG, :] = ext[at : at + SEG, :] + jnp.where(place < SEG - 1, later, 0.0)
    front_grad[...] = ext[3 * SEG :, :]


def expert_kernel(at, buffer, grads, up, down, returned, buffer_grad, weight_grads):
    def product(left, right, contract):
        return lax.dot_general(
            left, right, (contract, ((), ())), preferred_element_type=jnp.float32
        )

    @pl.when(pl.program_id(0) == 0)
    def _():
        returned[...] = jnp.zeros_like(returned)
        buffer_grad[...] = jnp.zeros_like(buffer_grad)

    values, cot = buffer[...], grads[...]
    ups, downs = (w[...].reshape(-1, values.shape[1]) for w in (up, down))
    hidden = product(values, ups, ((1,), (1,)))
    below = 0.5 * (1.0 + lax.erf(hidden * math.sqrt(0.5)))
    density = jnp.exp(-0.5 * hidden * hidden) * (1.0 / math.sqrt(2.0 * math.pi))
    active = (hidden * below).astype(jnp.bfloat16)
    active_grad = product(cot, downs, ((1,), (1,)))
    hidden_grad = (active_grad * (below + hidden * density)).astype(jnp.bfloat16)
    returned[...] += product(active, downs, ((1,), (0,)))
    buffer_grad[...] += product(hidden_grad, ups, ((1,), (0,)))
    pieces = weight_grads.shape[0], weight_grads.shape[3], weight_grads.shape[4]
    for k, (left, right) in enumerate(((hidden_grad, values), (active, cot))):
        weight_grads[:, 0, k] = product(left, right, ((0,), (0,))).astype(jnp.bfloat16).reshape(pieces)


def column_specs(rows, width):
    return (
        pl.BlockSpec((rows, width), lambda j: (0, j)),
        pl.BlockSpec((rows, LANE), lambda j: (0, 0)),
        pl.BlockSpec((rows, NS), lambda j: (0, 0)),
        pl.BlockSpec((NS, width), lambda j: (0, j)),
        pl.BlockSpec((NS, SEG, width), lambda j: (0, 0, j)),
        pl.BlockSpec((1, width), lambda j: (0, j)),
    )


def params(mib):
    return pltpu.CompilerParams(
        dimension_semantics=("arbitrary",), vmem_limit_bytes=mib * 2**20
    )


def cost(rows, channels, passes):
    return pl.CostEstimate(
        flops=0, bytes_accessed=int(rows * channels * passes) // 4, transcendentals=0
    )


def segment_ends(delta, driven, kept, select, rate, reverse, width=LANE):
    rows, channels = delta.shape
    block, flag, columns, state, segments, _ = column_specs(rows, width)
    return pl.pallas_call(
        functools.partial(ends_kernel, reverse),
        grid=(channels // width,),
        in_specs=[block, block, flag, columns, state],
        out_specs=[segments, segments, state, state],
        out_shape=[jax.ShapeDtypeStruct((NS, SEG, channels), jnp.float32)] * 2
        + [jax.ShapeDtypeStruct((NS, channels), jnp.float32)] * 2,
        scratch_shapes=[pltpu.VMEM((NS, rows, LANE), jnp.float32)],
        compiler_params=params(24),
        cost_estimate=cost(rows, channels, 75),
    )(delta, driven, kept, select, rate)


def scan_output(
    delta, driven, inner, gate, kept, in_select, out_select, rate, skip, pre, entry, width=LANE
):
    rows, channels = delta.shape
    block, flag, columns, state, segments, line = column_specs(rows, width)
    wide = pltpu.VMEM((NS, rows, LANE), jnp.float32)
    return pl.pallas_call(
        output_kernel,
        grid=(channels // width,),
        in_specs=[block] * 4 + [flag, columns, columns, state, line, segments, segments, state],
        out_specs=[block, block],
        out_shape=[
            jax.ShapeDtypeStruct((rows, channels), jnp.float32),
            jax.ShapeDtypeStruct((rows, channels), jnp.bfloat16),
        ],
        scratch_shapes=[wide, wide],
        compiler_params=params(24),
        cost_estimate=cost(rows, channels, 95),
    )(delta, driven, inner, gate, kept, in_select, out_select, rate, skip, *pre, entry)


def scan_adjoint(
    delta, driven, inner, grad, step_pre, kept, in_select, out_select, rate, skip, pre, entry,
    post, exit_, width=LANE,
):
    rows, channels = delta.shape
    block, flag, columns, state, segments, line = column_specs(rows, width)
    wide = pltpu.VMEM((NS, rows, LANE), jnp.float32)
    whole = pltpu.VMEM((rows, width), jnp.float32)
    return pl.pallas_call(
        adjoint_kernel,
        grid=(channels // width,),
        in_specs=[block] * 5
        + [flag, columns, columns, state, line]
        + [segments, segments, state, segments, segments, state],
        out_specs=[block, block, state, line, line, columns, columns],
        out_shape=[
            jax.ShapeDtypeStruct((rows, channels), jnp.bfloat16),
            jax.ShapeDtypeStruct((rows, channels), jnp.float32),
            jax.ShapeDtypeStruct((NS, channels), jnp.float32),
        ]
        + [jax.ShapeDtypeStruct((1, channels), jnp.float32)] * 2
        + [jax.ShapeDtypeStruct((rows, NS), jnp.float32)] * 2,
        scratch_shapes=[
            pltpu.VMEM((rows // SEG, NS, SEG, width), jnp.float32),
            wide, wide, wide, wide, whole, whole,
        ],
        compiler_params=params(40),
        cost_estimate=cost(rows, channels, 280),
    )(
        delta, driven, inner, grad, step_pre, kept, in_select, out_select, rate, skip, *pre, entry,
        *post, exit_,
    )


def conv_specs(rows, width):
    return (
        pl.BlockSpec((rows + SEG, width), lambda j: (0, j)),
        pl.BlockSpec((3, rows, LANE), lambda j: (0, 0, 0)),
        pl.BlockSpec((4, width), lambda j: (0, j)),
        pl.BlockSpec((rows, width), lambda j: (0, j)),
    )


def convolved(front, same, taps, bias, width):
    rows, channels = front.shape[0] - SEG, front.shape[1]
    ahead, flags, weights, block = conv_specs(rows, width)
    return pl.pallas_call(
        conv_kernel,
        grid=(channels // width,),
        in_specs=[ahead, flags, weights, pl.BlockSpec((1, width), lambda j: (0, j))],
        out_specs=[block, block],
        out_shape=[
            jax.ShapeDtypeStruct((rows, channels), jnp.float32),
            jax.ShapeDtypeStruct((rows, channels), jnp.bfloat16),
        ],
        scratch_shapes=[pltpu.VMEM((rows + 3 * SEG, width), jnp.float32)],
        compiler_params=params(24),
        cost_estimate=cost(rows, channels, 25),
    )(front, same, taps, bias)


def convolved_back(front, same, taps, conv_sum, inner_part, select_low, select, width):
    rows, channels = conv_sum.shape
    ahead, flags, weights, block = conv_specs(rows, width)
    inputs = select.shape[1]
    return pl.pallas_call(
        conv_back_kernel,
        grid=(channels // width,),
        in_specs=[
            ahead,
            flags,
            weights,
            block,
            block,
            pl.BlockSpec((rows, inputs), lambda j: (0, 0)),
            pl.BlockSpec((width, inputs), lambda j: (j, 0)),
        ],
        out_specs=[
            block,
            pl.BlockSpec((3 * SEG, width), lambda j: (0, j)),
            pl.BlockSpec((SEG, width), lambda j: (0, j)),
        ],
        out_shape=[
            jax.ShapeDtypeStruct((rows, channels), jnp.float32),
            jax.ShapeDtypeStruct((3 * SEG, channels), jnp.float32),
            jax.ShapeDtypeStruct((SEG, channels), jnp.float32),
        ],
        scratch_shapes=[pltpu.VMEM((rows + 3 * SEG, width), jnp.float32)],
        compiler_params=params(24),
        cost_estimate=cost(rows, channels, 40),
    )(front, same, taps, conv_sum, inner_part, select_low, select)


def expert_pass(core, buffer, grads, weights, depth):
    slots, width = buffer.shape
    devices, _, part, _ = weights.shape
    direct = part % 16 == 0
    if direct:
        tile, strip = depth, part
    else:
        tile, strip = 1, depth * part
        weights = weights.swapaxes(0, 1).reshape(1, 4, devices * part, width)
    steps = devices // depth
    whole = pl.BlockSpec((slots, width), lambda j, at: (0, 0))

    def weight(k):
        def place(j, at):
            return (j, 2 * at[0] + k, 0, 0) if direct else (0, 2 * at[0] + k, j, 0)

        return pl.BlockSpec((tile, 1, strip, width), place)

    returned, buffer_grad, weight_grads = pl.pallas_call(
        expert_kernel,
        grid_spec=pltpu.PrefetchScalarGridSpec(
            num_scalar_prefetch=1,
            grid=(steps,),
            in_specs=[whole, whole, weight(0), weight(1)],
            out_specs=[
                whole,
                whole,
                pl.BlockSpec(
                    (tile, 1, 2, strip, width),
                    lambda j, at: (lax.div(j, 2), lax.rem(j, 2), 0, 0, 0),
                ),
            ],
        ),
        out_shape=[jax.ShapeDtypeStruct((slots, width), jnp.float32)] * 2
        + [jax.ShapeDtypeStruct((steps // 2 * tile, 2, 2, strip, width), jnp.bfloat16)],
        compiler_params=params(52),
        cost_estimate=pl.CostEstimate(
            flops=12 * slots * width * devices * part,
            bytes_accessed=8 * devices * part * width,
            transcendentals=0,
        ),
    )(core.reshape(1).astype(jnp.int32), buffer, grads, weights, weights)
    if not direct:
        parts = weight_grads.reshape(steps // 2, 2, 2, depth, part, width)
        weight_grads = parts.transpose(0, 3, 1, 2, 4, 5).reshape(-1, 2, 2, part, width)
    return returned, buffer_grad, weight_grads


MODEL_WIDTH = 1152
DI = 2304
R = 72
KC = 4
EXPERT_COUNT = 2
EPS = 1e-05
REACH = KC - 1
BOTH = ("dp", "seq")
HIGHEST = lax.Precision.HIGHEST
F32 = jnp.float32
BF16 = jnp.bfloat16


def passed_along(array, axis, by):
    size = lax.axis_size(axis)
    pairs = [(i, i + by) for i in range(size) if 0 <= i + by < size]
    return lax.ppermute(array, axis, pairs)


def interleave(array):
    split = array.reshape((SEG, array.shape[0] // SEG) + array.shape[1:])
    return split.swapaxes(0, 1).reshape(array.shape)


def in_order(array):
    split = array.reshape((array.shape[0] // SEG, SEG) + array.shape[1:])
    return split.swapaxes(0, 1).reshape(array.shape)


def with_earlier(array, earlier):
    last = array[array.shape[0] - REACH * SEG :].reshape((REACH, SEG) + array.shape[1:])
    front = jnp.concatenate([earlier[:, None], last[:, : SEG - 1]], 1)
    return jnp.concatenate([front.reshape((REACH * SEG,) + array.shape[1:]), array])


def entering(decays, values, reverse):
    size, mine = lax.axis_size("seq"), lax.axis_index("seq")
    pairs = jnp.stack([jnp.concatenate(decays, 1), jnp.concatenate(values, 1)]).astype(BF16)
    gathered = lax.all_gather(pairs, "seq")
    state = jnp.zeros(pairs.shape[1:], F32)
    for k in range(size):
        at = size - 1 - k if reverse else k
        reached = at > mine if reverse else at < mine
        part = gathered[at].astype(F32)
        state = jnp.where(reached, part[0] * state + part[1], state)
    return jnp.split(state, 2, 1)


def silu_slope(value):
    logistic = jax.nn.sigmoid(value)
    return logistic * (1.0 + value * (1.0 - logistic))


def gelu_slope(value):
    return 0.5 * (1.0 + lax.erf(value / math.sqrt(2.0))) + value * jnp.exp(
        -0.5 * value * value
    ) / math.sqrt(2.0 * math.pi)


def dot(left, right, contract, precision=None):
    return lax.dot_general(
        left, right, (contract, ((), ())), precision=precision, preferred_element_type=F32
    )


def sides():
    return math.isqrt(lax.axis_size("dp") // 2)


def moved(array, axis, by=1):
    if axis == "z":
        size = lax.axis_size("seq")
        return lax.ppermute(array, "seq", [(i, (i + by) % size) for i in range(size)])
    side = sides()
    stride, size = {"core": (1, 2), "x": (2, side), "y": (2 * side, side)}[axis]
    pairs = []
    for i in range(lax.axis_size("dp")):
        at = i // stride % size
        pairs.append((i, i + stride * ((at + by) % size - at)))
    return lax.ppermute(array, "dp", pairs)


def size_of(axis):
    return lax.axis_size("seq") if axis == "z" else 2 if axis == "core" else sides()


def ring_gather(block, axis, absolute=False):
    pieces = [block]
    for k in range(1, size_of(axis)):
        pieces.append(moved(block, axis, k))
    if absolute:
        whole = jnp.zeros((len(pieces),) + block.shape, block.dtype)
        for k, piece in enumerate(pieces):
            whole = lax.dynamic_update_index_in_dim(whole, piece, depth_of(k), 0)
        return whole
    return jnp.stack(pieces)


def depth_of(k):
    size = lax.axis_size("seq")
    return lax.rem(lax.axis_index("seq") + size - k, size)


def added(left, right):
    return (left.astype(F32) + right.astype(F32)).astype(BF16)


def ring_scatter(parts, axis, absolute=False):
    size = size_of(axis)
    if absolute:
        parts = [lax.dynamic_index_in_dim(parts, depth_of(k), 0, False) for k in range(size)]
    total = parts[0].astype(F32)
    for k in range(1, size):
        total = total + moved(parts[k], axis, -k).astype(F32)
    return total.astype(BF16)


def cut_of(columns):
    return (columns // LANE + 1) // 2 * LANE


def after(value, *others):
    mark = sum(other[(0,) * other.ndim].astype(F32) for other in others)
    return jnp.where(mark != mark, jnp.zeros_like(value), value)


def wide_gather(pieces):
    cut = cut_of(pieces.shape[-1])
    left = ring_gather(pieces[..., :cut], "x")
    right = ring_gather(pieces[..., cut:], "y")
    return left, right


def last_gather(left, right):
    return ring_gather(left, "y"), ring_gather(right, "x")


def first_scatter(left, right):
    return ring_scatter(left, "y"), ring_scatter(right, "x")


def second_scatter(left, right):
    return jnp.concatenate([ring_scatter(left, "x"), ring_scatter(right, "y")], -1)


def by_place(pieces, axis):
    size = size_of(axis)
    mine = lax.axis_index("dp") // {"core": 1, "x": 2, "y": 2 * sides()}[axis]
    order = []
    for j in range(size):
        piece = pieces[size - 1]
        for k in range(size - 1):
            piece = jnp.where(lax.rem(lax.rem(mine, size) - j + size, size) == k, pieces[k], piece)
        order.append(piece)
    return order


def unit_blocks(whole, inverse=False):
    side = sides()
    dp = lax.axis_index("dp")
    at_x, at_core = lax.rem(dp // 2, side), lax.rem(dp, 2)
    parts = whole.reshape((side // 2, side, 2, -1) + whole.shape[1:])
    if inverse:
        parts = whole.reshape((2, side // 2, side, -1) + whole.shape[1:]).transpose(1, 2, 0, 3, 4)
    rows = []
    for k in range(side):
        piece = lax.dynamic_index_in_dim(parts, lax.rem(at_x - k + side, side), 1, False)
        pair = [piece[:, 0], piece[:, 1]]
        rows.append([jnp.where(at_core == 0, pair[c], pair[1 - c]) for c in range(2)])
    if inverse:
        return jnp.stack([jnp.stack(r, 1) for r in rows], 1).reshape(whole.shape)
    return [jnp.stack([r[c] for r in rows], 1).reshape((-1,) + whole.shape[1:]) for c in range(2)]


def unit_pairs():
    side, depth = sides(), lax.axis_size("seq")
    half = max(side // 2, 1)
    pairs = []
    for unit in range(lax.axis_size("dp") * depth):
        k, b = unit // 2, unit % 2
        high, low = divmod(k, side * 2 * depth)
        pairs.append((unit, (high + b * half) * side * 2 * depth + low))
    return pairs


def halved_scatter(whole):
    size, depth = lax.axis_size("dp"), lax.axis_size("seq")
    rest = whole.reshape((size, depth, -1) + whole.shape[1:])
    for axis, at in (("dp", 0), ("seq", 1)):
        count, mine = lax.axis_size(axis), lax.axis_index(axis)
        bits = [1 << k for k in range(count.bit_length() - 1)]
        for bit in bits:
            parts = rest.reshape(rest.shape[:at] + (rest.shape[at] // 2, 2) + rest.shape[at + 1 :])
            low, high = (lax.index_in_dim(parts, k, at + 1, False) for k in range(2))
            own = (mine & bit) == 0
            sent = jnp.where(own, high, low)
            got = lax.ppermute(sent, axis, [(i, i ^ bit) for i in range(count)])
            rest = added(jnp.where(own, low, high), got)
            yield rest


def units_in_order(near, far):
    side, depth = sides(), lax.axis_size("seq")
    cores = []
    for part in by_place([near, far], "core"):
        rows = by_place([part[k] for k in range(side)], "y")
        cores.append(jnp.stack([jnp.stack(by_place([r[k] for k in range(side)], "x")) for r in rows]))
    whole = jnp.stack(cores, 2)
    whole = whole.reshape(side, side, 2, depth, 2, -1, whole.shape[-1])
    whole = jnp.concatenate([whole[..., 0, :, :], whole[..., 1, :, :]], -1)
    return whole.reshape(-1, whole.shape[-1])


def plane_rows(plane):
    side, depth = sides(), lax.axis_size("seq")
    columns = plane.shape[1]
    parts = plane.reshape(side // 2, side, depth, 2, -1, columns)
    parts = jnp.stack(by_place([parts[:, k] for k in range(side)], "x"))
    parts = parts.transpose(3, 1, 0, 2, 4, 5).reshape(side * side, depth, -1, columns)
    return jnp.pad(parts, ((0, 0), (0, 0), (0, -parts.shape[2] % 32), (0, 0)))


def everywhere(array):
    for axis in ("dp", "seq"):
        size = lax.axis_size(axis)
        bit = 1
        while bit < size:
            array = array + lax.ppermute(array, axis, [(i, i ^ bit) for i in range(size)])
            bit *= 2
    return array


def per_device(
    tokens,
    doc_ids,
    token_expert,
    out_grad,
    norm_gains,
    in_proj,
    conv_weight,
    conv_bias,
    select_proj,
    step_proj,
    step_bias,
    decay_log,
    skip_gain,
    out_proj,
    router,
    expert_up,
    expert_down,
):
    rows = tokens.shape[1]
    slots_per = 5 * rows // (4 * EXPERT_COUNT)
    slots = EXPERT_COUNT * slots_per
    half = DI // 2
    wide = half // 3
    core = lax.rem(lax.axis_index("dp"), 2)
    side, depth = sides(), lax.axis_size("seq")
    both = range(2)

    last_doc = jnp.broadcast_to(doc_ids[0, rows - REACH :, None].astype(BF16), (REACH, LANE))
    prior = passed_along(jnp.concatenate([tokens[0, rows - REACH :], last_doc], 1), "seq", 1)
    prior_tokens = prior[:, :MODEL_WIDTH]
    prior_doc = prior[:, MODEL_WIDTH].astype(jnp.int32)
    lines = lax.all_gather(jnp.concatenate([norm_gains, router.T]), "dp", axis=1, tiled=True)
    gains_all = lines[:2].astype(F32)
    router_all = lines[2:].astype(F32)

    small = jnp.concatenate(
        [
            select_proj,
            step_proj.T,
            decay_log,
            conv_weight.T,
            conv_bias[:, None],
            step_bias[:, None],
            skip_gain[:, None],
        ],
        1,
    )
    columns = small.shape[1]

    small = jnp.pad(small, ((0, 0), (0, 2 * LANE - columns)))
    small = jnp.concatenate([small[:, :LANE], small[:, LANE:]])
    in_z = ring_gather(jnp.concatenate([in_proj.T, small], 1), "z", True)
    in_wide = wide_gather(in_z)
    left, right = last_gather(*in_wide)
    right = right.swapaxes(0, 1)
    rest = MODEL_WIDTH - left.shape[-1]
    in_near = jnp.concatenate([left, right[..., :rest]], -1).reshape(DI, MODEL_WIDTH)
    in_full = (in_near, moved(in_near, "core"))
    small_near = right[..., rest:]
    small_full = unit_blocks(units_in_order(small_near, moved(small_near, "core")))
    out_full = unit_blocks(lax.all_gather(out_proj, BOTH, axis=0, tiled=True))
    experts = jnp.stack([expert_up.swapaxes(1, 2), expert_down], 1)
    experts = after(experts.reshape(-1, MODEL_WIDTH), in_z)
    experts = lax.all_gather(experts, BOTH, axis=0, tiled=True)
    experts = experts.reshape(lax.axis_size("dp") * depth, 4, -1, MODEL_WIDTH)

    at = R + 2 * NS
    select_full = [w[:, :at] for w in small_full]
    step_full = [w[:, at : at + R] for w in small_full]
    line_full = [w[:, at + R : columns].astype(F32).T for w in small_full]
    decay_rate = [-jnp.exp(w[:NS]) for w in line_full]
    conv_taps = [w[NS : NS + KC] for w in line_full]
    bias_conv, bias_step, skip_wide = (
        [w[NS + KC + k][None] for w in line_full] for k in range(3)
    )

    mine = interleave(tokens[0])
    doc_row = interleave(doc_ids[0])
    route = interleave(token_expert[0, :, 0])
    out_cot = interleave(out_grad[0]).astype(F32)

    extended = jnp.concatenate([mine, prior_tokens, jnp.zeros_like(mine[: SEG - REACH])])
    stream_ext = extended.astype(F32)
    inv_ext = lax.rsqrt(jnp.mean(stream_ext * stream_ext, -1, keepdims=True) + EPS)
    hat_ext = stream_ext * inv_ext
    normed_ext = (hat_ext * gains_all[0]).astype(BF16)
    stream, inv_first, hat_first, normed = (
        a[:rows] for a in (stream_ext, inv_ext, hat_ext, normed_ext)
    )
    ext_ids = with_earlier(doc_row, prior_doc)
    same = jnp.stack(
        [(ext_ids[k * SEG : k * SEG + rows] == doc_row).astype(F32) for k in range(REACH)]
    )
    same = jnp.broadcast_to(same[:, :, None], (REACH, rows, LANE))
    kept = same[REACH - 1]

    strip = DI // side
    front, gate, conv_sum, inner = [], [], [], []
    for h in both:
        proj = dot(normed_ext, in_full[h], ((1,), (1,))).astype(BF16)
        parts = by_place([proj[:, k * strip : (k + 1) * strip] for k in range(side)], "y")
        front.append(jnp.concatenate(parts[: side // 2], 1))
        gate.append(jnp.concatenate(parts[side // 2 :], 1)[:rows])
        made = convolved(front[h], same, conv_taps[h], bias_conv[h], wide)
        conv_sum.append(made[0])
        inner.append(made[1])
    select = sum(dot(inner[h], select_full[h], ((1,), (0,))) for h in both)
    steps_low = select[:, :R].astype(BF16)
    in_select = select[:, R : R + NS]
    out_select = select[:, R + NS :]
    step_pre = [dot(steps_low, step_full[h], ((1,), (1,))) + bias_step[h] for h in both]
    delta = [jax.nn.softplus(p) for p in step_pre]
    driven = [d * x.astype(F32) for d, x in zip(delta, inner)]
    rate = [r * math.log2(math.e) for r in decay_rate]

    ends = [
        segment_ends(delta[h], driven[h], kept, in_select, rate[h], False, wide) for h in both
    ]
    pre = [e[:2] for e in ends]
    state_in = entering([e[2] for e in ends], [e[3] for e in ends], False)
    scanned, gated = zip(
        *(
            scan_output(
                delta[h], driven[h], inner[h], gate[h], kept, in_select, out_select, rate[h],
                skip_wide[h], pre[h], state_in[h], wide,
            )
            for h in both
        )
    )
    mixed = sum(dot(gated[h], out_full[h], ((1,), (0,))) for h in both)
    resid = stream + mixed
    inv_second = lax.rsqrt(jnp.mean(resid * resid, -1, keepdims=True) + EPS)
    hat_second = resid * inv_second
    normed_moe = (hat_second * gains_all[1]).astype(BF16)
    normed_wide = normed_moe.astype(F32)
    logits = dot(normed_wide, router_all, ((1,), (1,)), HIGHEST)
    probs = jax.nn.softmax(logits, -1)
    route_hot = route[:, None] == jnp.arange(EXPERT_COUNT, dtype=jnp.int32)[None, :]
    hot_wide = route_hot.astype(F32)
    chosen = jnp.sum(probs * hot_wide, 1, keepdims=True)
    place = jnp.arange(rows, dtype=jnp.int32)
    lower = (place[:, None] >= place[None, :]).astype(BF16)
    rank_in = dot(lower, route_hot.astype(BF16), ((1,), (0,))) - 1.0
    slot = jnp.sum(rank_in * hot_wide, 1).astype(jnp.int32)
    target = jnp.where(route == core, 0, slots_per) + slot
    pick = (jnp.arange(slots, dtype=jnp.int32)[:, None] == target[None, :]).astype(BF16)
    returned_grad = (chosen * out_cot).astype(BF16)
    placed = dot(pick, jnp.concatenate([normed_moe, returned_grad], 1), ((1,), (0,))).astype(BF16)
    placed = jnp.concatenate([placed[:slots_per], moved(placed[slots_per:], "core")])
    buffer, grad_slots = placed[:, :MODEL_WIDTH], placed[:, MODEL_WIDTH:]

    def from_slots(parts):
        parts = jnp.concatenate([parts[:slots_per], moved(parts[slots_per:], "core")])
        return dot(pick.astype(F32), parts, ((0,), (0,)), HIGHEST)

    gated_other = moved(gated[1], "core")
    returned, buffer_grad, expert_grads = expert_pass(core, buffer, grad_slots, experts, depth)
    returned = from_slots(returned)
    buffer_grad = from_slots(buffer_grad)
    groups = [list(range(c, lax.axis_size("dp"), 2)) for c in range(2)]
    expert_sum = lax.psum_scatter(
        expert_grads, "dp", scatter_dimension=0, tiled=True, axis_index_groups=groups
    )
    branch = chosen * returned
    layer_out = (resid + branch).astype(BF16)
    squared_values = jnp.stack(
        [jnp.sum(resid * resid), jnp.sum(mixed * mixed), jnp.sum(branch * branch)]
    )
    chosen_grad = jnp.sum(out_cot * returned, 1, keepdims=True)
    logit_grad = chosen_grad * chosen * (hot_wide - probs)
    grad_router = dot(logit_grad, normed_wide, ((0,), (0,)), HIGHEST)
    moe_grad = buffer_grad + dot(logit_grad, router_all, ((1,), (0,)), HIGHEST)
    second_gain_grad = jnp.sum(moe_grad * hat_second, 0)
    scaled_second = moe_grad * gains_all[1]
    resid_grad = out_cot + inv_second * (
        scaled_second - hat_second * jnp.mean(scaled_second * hat_second, -1, keepdims=True)
    )
    mixed_grad = resid_grad.astype(BF16)
    crossed = moved(jnp.concatenate([mixed_grad, normed]), "core")
    gated_near = jnp.concatenate([gated[0], gated_other])
    grad_out = dot(gated_near, jnp.concatenate([mixed_grad, crossed[:rows]]), ((0,), (0,)))
    gated_grad = [dot(mixed_grad, out_full[h], ((1,), (1,))) for h in both]
    gates = [g.astype(F32) for g in gate]
    scan_grad = [gated_grad[h] * jax.nn.silu(gates[h]) for h in both]
    gate_grad = [(gated_grad[h] * scanned[h] * silu_slope(gates[h])).astype(BF16) for h in both]
    ends = [
        segment_ends(delta[h], scan_grad[h], kept, out_select, rate[h], True, wide) for h in both
    ]
    post = [e[:2] for e in ends]
    adjoint_in = entering([e[2] for e in ends], [e[3] for e in ends], True)
    out_sum = lax.psum_scatter(
        plane_rows(grad_out.astype(BF16)), "dp", scatter_dimension=0, tiled=True,
        axis_index_groups=groups,
    )[0]
    expert_sum = expert_sum.reshape(depth, -1, MODEL_WIDTH)
    own_rows = expert_sum.shape[1]
    both_sum = lax.psum_scatter(
        jnp.concatenate([expert_sum, out_sum], 1), "seq", scatter_dimension=0, tiled=True
    )[0]
    out_sum = both_sum[own_rows : own_rows + out_proj.shape[0]]
    out_sum = lax.ppermute(out_sum, BOTH, [(b, a) for a, b in unit_pairs()]).astype(F32)
    expert_sum = both_sum[:own_rows].reshape(2, 2, -1, MODEL_WIDTH)
    mine_sum = jnp.where(core == 0, expert_sum[0], expert_sum[1])
    other_sum = moved(jnp.where(core == 0, expert_sum[1], expert_sum[0]), "core")
    expert_sum = jnp.stack(
        [jnp.where(core == e, mine_sum, other_sum) for e in range(EXPERT_COUNT)]
    ).astype(F32)
    rate = [after(r, grad_out) for r in rate]
    made = [
        scan_adjoint(
            delta[h], driven[h], inner[h], scan_grad[h], step_pre[h], kept, in_select, out_select,
            rate[h], skip_wide[h], pre[h], state_in[h], post[h], adjoint_in[h], wide,
        )
        for h in both
    ]
    pre_low, inner_part, rate_sum, step_sum, skip_sum, in_grad, out_grads = map(list, zip(*made))
    steps_grad = sum(dot(pre_low[h], step_full[h], ((1,), (0,))) for h in both)
    select_low = jnp.concatenate(
        [steps_grad, in_grad[0] + in_grad[1], out_grads[0] + out_grads[1]], 1
    ).astype(BF16)
    front_grad, early, tap_sums = zip(
        *(
            convolved_back(
                front[h], same, conv_taps[h], conv_sum[h], inner_part[h], select_low,
                select_full[h], wide,
            )
            for h in both
        )
    )
    grad_small = []
    for h in both:
        lines = [rate_sum[h] * decay_rate[h], tap_sums[h][: KC + 1], step_sum[h], skip_sum[h]]
        grad_small.append(
            jnp.concatenate(
                [
                    dot(inner[h], select_low, ((0,), (0,))),
                    dot(pre_low[h], steps_low, ((0,), (0,))),
                    jnp.concatenate(lines).T,
                    jnp.zeros((half, -columns % LANE), F32),
                ],
                1,
            ).astype(BF16)
        )
    proj_grad = []
    for h in both:
        incoming = passed_along(early[h].reshape(REACH, SEG, half)[:, 0], "seq", -1)
        tail = jnp.pad(incoming[:, None], ((0, 0), (SEG - 1, 0), (0, 0)))
        tail = jnp.pad(tail.reshape(REACH * SEG, half), ((rows - REACH * SEG, 0), (0, 0)))
        whole = jnp.concatenate([(front_grad[h] + tail).astype(BF16), gate_grad[h]], 1)
        parts = [whole[:, k * strip : (k + 1) * strip] for k in range(side)]
        proj_grad.append(jnp.concatenate(by_place(parts, "y"), 1))
    proj_other = moved(proj_grad[1], "core")
    grad_in = dot(
        jnp.concatenate([proj_grad[0], proj_other]),
        jnp.concatenate([normed, crossed[rows:]]),
        ((0,), (0,)),
    ).astype(BF16)
    in_plane = grad_in.reshape(side, side, depth, -1, MODEL_WIDTH)
    cut = cut_of(MODEL_WIDTH)
    in_plane = first_scatter(in_plane[..., :cut], in_plane[..., cut:].swapaxes(0, 1))
    grad_small = [after(g, grad_in) for g in grad_small]
    normed_grad = sum(dot(proj_grad[h], in_full[h], ((1,), (0,))) for h in both)
    first_gain_grad = jnp.sum(normed_grad * hat_first, 0)
    scaled_first = normed_grad * gains_all[0]
    stream_grad = resid_grad + inv_first * (
        scaled_first - hat_first * jnp.mean(scaled_first * hat_first, -1, keepdims=True)
    )

    parts, width = lax.axis_size("dp"), MODEL_WIDTH // lax.axis_size("dp")
    unit = DI // (parts * depth)
    shared = jnp.concatenate([first_gain_grad[None], second_gain_grad[None], grad_router])
    shared = shared.reshape(4, parts, width).swapaxes(0, 1).reshape(parts, 1, 4 * width)
    extra = -(-4 * width // unit)
    shared = jnp.pad(shared, ((0, 0), (0, 0), (0, extra * unit - 4 * width)))
    shared = jnp.broadcast_to(shared, (parts, depth, extra * unit)).reshape(DI, extra)
    whole = unit_blocks(jnp.concatenate(grad_small), True)
    shared = jnp.pad(shared, ((0, 0), (columns, whole.shape[1] - columns - extra)))
    *_, small_sum = halved_scatter(whole + shared.astype(BF16))
    in_last = second_scatter(*in_plane)
    in_sum = ring_scatter(in_last, "z", True).astype(F32)
    squared_values = after(squared_values, in_last)
    small_sum = small_sum.reshape(unit, -1).astype(F32)
    line_sum = small_sum[:, at + R : columns]
    shared = small_sum[:, columns : columns + extra].reshape(-1)[: 4 * width].reshape(4, width)
    square_total = everywhere(jnp.pad(squared_values, (0, LANE - 3))[None])[0, :3]
    stats = jnp.sqrt(square_total / (rows * parts * depth * MODEL_WIDTH))
    return (
        in_order(layer_out)[None],
        in_order(stream_grad.astype(BF16))[None],
        shared[:2],
        in_sum.T,
        line_sum[:, NS : NS + KC].T,
        line_sum[:, NS + KC],
        small_sum[:, :at],
        small_sum[:, at : at + R].T,
        line_sum[:, NS + KC + 1],
        line_sum[:, :NS],
        line_sum[:, NS + KC + 2],
        out_sum,
        shared[2:].T,
        expert_sum[:, 0].swapaxes(1, 2),
        expert_sum[:, 1],
        stats,
    )


def solution(mesh):
    return jax.shard_map(
        per_device,
        mesh=mesh,
        in_specs=(
            P("dp", "seq", None),
            P("dp", "seq"),
            P("dp", "seq", None),
            P("dp", "seq", None),
            P(None, "dp"),
            P(None, ("dp", "seq")),
            P(None, ("dp", "seq")),
            P(("dp", "seq")),
            P(("dp", "seq"), None),
            P(None, ("dp", "seq")),
            P(("dp", "seq")),
            P(("dp", "seq"), None),
            P(("dp", "seq")),
            P(("dp", "seq"), None),
            P("dp", None),
            P(None, None, ("dp", "seq")),
            P(None, ("dp", "seq"), None),
        ),
        out_specs=(
            P("dp", "seq", None),
            P("dp", "seq", None),
            P(None, "dp"),
            P(None, ("dp", "seq")),
            P(None, ("dp", "seq")),
            P(("dp", "seq")),
            P(("dp", "seq"), None),
            P(None, ("dp", "seq")),
            P(("dp", "seq")),
            P(("dp", "seq"), None),
            P(("dp", "seq")),
            P(("dp", "seq"), None),
            P("dp", None),
            P(None, None, ("dp", "seq")),
            P(None, ("dp", "seq"), None),
            P(),
        ),
        check_vma=False,
    )
```

```python
import functools, math
import jax
import jax.numpy as jnp
from jax import lax
from jax.experimental import pallas as pl
from jax.experimental.pallas import tpu as pltpu
from jax.sharding import PartitionSpec as P

NS = 16
SEG = 8
LANE = 128
FAR = 1e30


def spread_columns(wide, columns):
    for n in range(NS):
        wide[n] = jnp.broadcast_to(columns[:, n : n + 1], wide.shape[1:])


def rows_of(i):
    return pl.ds(pl.multiple_of(i * SEG, SEG), SEG)


def rate_rows(rate):
    return [jnp.broadcast_to(rate[n : n + 1, :], (SEG, rate.shape[1])) for n in range(NS)]


def tiled_lanes(block, width):
    return block if width == LANE else jnp.concatenate([block] * (width // LANE), 1)


def prefix_pairs(decay, value, reverse):
    place = lax.broadcasted_iota(jnp.int32, decay.shape, 0)

    def shifted(array, by, fill):
        if reverse:
            return jnp.where(place < SEG - by, pltpu.roll(array, SEG - by, 0), fill)
        return jnp.where(place >= by, pltpu.roll(array, by, 0), fill)

    for by in (1, 2, 4):
        value = decay * shifted(value, by, 0.0) + value
        decay = decay * shifted(decay, by, 1.0)
    last = slice(0, 1) if reverse else slice(SEG - 1, SEG)
    return shifted(decay, 1, 1.0), shifted(value, 1, 0.0), decay[last], value[last]


def ends_kernel(
    reverse, delta, driven, kept, select, rate, pre_decay, pre_value, all_decay, all_value, wide
):
    @pl.when(pl.program_id(0) == 0)
    def _():
        spread_columns(wide, select)

    width = delta.shape[1]
    length = delta.shape[0] // SEG
    rates = rate_rows(rate)
    zero = jnp.zeros((SEG, width), jnp.float32)

    def step(k, carry):
        total, states = carry
        i = length - 1 - k if reverse else k
        rows = rows_of(i)
        reach = jnp.where(tiled_lanes(kept[rows, :], width) > 0, delta[rows, :], FAR)
        drive = driven[rows, :]
        new = []
        for n in range(NS):
            factor = jnp.exp2(reach * rates[n])
            term = drive * tiled_lanes(wide[n, rows, :], width)
            new.append(factor * (states[n] + term) if reverse else factor * states[n] + term)
        return total + reach, tuple(new)

    total, states = lax.fori_loop(0, length, step, (zero, (zero,) * NS))
    for n in range(NS):
        before_decay, before_value, whole_decay, whole_value = prefix_pairs(
            jnp.exp2(total * rates[n]), states[n], reverse
        )
        pre_decay[n] = before_decay
        pre_value[n] = before_value
        all_decay[n : n + 1, :] = whole_decay
        all_value[n : n + 1, :] = whole_value


def output_kernel(
    delta, driven, inner, gate, kept, in_select, out_select, rate, skip, pre_decay, pre_value,
    entry, scanned, gated, wide_in, wide_out,
):
    @pl.when(pl.program_id(0) == 0)
    def _():
        spread_columns(wide_in, in_select)
        spread_columns(wide_out, out_select)

    width = delta.shape[1]
    length = delta.shape[0] // SEG
    rates = rate_rows(rate)
    start = tuple(pre_decay[n] * entry[n : n + 1, :] + pre_value[n] for n in range(NS))

    def step(i, states):
        rows = rows_of(i)
        reach = jnp.where(tiled_lanes(kept[rows, :], width) > 0, delta[rows, :], FAR)
        drive = driven[rows, :]
        new, parts = [], [0.0] * 4
        for n in range(NS):
            state = jnp.exp2(reach * rates[n]) * states[n] + drive * tiled_lanes(
                wide_in[n, rows, :], width
            )
            parts[n % 4] = parts[n % 4] + state * tiled_lanes(wide_out[n, rows, :], width)
            new.append(state)
        scanned[rows, :] = (parts[0] + parts[1]) + (parts[2] + parts[3])
        return tuple(new)

    lax.fori_loop(0, length, step, start)
    value = scanned[...] + skip[...] * inner[...].astype(jnp.float32)
    scanned[...] = value
    half = gate[...].astype(jnp.float32)
    gated[...] = (value * (half * jax.nn.sigmoid(half))).astype(jnp.bfloat16)


def adjoint_kernel(
    delta, driven, inner, grad, step_pre, kept, in_select, out_select, rate, skip, pre_decay,
    pre_value, entry, post_decay, post_value, exit_, pre_low, inner_part, rate_sum, step_sum,
    skip_sum, in_grad, out_grad, states, wide_in, wide_out, in_total, out_total, inner_grad,
    delta_grad,
):
    j = pl.program_id(0)

    @pl.when(j == 0)
    def _():
        spread_columns(wide_in, in_select)
        spread_columns(wide_out, out_select)
        in_total[...] = jnp.zeros_like(in_total)
        out_total[...] = jnp.zeros_like(out_total)

    width = delta.shape[1]
    length = delta.shape[0] // SEG
    rates = rate_rows(rate)
    start = tuple(pre_decay[n] * entry[n : n + 1, :] + pre_value[n] for n in range(NS))

    def folded(value):
        return sum(value[:, k : k + LANE] for k in range(0, width, LANE))

    def advance(i, carry):
        rows = rows_of(i)
        reach = jnp.where(tiled_lanes(kept[rows, :], width) > 0, delta[rows, :], FAR)
        drive, grad_t = driven[rows, :], grad[rows, :]
        new = []
        for n in range(NS):
            states[i, n] = carry[n]
            state = jnp.exp2(reach * rates[n]) * carry[n] + drive * tiled_lanes(
                wide_in[n, rows, :], width
            )
            out_total[n, rows, :] = out_total[n, rows, :] + folded(grad_t * state)
            new.append(state)
        return tuple(new)

    lax.fori_loop(0, length, advance, start)
    back = tuple(post_decay[n] * exit_[n : n + 1, :] + post_value[n] for n in range(NS))
    zero = jnp.zeros((SEG, width), jnp.float32)

    def retreat(k, carry):
        backs, sums = carry
        i = length - 1 - k
        rows = rows_of(i)
        step_t = delta[rows, :]
        reach = jnp.where(tiled_lanes(kept[rows, :], width) > 0, step_t, FAR)
        drive, grad_t = driven[rows, :], grad[rows, :]
        new_backs, new_sums = [], []
        weighted, slope = [0.0] * 2, [0.0] * 2
        for n in range(NS):
            adjoint = grad_t * tiled_lanes(wide_out[n, rows, :], width) + backs[n]
            passed = jnp.exp2(reach * rates[n]) * adjoint
            through = passed * states[i, n]
            weighted[n % 2] = weighted[n % 2] + adjoint * tiled_lanes(wide_in[n, rows, :], width)
            slope[n % 2] = slope[n % 2] + through * rates[n]
            in_total[n, rows, :] = in_total[n, rows, :] + folded(adjoint * drive)
            new_backs.append(passed)
            new_sums.append(sums[n] + through * step_t)
        inner_grad[rows, :] = weighted[0] + weighted[1]
        delta_grad[rows, :] = slope[0] + slope[1]
        return tuple(new_backs), tuple(new_sums)

    _, sums = lax.fori_loop(0, length, retreat, (back, (zero,) * NS))
    for n in range(NS):
        rate_sum[n : n + 1, :] = jnp.sum(sums[n], 0, keepdims=True)
    weighted, value, grads = inner_grad[...], inner[...].astype(jnp.float32), grad[...]
    slope = weighted * value + delta_grad[...] * math.log(2.0)
    pre = slope * jax.nn.sigmoid(step_pre[...])
    pre_low[...] = pre.astype(jnp.bfloat16)
    step_sum[...] = jnp.sum(pre, 0, keepdims=True)
    skip_sum[...] = jnp.sum(grads * value, 0, keepdims=True)
    inner_part[...] = grads * skip[...] + weighted * delta[...]

    @pl.when(j == pl.num_programs(0) - 1)
    def _():
        place = lax.broadcasted_iota(jnp.int32, in_grad.shape, 1)
        for total, result in ((in_total, in_grad), (out_total, out_grad)):
            value = jnp.zeros(result.shape, jnp.float32)
            for n in range(NS):
                column = jnp.sum(total[n], 1, keepdims=True)
                value = jnp.where(place == n, column, value)
            result[...] = value


def earlier_rows(ext, front, rows):
    own = front[0:rows, :].astype(jnp.float32)
    halo = front[rows : rows + SEG, :].astype(jnp.float32)
    place = lax.broadcasted_iota(jnp.int32, (SEG, own.shape[1]), 0)
    for b in range(3):
        at = rows - (3 - b) * SEG
        group = pltpu.roll(own[at : at + SEG], 1, 0)
        ext[b * SEG : (b + 1) * SEG, :] = jnp.where(place == 0, halo[b : b + 1], group)
    ext[3 * SEG :, :] = own


def masked_tap(ext, same, k, rows, width):
    tap = ext[k * SEG : k * SEG + rows, :]
    return tap if k == 3 else tap * tiled_lanes(same[k], width)


def conv_kernel(front, same, taps, bias, conv_sum, inner, ext):
    rows, width = conv_sum.shape
    earlier_rows(ext, front, rows)
    total = jnp.broadcast_to(bias[...], (rows, width))
    for k in range(4):
        total = total + taps[k : k + 1, :] * masked_tap(ext, same, k, rows, width)
    conv_sum[...] = total
    inner[...] = (total * jax.nn.sigmoid(total)).astype(jnp.bfloat16)


def conv_back_kernel(
    front, same, taps, conv_sum, inner_part, select_low, select, front_grad, early, sums, ext
):
    rows, width = conv_sum.shape
    total = conv_sum[...]
    logistic = jax.nn.sigmoid(total)
    back = lax.dot_general(
        select_low[...], select[...], (((1,), (1,)), ((), ())), preferred_element_type=jnp.float32
    )
    back = (inner_part[...] + back) * (logistic * (1.0 + total * (1.0 - logistic)))
    earlier_rows(ext, front, rows)
    for k in range(4):
        sums[k : k + 1, :] = jnp.sum(back * masked_tap(ext, same, k, rows, width), 0, keepdims=True)
    sums[4:5, :] = jnp.sum(back, 0, keepdims=True)
    sums[5:8, :] = jnp.zeros((3, width), jnp.float32)
    ext[0 : 3 * SEG, :] = jnp.zeros((3 * SEG, width), jnp.float32)
    ext[3 * SEG :, :] = back * taps[3:4, :]
    for k in range(3):
        part = back * taps[k : k + 1, :] * tiled_lanes(same[k], width)
        ext[k * SEG : k * SEG + rows, :] = ext[k * SEG : k * SEG + rows, :] + part
    place = lax.broadcasted_iota(jnp.int32, (SEG, width), 0)
    early[...] = ext[0 : 3 * SEG, :]
    for b in range(3):
        at = rows + b * SEG
        later = pltpu.roll(ext[b * SEG : (b + 1) * SEG, :], SEG - 1, 0)
        ext[at : at + SEG, :] = ext[at : at + SEG, :] + jnp.where(place < SEG - 1, later, 0.0)
    front_grad[...] = ext[3 * SEG :, :]


def expert_kernel(at, buffer, grads, up, down, returned, buffer_grad, weight_grads):
    def product(left, right, contract):
        return lax.dot_general(
            left, right, (contract, ((), ())), preferred_element_type=jnp.float32
        )

    @pl.when(pl.program_id(0) == 0)
    def _():
        returned[...] = jnp.zeros_like(returned)
        buffer_grad[...] = jnp.zeros_like(buffer_grad)

    values, cot = buffer[...], grads[...]
    ups, downs = (w[...].reshape(-1, values.shape[1]) for w in (up, down))
    hidden = product(values, ups, ((1,), (1,)))
    below = 0.5 * (1.0 + lax.erf(hidden * math.sqrt(0.5)))
    density = jnp.exp(-0.5 * hidden * hidden) * (1.0 / math.sqrt(2.0 * math.pi))
    active = (hidden * below).astype(jnp.bfloat16)
    active_grad = product(cot, downs, ((1,), (1,)))
    hidden_grad = (active_grad * (below + hidden * density)).astype(jnp.bfloat16)
    returned[...] += product(active, downs, ((1,), (0,)))
    buffer_grad[...] += product(hidden_grad, ups, ((1,), (0,)))
    pieces = weight_grads.shape[0], weight_grads.shape[2], weight_grads.shape[3]
    for k, (left, right) in enumerate(((hidden_grad, values), (active, cot))):
        weight_grads[:, k] = product(left, right, ((0,), (0,))).astype(jnp.bfloat16).reshape(pieces)


def column_specs(rows, width):
    return (
        pl.BlockSpec((rows, width), lambda j: (0, j)),
        pl.BlockSpec((rows, LANE), lambda j: (0, 0)),
        pl.BlockSpec((rows, NS), lambda j: (0, 0)),
        pl.BlockSpec((NS, width), lambda j: (0, j)),
        pl.BlockSpec((NS, SEG, width), lambda j: (0, 0, j)),
        pl.BlockSpec((1, width), lambda j: (0, j)),
    )


def params(mib):
    return pltpu.CompilerParams(
        dimension_semantics=("arbitrary",), vmem_limit_bytes=mib * 2**20
    )


def cost(rows, channels, passes):
    return pl.CostEstimate(
        flops=0, bytes_accessed=int(rows * channels * passes) // 4, transcendentals=0
    )


def segment_ends(delta, driven, kept, select, rate, reverse, width=LANE):
    rows, channels = delta.shape
    block, flag, columns, state, segments, _ = column_specs(rows, width)
    return pl.pallas_call(
        functools.partial(ends_kernel, reverse),
        grid=(channels // width,),
        in_specs=[block, block, flag, columns, state],
        out_specs=[segments, segments, state, state],
        out_shape=[jax.ShapeDtypeStruct((NS, SEG, channels), jnp.float32)] * 2
        + [jax.ShapeDtypeStruct((NS, channels), jnp.float32)] * 2,
        scratch_shapes=[pltpu.VMEM((NS, rows, LANE), jnp.float32)],
        compiler_params=params(24),
        cost_estimate=cost(rows, channels, 75),
    )(delta, driven, kept, select, rate)


def scan_output(
    delta, driven, inner, gate, kept, in_select, out_select, rate, skip, pre, entry, width=LANE
):
    rows, channels = delta.shape
    block, flag, columns, state, segments, line = column_specs(rows, width)
    wide = pltpu.VMEM((NS, rows, LANE), jnp.float32)
    return pl.pallas_call(
        output_kernel,
        grid=(channels // width,),
        in_specs=[block] * 4 + [flag, columns, columns, state, line, segments, segments, state],
        out_specs=[block, block],
        out_shape=[
            jax.ShapeDtypeStruct((rows, channels), jnp.float32),
            jax.ShapeDtypeStruct((rows, channels), jnp.bfloat16),
        ],
        scratch_shapes=[wide, wide],
        compiler_params=params(24),
        cost_estimate=cost(rows, channels, 95),
    )(delta, driven, inner, gate, kept, in_select, out_select, rate, skip, *pre, entry)


def scan_adjoint(
    delta, driven, inner, grad, step_pre, kept, in_select, out_select, rate, skip, pre, entry,
    post, exit_, width=LANE,
):
    rows, channels = delta.shape
    block, flag, columns, state, segments, line = column_specs(rows, width)
    wide = pltpu.VMEM((NS, rows, LANE), jnp.float32)
    whole = pltpu.VMEM((rows, width), jnp.float32)
    return pl.pallas_call(
        adjoint_kernel,
        grid=(channels // width,),
        in_specs=[block] * 5
        + [flag, columns, columns, state, line]
        + [segments, segments, state, segments, segments, state],
        out_specs=[block, block, state, line, line, columns, columns],
        out_shape=[
            jax.ShapeDtypeStruct((rows, channels), jnp.bfloat16),
            jax.ShapeDtypeStruct((rows, channels), jnp.float32),
            jax.ShapeDtypeStruct((NS, channels), jnp.float32),
        ]
        + [jax.ShapeDtypeStruct((1, channels), jnp.float32)] * 2
        + [jax.ShapeDtypeStruct((rows, NS), jnp.float32)] * 2,
        scratch_shapes=[
            pltpu.VMEM((rows // SEG, NS, SEG, width), jnp.float32),
            wide, wide, wide, wide, whole, whole,
        ],
        compiler_params=params(40),
        cost_estimate=cost(rows, channels, 280),
    )(
        delta, driven, inner, grad, step_pre, kept, in_select, out_select, rate, skip, *pre, entry,
        *post, exit_,
    )


def conv_specs(rows, width):
    return (
        pl.BlockSpec((rows + SEG, width), lambda j: (0, j)),
        pl.BlockSpec((3, rows, LANE), lambda j: (0, 0, 0)),
        pl.BlockSpec((4, width), lambda j: (0, j)),
        pl.BlockSpec((rows, width), lambda j: (0, j)),
    )


def convolved(front, same, taps, bias, width):
    rows, channels = front.shape[0] - SEG, front.shape[1]
    ahead, flags, weights, block = conv_specs(rows, width)
    return pl.pallas_call(
        conv_kernel,
        grid=(channels // width,),
        in_specs=[ahead, flags, weights, pl.BlockSpec((1, width), lambda j: (0, j))],
        out_specs=[block, block],
        out_shape=[
            jax.ShapeDtypeStruct((rows, channels), jnp.float32),
            jax.ShapeDtypeStruct((rows, channels), jnp.bfloat16),
        ],
        scratch_shapes=[pltpu.VMEM((rows + 3 * SEG, width), jnp.float32)],
        compiler_params=params(24),
        cost_estimate=cost(rows, channels, 25),
    )(front, same, taps, bias)


def convolved_back(front, same, taps, conv_sum, inner_part, select_low, select, width):
    rows, channels = conv_sum.shape
    ahead, flags, weights, block = conv_specs(rows, width)
    inputs = select.shape[1]
    return pl.pallas_call(
        conv_back_kernel,
        grid=(channels // width,),
        in_specs=[
            ahead,
            flags,
            weights,
            block,
            block,
            pl.BlockSpec((rows, inputs), lambda j: (0, 0)),
            pl.BlockSpec((width, inputs), lambda j: (j, 0)),
        ],
        out_specs=[
            block,
            pl.BlockSpec((3 * SEG, width), lambda j: (0, j)),
            pl.BlockSpec((SEG, width), lambda j: (0, j)),
        ],
        out_shape=[
            jax.ShapeDtypeStruct((rows, channels), jnp.float32),
            jax.ShapeDtypeStruct((3 * SEG, channels), jnp.float32),
            jax.ShapeDtypeStruct((SEG, channels), jnp.float32),
        ],
        scratch_shapes=[pltpu.VMEM((rows + 3 * SEG, width), jnp.float32)],
        compiler_params=params(24),
        cost_estimate=cost(rows, channels, 40),
    )(front, same, taps, conv_sum, inner_part, select_low, select)


def expert_pass(core, buffer, grads, weights, depth):
    slots, width = buffer.shape
    devices, _, part, _ = weights.shape
    direct = part % 16 == 0
    if direct:
        tile, strip = depth, part
    else:
        tile, strip = 1, depth * part
        weights = weights.swapaxes(0, 1).reshape(1, 4, devices * part, width)
    steps = devices // depth
    whole = pl.BlockSpec((slots, width), lambda j, at: (0, 0))

    def weight(k):
        def place(j, at):
            return (j, 2 * at[0] + k, 0, 0) if direct else (0, 2 * at[0] + k, j, 0)

        return pl.BlockSpec((tile, 1, strip, width), place)

    returned, buffer_grad, weight_grads = pl.pallas_call(
        expert_kernel,
        grid_spec=pltpu.PrefetchScalarGridSpec(
            num_scalar_prefetch=1,
            grid=(steps,),
            in_specs=[whole, whole, weight(0), weight(1)],
            out_specs=[
                whole,
                whole,
                pl.BlockSpec(
                    (tile, 2, strip, width), lambda j, at: (lax.div(j, 2), lax.rem(j, 2), 0, 0)
                ),
            ],
        ),
        out_shape=[jax.ShapeDtypeStruct((slots, width), jnp.float32)] * 2
        + [jax.ShapeDtypeStruct((steps // 2 * tile, 5, strip, width), jnp.bfloat16)],
        compiler_params=params(52),
        cost_estimate=pl.CostEstimate(
            flops=12 * slots * width * devices * part,
            bytes_accessed=8 * devices * part * width,
            transcendentals=0,
        ),
    )(core.reshape(1).astype(jnp.int32), buffer, grads, weights, weights)
    if not direct:
        parts = weight_grads.reshape(steps // 2, 5, depth, part, width)
        weight_grads = parts.swapaxes(1, 2).reshape(-1, 5, part, width)
    return returned, buffer_grad, weight_grads


MODEL_WIDTH = 1152
DI = 2304
R = 72
KC = 4
EXPERT_COUNT = 2
EPS = 1e-05
REACH = KC - 1
BOTH = ("dp", "seq")
HIGHEST = lax.Precision.HIGHEST
F32 = jnp.float32
BF16 = jnp.bfloat16


def passed_along(array, axis, by):
    size = lax.axis_size(axis)
    pairs = [(i, i + by) for i in range(size) if 0 <= i + by < size]
    return lax.ppermute(array, axis, pairs)


def interleave(array):
    split = array.reshape((SEG, array.shape[0] // SEG) + array.shape[1:])
    return split.swapaxes(0, 1).reshape(array.shape)


def in_order(array):
    split = array.reshape((array.shape[0] // SEG, SEG) + array.shape[1:])
    return split.swapaxes(0, 1).reshape(array.shape)


def with_earlier(array, earlier):
    last = array[array.shape[0] - REACH * SEG :].reshape((REACH, SEG) + array.shape[1:])
    front = jnp.concatenate([earlier[:, None], last[:, : SEG - 1]], 1)
    return jnp.concatenate([front.reshape((REACH * SEG,) + array.shape[1:]), array])


def entering(decays, values, reverse):
    size, mine = lax.axis_size("seq"), lax.axis_index("seq")
    pairs = jnp.stack([jnp.concatenate(decays, 1), jnp.concatenate(values, 1)]).astype(BF16)
    gathered = lax.all_gather(pairs, "seq")
    state = jnp.zeros(pairs.shape[1:], F32)
    for k in range(size):
        at = size - 1 - k if reverse else k
        reached = at > mine if reverse else at < mine
        part = gathered[at].astype(F32)
        state = jnp.where(reached, part[0] * state + part[1], state)
    return jnp.split(state, 2, 1)


def silu_slope(value):
    logistic = jax.nn.sigmoid(value)
    return logistic * (1.0 + value * (1.0 - logistic))


def gelu_slope(value):
    return 0.5 * (1.0 + lax.erf(value / math.sqrt(2.0))) + value * jnp.exp(
        -0.5 * value * value
    ) / math.sqrt(2.0 * math.pi)


def dot(left, right, contract, precision=None):
    return lax.dot_general(
        left, right, (contract, ((), ())), precision=precision, preferred_element_type=F32
    )


def sides():
    return math.isqrt(lax.axis_size("dp") // 2)


def moved(array, axis, by=1):
    if axis == "z":
        size = lax.axis_size("seq")
        return lax.ppermute(array, "seq", [(i, (i + by) % size) for i in range(size)])
    side = sides()
    stride, size = {"core": (1, 2), "x": (2, side), "y": (2 * side, side)}[axis]
    pairs = []
    for i in range(lax.axis_size("dp")):
        at = i // stride % size
        pairs.append((i, i + stride * ((at + by) % size - at)))
    return lax.ppermute(array, "dp", pairs)


def size_of(axis):
    return lax.axis_size("seq") if axis == "z" else 2 if axis == "core" else sides()


def ring_gather(block, axis, absolute=False):
    pieces = [block]
    for k in range(1, size_of(axis)):
        pieces.append(moved(block, axis, k))
    if absolute:
        whole = jnp.zeros((len(pieces),) + block.shape, block.dtype)
        for k, piece in enumerate(pieces):
            whole = lax.dynamic_update_index_in_dim(whole, piece, depth_of(k), 0)
        return whole
    return jnp.stack(pieces)


def depth_of(k):
    size = lax.axis_size("seq")
    return lax.rem(lax.axis_index("seq") + size - k, size)


def added(left, right):
    return (left.astype(F32) + right.astype(F32)).astype(BF16)


def ring_scatter(parts, axis, absolute=False):
    size = size_of(axis)
    if absolute:
        parts = [lax.dynamic_index_in_dim(parts, depth_of(k), 0, False) for k in range(size)]
    total = parts[0].astype(F32)
    for k in range(1, size):
        total = total + moved(parts[k], axis, -k).astype(F32)
    return total.astype(BF16)


def cut_of(columns):
    return (columns // LANE + 1) // 2 * LANE


def after(value, *others):
    mark = sum(other[(0,) * other.ndim].astype(F32) for other in others)
    return jnp.where(mark != mark, jnp.zeros_like(value), value)


def wide_gather(pieces):
    cut = cut_of(pieces.shape[-1])
    left = ring_gather(pieces[..., :cut], "x")
    right = ring_gather(pieces[..., cut:], "y")
    return left, right


def last_gather(left, right):
    return ring_gather(left, "y"), ring_gather(right, "x")


def first_scatter(left, right):
    return ring_scatter(left, "y"), ring_scatter(right, "x")


def second_scatter(left, right):
    return jnp.concatenate([ring_scatter(left, "x"), ring_scatter(right, "y")], -1)


def by_place(pieces, axis):
    size = size_of(axis)
    mine = lax.axis_index("dp") // {"core": 1, "x": 2, "y": 2 * sides()}[axis]
    order = []
    for j in range(size):
        piece = pieces[size - 1]
        for k in range(size - 1):
            piece = jnp.where(lax.rem(lax.rem(mine, size) - j + size, size) == k, pieces[k], piece)
        order.append(piece)
    return order


def unit_blocks(whole, inverse=False):
    side = sides()
    dp = lax.axis_index("dp")
    at_x, at_core = lax.rem(dp // 2, side), lax.rem(dp, 2)
    parts = whole.reshape((side // 2, side, 2, -1) + whole.shape[1:])
    if inverse:
        parts = whole.reshape((2, side // 2, side, -1) + whole.shape[1:]).transpose(1, 2, 0, 3, 4)
    rows = []
    for k in range(side):
        piece = lax.dynamic_index_in_dim(parts, lax.rem(at_x - k + side, side), 1, False)
        pair = [piece[:, 0], piece[:, 1]]
        rows.append([jnp.where(at_core == 0, pair[c], pair[1 - c]) for c in range(2)])
    if inverse:
        return jnp.stack([jnp.stack(r, 1) for r in rows], 1).reshape(whole.shape)
    return [jnp.stack([r[c] for r in rows], 1).reshape((-1,) + whole.shape[1:]) for c in range(2)]


def unit_pairs():
    side, depth = sides(), lax.axis_size("seq")
    half = max(side // 2, 1)
    pairs = []
    for unit in range(lax.axis_size("dp") * depth):
        k, b = unit // 2, unit % 2
        high, low = divmod(k, side * 2 * depth)
        pairs.append((unit, (high + b * half) * side * 2 * depth + low))
    return pairs


def units_in_order(near, far):
    side, depth = sides(), lax.axis_size("seq")
    cores = []
    for part in by_place([near, far], "core"):
        rows = by_place([part[k] for k in range(side)], "y")
        cores.append(jnp.stack([jnp.stack(by_place([r[k] for k in range(side)], "x")) for r in rows]))
    whole = jnp.stack(cores, 2)
    whole = whole.reshape(side, side, 2, depth, 2, -1, whole.shape[-1])
    whole = jnp.concatenate([whole[..., 0, :, :], whole[..., 1, :, :]], -1)
    return whole.reshape(-1, whole.shape[-1])


def units_from_order(whole):
    side, depth = sides(), lax.axis_size("seq")
    parts = whole.reshape(side, side, 2, depth, -1, 2, LANE)
    parts = jnp.concatenate([parts[..., 0, :], parts[..., 1, :]], 4)
    near, far = by_place([parts[:, :, k] for k in range(2)], "core")
    near = added(near, moved(far, "core"))
    rows = [jnp.stack(by_place([near[j, k] for k in range(side)], "x")) for j in range(side)]
    return jnp.stack(by_place(rows, "y"))


def plane_rows(plane):
    side, depth = sides(), lax.axis_size("seq")
    columns = plane.shape[1]
    parts = plane.reshape(side // 2, side, depth, 2, -1, columns)
    parts = jnp.stack(by_place([parts[:, k] for k in range(side)], "x"))
    return parts.transpose(3, 1, 0, 2, 4, 5).reshape(side * side * depth, -1, columns)


def everywhere(array):
    for axis in ("dp", "seq"):
        size = lax.axis_size(axis)
        bit = 1
        while bit < size:
            array = array + lax.ppermute(array, axis, [(i, i ^ bit) for i in range(size)])
            bit *= 2
    return array


def per_device(
    tokens,
    doc_ids,
    token_expert,
    out_grad,
    norm_gains,
    in_proj,
    conv_weight,
    conv_bias,
    select_proj,
    step_proj,
    step_bias,
    decay_log,
    skip_gain,
    out_proj,
    router,
    expert_up,
    expert_down,
):
    rows = tokens.shape[1]
    slots_per = 5 * rows // (4 * EXPERT_COUNT)
    slots = EXPERT_COUNT * slots_per
    half = DI // 2
    wide = half // 3
    core = lax.rem(lax.axis_index("dp"), 2)
    side, depth = sides(), lax.axis_size("seq")
    both = range(2)

    last_doc = jnp.broadcast_to(doc_ids[0, rows - REACH :, None].astype(BF16), (REACH, LANE))
    prior = passed_along(jnp.concatenate([tokens[0, rows - REACH :], last_doc], 1), "seq", 1)
    prior_tokens = prior[:, :MODEL_WIDTH]
    prior_doc = prior[:, MODEL_WIDTH].astype(jnp.int32)
    lines = lax.all_gather(jnp.concatenate([norm_gains, router.T]), "dp", axis=1, tiled=True)
    gains_all = lines[:2].astype(F32)
    router_all = lines[2:].astype(F32)

    small = jnp.concatenate(
        [
            select_proj,
            step_proj.T,
            decay_log,
            conv_weight.T,
            conv_bias[:, None],
            step_bias[:, None],
            skip_gain[:, None],
        ],
        1,
    )
    columns = small.shape[1]

    small = jnp.pad(small, ((0, 0), (0, 2 * LANE - columns)))
    small = jnp.concatenate([small[:, :LANE], small[:, LANE:]])
    in_z = ring_gather(jnp.concatenate([in_proj.T, small], 1), "z", True)
    in_wide = wide_gather(in_z)
    left, right = last_gather(*in_wide)
    right = right.swapaxes(0, 1)
    rest = MODEL_WIDTH - left.shape[-1]
    in_near = jnp.concatenate([left, right[..., :rest]], -1).reshape(DI, MODEL_WIDTH)
    in_full = (in_near, moved(in_near, "core"))
    small_near = right[..., rest:]
    small_full = unit_blocks(units_in_order(small_near, moved(small_near, "core")))
    out_full = unit_blocks(lax.all_gather(out_proj, BOTH, axis=0, tiled=True))
    experts = jnp.stack([expert_up.swapaxes(1, 2), expert_down], 1)
    experts = after(experts.reshape(-1, MODEL_WIDTH), in_z)
    experts = lax.all_gather(experts, BOTH, axis=0, tiled=True)
    experts = experts.reshape(lax.axis_size("dp") * depth, 4, -1, MODEL_WIDTH)

    at = R + 2 * NS
    select_full = [w[:, :at] for w in small_full]
    step_full = [w[:, at : at + R] for w in small_full]
    line_full = [w[:, at + R : columns].astype(F32).T for w in small_full]
    decay_rate = [-jnp.exp(w[:NS]) for w in line_full]
    conv_taps = [w[NS : NS + KC] for w in line_full]
    bias_conv, bias_step, skip_wide = (
        [w[NS + KC + k][None] for w in line_full] for k in range(3)
    )

    mine = interleave(tokens[0])
    doc_row = interleave(doc_ids[0])
    route = interleave(token_expert[0, :, 0])
    out_cot = interleave(out_grad[0]).astype(F32)

    extended = jnp.concatenate([mine, prior_tokens, jnp.zeros_like(mine[: SEG - REACH])])
    stream_ext = extended.astype(F32)
    inv_ext = lax.rsqrt(jnp.mean(stream_ext * stream_ext, -1, keepdims=True) + EPS)
    hat_ext = stream_ext * inv_ext
    normed_ext = (hat_ext * gains_all[0]).astype(BF16)
    stream, inv_first, hat_first, normed = (
        a[:rows] for a in (stream_ext, inv_ext, hat_ext, normed_ext)
    )
    ext_ids = with_earlier(doc_row, prior_doc)
    same = jnp.stack(
        [(ext_ids[k * SEG : k * SEG + rows] == doc_row).astype(F32) for k in range(REACH)]
    )
    same = jnp.broadcast_to(same[:, :, None], (REACH, rows, LANE))
    kept = same[REACH - 1]

    strip = DI // side
    front, gate, conv_sum, inner = [], [], [], []
    for h in both:
        proj = dot(normed_ext, in_full[h], ((1,), (1,))).astype(BF16)
        parts = by_place([proj[:, k * strip : (k + 1) * strip] for k in range(side)], "y")
        front.append(jnp.concatenate(parts[: side // 2], 1))
        gate.append(jnp.concatenate(parts[side // 2 :], 1)[:rows])
        made = convolved(front[h], same, conv_taps[h], bias_conv[h], wide)
        conv_sum.append(made[0])
        inner.append(made[1])
    select = sum(dot(inner[h], select_full[h], ((1,), (0,))) for h in both)
    steps_low = select[:, :R].astype(BF16)
    in_select = select[:, R : R + NS]
    out_select = select[:, R + NS :]
    step_pre = [dot(steps_low, step_full[h], ((1,), (1,))) + bias_step[h] for h in both]
    delta = [jax.nn.softplus(p) for p in step_pre]
    driven = [d * x.astype(F32) for d, x in zip(delta, inner)]
    rate = [r * math.log2(math.e) for r in decay_rate]

    ends = [
        segment_ends(delta[h], driven[h], kept, in_select, rate[h], False, wide) for h in both
    ]
    pre = [e[:2] for e in ends]
    state_in = entering([e[2] for e in ends], [e[3] for e in ends], False)
    scanned, gated = zip(
        *(
            scan_output(
                delta[h], driven[h], inner[h], gate[h], kept, in_select, out_select, rate[h],
                skip_wide[h], pre[h], state_in[h], wide,
            )
            for h in both
        )
    )
    mixed = sum(dot(gated[h], out_full[h], ((1,), (0,))) for h in both)
    resid = stream + mixed
    inv_second = lax.rsqrt(jnp.mean(resid * resid, -1, keepdims=True) + EPS)
    hat_second = resid * inv_second
    normed_moe = (hat_second * gains_all[1]).astype(BF16)
    normed_wide = normed_moe.astype(F32)
    logits = dot(normed_wide, router_all, ((1,), (1,)), HIGHEST)
    probs = jax.nn.softmax(logits, -1)
    route_hot = route[:, None] == jnp.arange(EXPERT_COUNT, dtype=jnp.int32)[None, :]
    hot_wide = route_hot.astype(F32)
    chosen = jnp.sum(probs * hot_wide, 1, keepdims=True)
    place = jnp.arange(rows, dtype=jnp.int32)
    lower = (place[:, None] >= place[None, :]).astype(BF16)
    rank_in = dot(lower, route_hot.astype(BF16), ((1,), (0,))) - 1.0
    slot = jnp.sum(rank_in * hot_wide, 1).astype(jnp.int32)
    target = jnp.where(route == core, 0, slots_per) + slot
    pick = (jnp.arange(slots, dtype=jnp.int32)[:, None] == target[None, :]).astype(BF16)
    returned_grad = (chosen * out_cot).astype(BF16)
    placed = dot(pick, jnp.concatenate([normed_moe, returned_grad], 1), ((1,), (0,))).astype(BF16)
    placed = jnp.concatenate([placed[:slots_per], moved(placed[slots_per:], "core")])
    buffer, grad_slots = placed[:, :MODEL_WIDTH], placed[:, MODEL_WIDTH:]

    def from_slots(parts):
        parts = jnp.concatenate([parts[:slots_per], moved(parts[slots_per:], "core")])
        return dot(pick.astype(F32), parts, ((0,), (0,)), HIGHEST)

    gated_other = moved(gated[1], "core")
    returned, buffer_grad, expert_grads = expert_pass(core, buffer, grad_slots, experts, depth)
    returned = from_slots(returned)
    buffer_grad = from_slots(buffer_grad)
    branch = chosen * returned
    layer_out = (resid + branch).astype(BF16)
    squared_values = jnp.stack(
        [jnp.sum(resid * resid), jnp.sum(mixed * mixed), jnp.sum(branch * branch)]
    )
    chosen_grad = jnp.sum(out_cot * returned, 1, keepdims=True)
    logit_grad = chosen_grad * chosen * (hot_wide - probs)
    grad_router = dot(logit_grad, normed_wide, ((0,), (0,)), HIGHEST)
    moe_grad = buffer_grad + dot(logit_grad, router_all, ((1,), (0,)), HIGHEST)
    second_gain_grad = jnp.sum(moe_grad * hat_second, 0)
    scaled_second = moe_grad * gains_all[1]
    resid_grad = out_cot + inv_second * (
        scaled_second - hat_second * jnp.mean(scaled_second * hat_second, -1, keepdims=True)
    )
    mixed_grad = resid_grad.astype(BF16)
    crossed = moved(jnp.concatenate([mixed_grad, normed]), "core")
    gated_near = jnp.concatenate([gated[0], gated_other])
    grad_out = dot(gated_near, jnp.concatenate([mixed_grad, crossed[:rows]]), ((0,), (0,)))
    gated_grad = [dot(mixed_grad, out_full[h], ((1,), (1,))) for h in both]
    gates = [g.astype(F32) for g in gate]
    scan_grad = [gated_grad[h] * jax.nn.silu(gates[h]) for h in both]
    gate_grad = [(gated_grad[h] * scanned[h] * silu_slope(gates[h])).astype(BF16) for h in both]
    ends = [
        segment_ends(delta[h], scan_grad[h], kept, out_select, rate[h], True, wide) for h in both
    ]
    post = [e[:2] for e in ends]
    adjoint_in = entering([e[2] for e in ends], [e[3] for e in ends], True)
    groups = [list(range(c, lax.axis_size("dp"), 2)) for c in range(2)]
    out_rows = plane_rows(grad_out.astype(BF16))
    unit = out_rows.shape[1]
    out_rows = jnp.pad(out_rows, ((0, 0), (0, expert_grads.shape[2] - unit), (0, 0)))
    both_sum = lax.dynamic_update_slice(expert_grads, out_rows[:, None], (0, 4, 0, 0))
    both_sum = lax.psum_scatter(
        both_sum, "dp", scatter_dimension=0, tiled=True, axis_index_groups=groups
    )
    both_sum = lax.psum_scatter(both_sum, "seq", scatter_dimension=0, tiled=True)[0]
    out_sum = lax.ppermute(both_sum[4, :unit], BOTH, [(b, a) for a, b in unit_pairs()])
    out_sum = out_sum.astype(F32)
    expert_sum = both_sum[:4].reshape(2, 2, -1, MODEL_WIDTH)
    mine_sum = jnp.where(core == 0, expert_sum[0], expert_sum[1])
    other_sum = moved(jnp.where(core == 0, expert_sum[1], expert_sum[0]), "core")
    expert_sum = jnp.stack(
        [jnp.where(core == e, mine_sum, other_sum) for e in range(EXPERT_COUNT)]
    ).astype(F32)
    made = [
        scan_adjoint(
            delta[h], driven[h], inner[h], scan_grad[h], step_pre[h], kept, in_select, out_select,
            rate[h], skip_wide[h], pre[h], state_in[h], post[h], adjoint_in[h], wide,
        )
        for h in both
    ]
    pre_low, inner_part, rate_sum, step_sum, skip_sum, in_grad, out_grads = map(list, zip(*made))
    steps_grad = sum(dot(pre_low[h], step_full[h], ((1,), (0,))) for h in both)
    select_low = jnp.concatenate(
        [steps_grad, in_grad[0] + in_grad[1], out_grads[0] + out_grads[1]], 1
    ).astype(BF16)
    front_grad, early, tap_sums = zip(
        *(
            convolved_back(
                front[h], same, conv_taps[h], conv_sum[h], inner_part[h], select_low,
                select_full[h], wide,
            )
            for h in both
        )
    )
    grad_small = []
    for h in both:
        lines = [rate_sum[h] * decay_rate[h], tap_sums[h][: KC + 1], step_sum[h], skip_sum[h]]
        grad_small.append(
            jnp.concatenate(
                [
                    dot(inner[h], select_low, ((0,), (0,))),
                    dot(pre_low[h], steps_low, ((0,), (0,))),
                    jnp.concatenate(lines).T,
                    jnp.zeros((half, -columns % LANE), F32),
                ],
                1,
            ).astype(BF16)
        )
    proj_grad = []
    for h in both:
        incoming = passed_along(early[h].reshape(REACH, SEG, half)[:, 0], "seq", -1)
        tail = jnp.pad(incoming[:, None], ((0, 0), (SEG - 1, 0), (0, 0)))
        tail = jnp.pad(tail.reshape(REACH * SEG, half), ((rows - REACH * SEG, 0), (0, 0)))
        whole = jnp.concatenate([(front_grad[h] + tail).astype(BF16), gate_grad[h]], 1)
        parts = [whole[:, k * strip : (k + 1) * strip] for k in range(side)]
        proj_grad.append(jnp.concatenate(by_place(parts, "y"), 1))
    proj_other = moved(proj_grad[1], "core")
    grad_in = dot(
        jnp.concatenate([proj_grad[0], proj_other]),
        jnp.concatenate([normed, crossed[rows:]]),
        ((0,), (0,)),
    ).astype(BF16)
    parts, width = lax.axis_size("dp"), MODEL_WIDTH // lax.axis_size("dp")
    unit = DI // (parts * depth)
    shared = jnp.concatenate([second_gain_grad[None], grad_router]).astype(BF16)
    shared = shared.reshape(3, parts, width).swapaxes(0, 1).reshape(parts, 1, 3 * width)
    extra = -(-3 * width // unit)
    shared = jnp.pad(shared, ((0, 0), (0, 0), (0, extra * unit - 3 * width)))
    shared = jnp.broadcast_to(shared, (parts, depth, extra * unit)).reshape(DI, extra)
    whole = unit_blocks(jnp.concatenate(grad_small), True)
    shared = jnp.pad(shared, ((0, 0), (columns, whole.shape[1] - columns - extra)))
    small_near = units_from_order(whole + shared)
    in_plane = grad_in.reshape(side, side, depth, -1, MODEL_WIDTH)
    cut = cut_of(MODEL_WIDTH + LANE)
    right = jnp.concatenate([in_plane[..., cut:], small_near], -1)
    in_plane = first_scatter(in_plane[..., :cut], right.swapaxes(0, 1))
    in_last = second_scatter(*in_plane)
    in_total = ring_scatter(in_last, "z", True).astype(F32)
    in_sum = in_total[:, :MODEL_WIDTH]
    small_sum = jnp.concatenate(jnp.split(in_total[:, MODEL_WIDTH:], 2), 1)
    line_sum = small_sum[:, at + R : columns]
    shared = small_sum[:, columns : columns + extra].reshape(-1)[: 3 * width].reshape(3, width)
    proj_grad = [after(p, grad_in) for p in proj_grad]
    normed_grad = sum(dot(proj_grad[h], in_full[h], ((1,), (0,))) for h in both)
    first_gain_grad = jnp.sum(normed_grad * hat_first, 0)
    scaled_first = normed_grad * gains_all[0]
    stream_grad = resid_grad + inv_first * (
        scaled_first - hat_first * jnp.mean(scaled_first * hat_first, -1, keepdims=True)
    )

    last = jnp.stack([first_gain_grad, jnp.pad(squared_values, (0, MODEL_WIDTH - 3))])
    last = everywhere(after(last, in_last))
    first_part = lax.dynamic_slice_in_dim(last[:1], lax.axis_index("dp") * width, width, 1)
    stats = jnp.sqrt(last[1, :3] / (rows * parts * depth * MODEL_WIDTH))
    return (
        in_order(layer_out)[None],
        in_order(stream_grad.astype(BF16))[None],
        jnp.concatenate([first_part, shared[:1]]),
        in_sum.T,
        line_sum[:, NS : NS + KC].T,
        line_sum[:, NS + KC],
        small_sum[:, :at],
        small_sum[:, at : at + R].T,
        line_sum[:, NS + KC + 1],
        line_sum[:, :NS],
        line_sum[:, NS + KC + 2],
        out_sum,
        shared[1:].T,
        expert_sum[:, 0].swapaxes(1, 2),
        expert_sum[:, 1],
        stats,
    )


def solution(mesh):
    return jax.shard_map(
        per_device,
        mesh=mesh,
        in_specs=(
            P("dp", "seq", None),
            P("dp", "seq"),
            P("dp", "seq", None),
            P("dp", "seq", None),
            P(None, "dp"),
            P(None, ("dp", "seq")),
            P(None, ("dp", "seq")),
            P(("dp", "seq")),
            P(("dp", "seq"), None),
            P(None, ("dp", "seq")),
            P(("dp", "seq")),
            P(("dp", "seq"), None),
            P(("dp", "seq")),
            P(("dp", "seq"), None),
            P("dp", None),
            P(None, None, ("dp", "seq")),
            P(None, ("dp", "seq"), None),
        ),
        out_specs=(
            P("dp", "seq", None),
            P("dp", "seq", None),
            P(None, "dp"),
            P(None, ("dp", "seq")),
            P(None, ("dp", "seq")),
            P(("dp", "seq")),
            P(("dp", "seq"), None),
            P(None, ("dp", "seq")),
            P(("dp", "seq")),
            P(("dp", "seq"), None),
            P(("dp", "seq")),
            P(("dp", "seq"), None),
            P("dp", None),
            P(None, None, ("dp", "seq")),
            P(None, ("dp", "seq"), None),
            P(),
        ),
        check_vma=False,
    )
```

```python
import functools, math
import jax
import jax.numpy as jnp
from jax import lax
from jax.experimental import pallas as pl
from jax.experimental.pallas import tpu as pltpu
from jax.sharding import PartitionSpec as P

NS = 16
SEG = 8
LANE = 128
FAR = 1e30


def spread_columns(wide, columns):
    for n in range(NS):
        wide[n] = jnp.broadcast_to(columns[:, n : n + 1], wide.shape[1:])


def rows_of(i):
    return pl.ds(pl.multiple_of(i * SEG, SEG), SEG)


def rate_rows(rate):
    return [jnp.broadcast_to(rate[n : n + 1, :], (SEG, rate.shape[1])) for n in range(NS)]


def tiled_lanes(block, width):
    return block if width == LANE else jnp.concatenate([block] * (width // LANE), 1)


def prefix_pairs(decay, value, reverse):
    place = lax.broadcasted_iota(jnp.int32, decay.shape, 0)

    def shifted(array, by, fill):
        if reverse:
            return jnp.where(place < SEG - by, pltpu.roll(array, SEG - by, 0), fill)
        return jnp.where(place >= by, pltpu.roll(array, by, 0), fill)

    for by in (1, 2, 4):
        value = decay * shifted(value, by, 0.0) + value
        decay = decay * shifted(decay, by, 1.0)
    last = slice(0, 1) if reverse else slice(SEG - 1, SEG)
    return shifted(decay, 1, 1.0), shifted(value, 1, 0.0), decay[last], value[last]


def ends_kernel(
    reverse, delta, driven, kept, select, rate, pre_decay, pre_value, all_decay, all_value, wide
):
    @pl.when(pl.program_id(0) == 0)
    def _():
        spread_columns(wide, select)

    width = delta.shape[1]
    length = delta.shape[0] // SEG
    rates = rate_rows(rate)
    zero = jnp.zeros((SEG, width), jnp.float32)

    def step(k, carry):
        total, states = carry
        i = length - 1 - k if reverse else k
        rows = rows_of(i)
        reach = jnp.where(tiled_lanes(kept[rows, :], width) > 0, delta[rows, :], FAR)
        drive = driven[rows, :]
        new = []
        for n in range(NS):
            factor = jnp.exp2(reach * rates[n])
            term = drive * tiled_lanes(wide[n, rows, :], width)
            new.append(factor * (states[n] + term) if reverse else factor * states[n] + term)
        return total + reach, tuple(new)

    total, states = lax.fori_loop(0, length, step, (zero, (zero,) * NS))
    for n in range(NS):
        before_decay, before_value, whole_decay, whole_value = prefix_pairs(
            jnp.exp2(total * rates[n]), states[n], reverse
        )
        pre_decay[n] = before_decay
        pre_value[n] = before_value
        all_decay[n : n + 1, :] = whole_decay
        all_value[n : n + 1, :] = whole_value


def output_kernel(
    delta, driven, inner, gate, kept, in_select, out_select, rate, skip, pre_decay, pre_value,
    entry, scanned, gated, wide_in, wide_out,
):
    @pl.when(pl.program_id(0) == 0)
    def _():
        spread_columns(wide_in, in_select)
        spread_columns(wide_out, out_select)

    width = delta.shape[1]
    length = delta.shape[0] // SEG
    rates = rate_rows(rate)
    start = tuple(pre_decay[n] * entry[n : n + 1, :] + pre_value[n] for n in range(NS))

    def step(i, states):
        rows = rows_of(i)
        reach = jnp.where(tiled_lanes(kept[rows, :], width) > 0, delta[rows, :], FAR)
        drive = driven[rows, :]
        new, parts = [], [0.0] * 4
        for n in range(NS):
            state = jnp.exp2(reach * rates[n]) * states[n] + drive * tiled_lanes(
                wide_in[n, rows, :], width
            )
            parts[n % 4] = parts[n % 4] + state * tiled_lanes(wide_out[n, rows, :], width)
            new.append(state)
        scanned[rows, :] = (parts[0] + parts[1]) + (parts[2] + parts[3])
        return tuple(new)

    lax.fori_loop(0, length, step, start)
    value = scanned[...] + skip[...] * inner[...].astype(jnp.float32)
    scanned[...] = value
    half = gate[...].astype(jnp.float32)
    gated[...] = (value * (half * jax.nn.sigmoid(half))).astype(jnp.bfloat16)


def adjoint_kernel(
    delta, driven, inner, grad, step_pre, kept, in_select, out_select, rate, skip, pre_decay,
    pre_value, entry, post_decay, post_value, exit_, pre_low, inner_part, rate_sum, step_sum,
    skip_sum, in_grad, out_grad, states, wide_in, wide_out, in_total, out_total, inner_grad,
    delta_grad,
):
    j = pl.program_id(0)

    @pl.when(j == 0)
    def _():
        spread_columns(wide_in, in_select)
        spread_columns(wide_out, out_select)
        in_total[...] = jnp.zeros_like(in_total)
        out_total[...] = jnp.zeros_like(out_total)

    width = delta.shape[1]
    length = delta.shape[0] // SEG
    rates = rate_rows(rate)
    start = tuple(pre_decay[n] * entry[n : n + 1, :] + pre_value[n] for n in range(NS))

    def folded(value):
        return sum(value[:, k : k + LANE] for k in range(0, width, LANE))

    def advance(i, carry):
        rows = rows_of(i)
        reach = jnp.where(tiled_lanes(kept[rows, :], width) > 0, delta[rows, :], FAR)
        drive, grad_t = driven[rows, :], grad[rows, :]
        new = []
        for n in range(NS):
            states[i, n] = carry[n]
            state = jnp.exp2(reach * rates[n]) * carry[n] + drive * tiled_lanes(
                wide_in[n, rows, :], width
            )
            out_total[n, rows, :] = out_total[n, rows, :] + folded(grad_t * state)
            new.append(state)
        return tuple(new)

    lax.fori_loop(0, length, advance, start)
    back = tuple(post_decay[n] * exit_[n : n + 1, :] + post_value[n] for n in range(NS))
    zero = jnp.zeros((SEG, width), jnp.float32)

    def retreat(k, carry):
        backs, sums = carry
        i = length - 1 - k
        rows = rows_of(i)
        step_t = delta[rows, :]
        reach = jnp.where(tiled_lanes(kept[rows, :], width) > 0, step_t, FAR)
        drive, grad_t = driven[rows, :], grad[rows, :]
        new_backs, new_sums = [], []
        weighted, slope = [0.0] * 2, [0.0] * 2
        for n in range(NS):
            adjoint = grad_t * tiled_lanes(wide_out[n, rows, :], width) + backs[n]
            passed = jnp.exp2(reach * rates[n]) * adjoint
            through = passed * states[i, n]
            weighted[n % 2] = weighted[n % 2] + adjoint * tiled_lanes(wide_in[n, rows, :], width)
            slope[n % 2] = slope[n % 2] + through * rates[n]
            in_total[n, rows, :] = in_total[n, rows, :] + folded(adjoint * drive)
            new_backs.append(passed)
            new_sums.append(sums[n] + through * step_t)
        inner_grad[rows, :] = weighted[0] + weighted[1]
        delta_grad[rows, :] = slope[0] + slope[1]
        return tuple(new_backs), tuple(new_sums)

    _, sums = lax.fori_loop(0, length, retreat, (back, (zero,) * NS))
    for n in range(NS):
        rate_sum[n : n + 1, :] = jnp.sum(sums[n], 0, keepdims=True)
    weighted, value, grads = inner_grad[...], inner[...].astype(jnp.float32), grad[...]
    slope = weighted * value + delta_grad[...] * math.log(2.0)
    pre = slope * jax.nn.sigmoid(step_pre[...])
    pre_low[...] = pre.astype(jnp.bfloat16)
    step_sum[...] = jnp.sum(pre, 0, keepdims=True)
    skip_sum[...] = jnp.sum(grads * value, 0, keepdims=True)
    inner_part[...] = grads * skip[...] + weighted * delta[...]

    @pl.when(j == pl.num_programs(0) - 1)
    def _():
        place = lax.broadcasted_iota(jnp.int32, in_grad.shape, 1)
        for total, result in ((in_total, in_grad), (out_total, out_grad)):
            value = jnp.zeros(result.shape, jnp.float32)
            for n in range(NS):
                column = jnp.sum(total[n], 1, keepdims=True)
                value = jnp.where(place == n, column, value)
            result[...] = value


def earlier_rows(ext, front, rows):
    own = front[0:rows, :].astype(jnp.float32)
    halo = front[rows : rows + SEG, :].astype(jnp.float32)
    place = lax.broadcasted_iota(jnp.int32, (SEG, own.shape[1]), 0)
    for b in range(3):
        at = rows - (3 - b) * SEG
        group = pltpu.roll(own[at : at + SEG], 1, 0)
        ext[b * SEG : (b + 1) * SEG, :] = jnp.where(place == 0, halo[b : b + 1], group)
    ext[3 * SEG :, :] = own


def masked_tap(ext, same, k, rows, width):
    tap = ext[k * SEG : k * SEG + rows, :]
    return tap if k == 3 else tap * tiled_lanes(same[k], width)


def conv_kernel(front, same, taps, bias, conv_sum, inner, ext):
    rows, width = conv_sum.shape
    earlier_rows(ext, front, rows)
    total = jnp.broadcast_to(bias[...], (rows, width))
    for k in range(4):
        total = total + taps[k : k + 1, :] * masked_tap(ext, same, k, rows, width)
    conv_sum[...] = total
    inner[...] = (total * jax.nn.sigmoid(total)).astype(jnp.bfloat16)


def conv_back_kernel(
    front, same, taps, conv_sum, inner_part, select_low, select, front_grad, early, sums, ext
):
    rows, width = conv_sum.shape
    total = conv_sum[...]
    logistic = jax.nn.sigmoid(total)
    back = lax.dot_general(
        select_low[...], select[...], (((1,), (1,)), ((), ())), preferred_element_type=jnp.float32
    )
    back = (inner_part[...] + back) * (logistic * (1.0 + total * (1.0 - logistic)))
    earlier_rows(ext, front, rows)
    for k in range(4):
        sums[k : k + 1, :] = jnp.sum(back * masked_tap(ext, same, k, rows, width), 0, keepdims=True)
    sums[4:5, :] = jnp.sum(back, 0, keepdims=True)
    sums[5:8, :] = jnp.zeros((3, width), jnp.float32)
    ext[0 : 3 * SEG, :] = jnp.zeros((3 * SEG, width), jnp.float32)
    ext[3 * SEG :, :] = back * taps[3:4, :]
    for k in range(3):
        part = back * taps[k : k + 1, :] * tiled_lanes(same[k], width)
        ext[k * SEG : k * SEG + rows, :] = ext[k * SEG : k * SEG + rows, :] + part
    place = lax.broadcasted_iota(jnp.int32, (SEG, width), 0)
    early[...] = ext[0 : 3 * SEG, :]
    for b in range(3):
        at = rows + b * SEG
        later = pltpu.roll(ext[b * SEG : (b + 1) * SEG, :], SEG - 1, 0)
        ext[at : at + SEG, :] = ext[at : at + SEG, :] + jnp.where(place < SEG - 1, later, 0.0)
    front_grad[...] = ext[3 * SEG :, :]


def expert_kernel(at, buffer, grads, up, down, returned, buffer_grad, weight_grads):
    def product(left, right, contract):
        return lax.dot_general(
            left, right, (contract, ((), ())), preferred_element_type=jnp.float32
        )

    @pl.when(pl.program_id(0) == 0)
    def _():
        returned[...] = jnp.zeros_like(returned)
        buffer_grad[...] = jnp.zeros_like(buffer_grad)

    values, cot = buffer[...], grads[...]
    ups, downs = (w[...].reshape(-1, values.shape[1]) for w in (up, down))
    hidden = product(values, ups, ((1,), (1,)))
    below = 0.5 * (1.0 + lax.erf(hidden * math.sqrt(0.5)))
    density = jnp.exp(-0.5 * hidden * hidden) * (1.0 / math.sqrt(2.0 * math.pi))
    active = (hidden * below).astype(jnp.bfloat16)
    active_grad = product(cot, downs, ((1,), (1,)))
    hidden_grad = (active_grad * (below + hidden * density)).astype(jnp.bfloat16)
    returned[...] += product(active, downs, ((1,), (0,)))
    buffer_grad[...] += product(hidden_grad, ups, ((1,), (0,)))
    pieces = weight_grads.shape[0], weight_grads.shape[2], weight_grads.shape[3]
    for k, (left, right) in enumerate(((hidden_grad, values), (active, cot))):
        weight_grads[:, k] = product(left, right, ((0,), (0,))).astype(jnp.bfloat16).reshape(pieces)


def column_specs(rows, width):
    return (
        pl.BlockSpec((rows, width), lambda j: (0, j)),
        pl.BlockSpec((rows, LANE), lambda j: (0, 0)),
        pl.BlockSpec((rows, NS), lambda j: (0, 0)),
        pl.BlockSpec((NS, width), lambda j: (0, j)),
        pl.BlockSpec((NS, SEG, width), lambda j: (0, 0, j)),
        pl.BlockSpec((1, width), lambda j: (0, j)),
    )


def params(mib):
    return pltpu.CompilerParams(
        dimension_semantics=("arbitrary",), vmem_limit_bytes=mib * 2**20
    )


def cost(rows, channels, passes):
    return pl.CostEstimate(
        flops=0, bytes_accessed=int(rows * channels * passes) // 4, transcendentals=0
    )


def segment_ends(delta, driven, kept, select, rate, reverse, width=LANE):
    rows, channels = delta.shape
    block, flag, columns, state, segments, _ = column_specs(rows, width)
    return pl.pallas_call(
        functools.partial(ends_kernel, reverse),
        grid=(channels // width,),
        in_specs=[block, block, flag, columns, state],
        out_specs=[segments, segments, state, state],
        out_shape=[jax.ShapeDtypeStruct((NS, SEG, channels), jnp.float32)] * 2
        + [jax.ShapeDtypeStruct((NS, channels), jnp.float32)] * 2,
        scratch_shapes=[pltpu.VMEM((NS, rows, LANE), jnp.float32)],
        compiler_params=params(24),
        cost_estimate=cost(rows, channels, 75),
    )(delta, driven, kept, select, rate)


def scan_output(
    delta, driven, inner, gate, kept, in_select, out_select, rate, skip, pre, entry, width=LANE
):
    rows, channels = delta.shape
    block, flag, columns, state, segments, line = column_specs(rows, width)
    wide = pltpu.VMEM((NS, rows, LANE), jnp.float32)
    return pl.pallas_call(
        output_kernel,
        grid=(channels // width,),
        in_specs=[block] * 4 + [flag, columns, columns, state, line, segments, segments, state],
        out_specs=[block, block],
        out_shape=[
            jax.ShapeDtypeStruct((rows, channels), jnp.float32),
            jax.ShapeDtypeStruct((rows, channels), jnp.bfloat16),
        ],
        scratch_shapes=[wide, wide],
        compiler_params=params(24),
        cost_estimate=cost(rows, channels, 95),
    )(delta, driven, inner, gate, kept, in_select, out_select, rate, skip, *pre, entry)


def scan_adjoint(
    delta, driven, inner, grad, step_pre, kept, in_select, out_select, rate, skip, pre, entry,
    post, exit_, width=LANE,
):
    rows, channels = delta.shape
    block, flag, columns, state, segments, line = column_specs(rows, width)
    wide = pltpu.VMEM((NS, rows, LANE), jnp.float32)
    whole = pltpu.VMEM((rows, width), jnp.float32)
    return pl.pallas_call(
        adjoint_kernel,
        grid=(channels // width,),
        in_specs=[block] * 5
        + [flag, columns, columns, state, line]
        + [segments, segments, state, segments, segments, state],
        out_specs=[block, block, state, line, line, columns, columns],
        out_shape=[
            jax.ShapeDtypeStruct((rows, channels), jnp.bfloat16),
            jax.ShapeDtypeStruct((rows, channels), jnp.float32),
            jax.ShapeDtypeStruct((NS, channels), jnp.float32),
        ]
        + [jax.ShapeDtypeStruct((1, channels), jnp.float32)] * 2
        + [jax.ShapeDtypeStruct((rows, NS), jnp.float32)] * 2,
        scratch_shapes=[
            pltpu.VMEM((rows // SEG, NS, SEG, width), jnp.float32),
            wide, wide, wide, wide, whole, whole,
        ],
        compiler_params=params(40),
        cost_estimate=cost(rows, channels, 280),
    )(
        delta, driven, inner, grad, step_pre, kept, in_select, out_select, rate, skip, *pre, entry,
        *post, exit_,
    )


def conv_specs(rows, width):
    return (
        pl.BlockSpec((rows + SEG, width), lambda j: (0, j)),
        pl.BlockSpec((3, rows, LANE), lambda j: (0, 0, 0)),
        pl.BlockSpec((4, width), lambda j: (0, j)),
        pl.BlockSpec((rows, width), lambda j: (0, j)),
    )


def convolved(front, same, taps, bias, width):
    rows, channels = front.shape[0] - SEG, front.shape[1]
    ahead, flags, weights, block = conv_specs(rows, width)
    return pl.pallas_call(
        conv_kernel,
        grid=(channels // width,),
        in_specs=[ahead, flags, weights, pl.BlockSpec((1, width), lambda j: (0, j))],
        out_specs=[block, block],
        out_shape=[
            jax.ShapeDtypeStruct((rows, channels), jnp.float32),
            jax.ShapeDtypeStruct((rows, channels), jnp.bfloat16),
        ],
        scratch_shapes=[pltpu.VMEM((rows + 3 * SEG, width), jnp.float32)],
        compiler_params=params(24),
        cost_estimate=cost(rows, channels, 25),
    )(front, same, taps, bias)


def convolved_back(front, same, taps, conv_sum, inner_part, select_low, select, width):
    rows, channels = conv_sum.shape
    ahead, flags, weights, block = conv_specs(rows, width)
    inputs = select.shape[1]
    return pl.pallas_call(
        conv_back_kernel,
        grid=(channels // width,),
        in_specs=[
            ahead,
            flags,
            weights,
            block,
            block,
            pl.BlockSpec((rows, inputs), lambda j: (0, 0)),
            pl.BlockSpec((width, inputs), lambda j: (j, 0)),
        ],
        out_specs=[
            block,
            pl.BlockSpec((3 * SEG, width), lambda j: (0, j)),
            pl.BlockSpec((SEG, width), lambda j: (0, j)),
        ],
        out_shape=[
            jax.ShapeDtypeStruct((rows, channels), jnp.float32),
            jax.ShapeDtypeStruct((3 * SEG, channels), jnp.float32),
            jax.ShapeDtypeStruct((SEG, channels), jnp.float32),
        ],
        scratch_shapes=[pltpu.VMEM((rows + 3 * SEG, width), jnp.float32)],
        compiler_params=params(24),
        cost_estimate=cost(rows, channels, 40),
    )(front, same, taps, conv_sum, inner_part, select_low, select)


def expert_pass(core, buffer, grads, weights, depth):
    slots, width = buffer.shape
    devices, _, part, _ = weights.shape
    direct = part % 16 == 0
    if direct:
        tile, strip = depth, part
    else:
        tile, strip = 1, depth * part
        weights = weights.swapaxes(0, 1).reshape(1, 4, devices * part, width)
    steps = devices // depth
    whole = pl.BlockSpec((slots, width), lambda j, at: (0, 0))

    def weight(k):
        def place(j, at):
            return (j, 2 * at[0] + k, 0, 0) if direct else (0, 2 * at[0] + k, j, 0)

        return pl.BlockSpec((tile, 1, strip, width), place)

    returned, buffer_grad, weight_grads = pl.pallas_call(
        expert_kernel,
        grid_spec=pltpu.PrefetchScalarGridSpec(
            num_scalar_prefetch=1,
            grid=(steps,),
            in_specs=[whole, whole, weight(0), weight(1)],
            out_specs=[
                whole,
                whole,
                pl.BlockSpec(
                    (tile, 2, strip, width), lambda j, at: (lax.div(j, 2), lax.rem(j, 2), 0, 0)
                ),
            ],
        ),
        out_shape=[jax.ShapeDtypeStruct((slots, width), jnp.float32)] * 2
        + [jax.ShapeDtypeStruct((steps // 2 * tile, 5, strip, width), jnp.bfloat16)],
        compiler_params=params(52),
        cost_estimate=pl.CostEstimate(
            flops=12 * slots * width * devices * part,
            bytes_accessed=8 * devices * part * width,
            transcendentals=0,
        ),
    )(core.reshape(1).astype(jnp.int32), buffer, grads, weights, weights)
    if not direct:
        parts = weight_grads.reshape(steps // 2, 5, depth, part, width)
        weight_grads = parts.swapaxes(1, 2).reshape(-1, 5, part, width)
    return returned, buffer_grad, weight_grads


MODEL_WIDTH = 1152
DI = 2304
R = 72
KC = 4
EXPERT_COUNT = 2
EPS = 1e-05
REACH = KC - 1
BOTH = ("dp", "seq")
HIGHEST = lax.Precision.HIGHEST
F32 = jnp.float32
BF16 = jnp.bfloat16


def passed_along(array, axis, by):
    size = lax.axis_size(axis)
    pairs = [(i, i + by) for i in range(size) if 0 <= i + by < size]
    return lax.ppermute(array, axis, pairs)


def interleave(array):
    split = array.reshape((SEG, array.shape[0] // SEG) + array.shape[1:])
    return split.swapaxes(0, 1).reshape(array.shape)


def in_order(array):
    split = array.reshape((array.shape[0] // SEG, SEG) + array.shape[1:])
    return split.swapaxes(0, 1).reshape(array.shape)


def with_earlier(array, earlier):
    last = array[array.shape[0] - REACH * SEG :].reshape((REACH, SEG) + array.shape[1:])
    front = jnp.concatenate([earlier[:, None], last[:, : SEG - 1]], 1)
    return jnp.concatenate([front.reshape((REACH * SEG,) + array.shape[1:]), array])


def entering(decays, values, reverse):
    size, mine = lax.axis_size("seq"), lax.axis_index("seq")
    pairs = jnp.stack([jnp.concatenate(decays, 1), jnp.concatenate(values, 1)]).astype(BF16)
    gathered = lax.all_gather(pairs, "seq")
    state = jnp.zeros(pairs.shape[1:], F32)
    for k in range(size):
        at = size - 1 - k if reverse else k
        reached = at > mine if reverse else at < mine
        part = gathered[at].astype(F32)
        state = jnp.where(reached, part[0] * state + part[1], state)
    return jnp.split(state, 2, 1)


def silu_slope(value):
    logistic = jax.nn.sigmoid(value)
    return logistic * (1.0 + value * (1.0 - logistic))


def gelu_slope(value):
    return 0.5 * (1.0 + lax.erf(value / math.sqrt(2.0))) + value * jnp.exp(
        -0.5 * value * value
    ) / math.sqrt(2.0 * math.pi)


def dot(left, right, contract, precision=None):
    return lax.dot_general(
        left, right, (contract, ((), ())), precision=precision, preferred_element_type=F32
    )


def sides():
    return math.isqrt(lax.axis_size("dp") // 2)


def moved(array, axis, by=1):
    if axis == "z":
        size = lax.axis_size("seq")
        return lax.ppermute(array, "seq", [(i, (i + by) % size) for i in range(size)])
    side = sides()
    stride, size = {"core": (1, 2), "x": (2, side), "y": (2 * side, side)}[axis]
    pairs = []
    for i in range(lax.axis_size("dp")):
        at = i // stride % size
        pairs.append((i, i + stride * ((at + by) % size - at)))
    return lax.ppermute(array, "dp", pairs)


def size_of(axis):
    return lax.axis_size("seq") if axis == "z" else 2 if axis == "core" else sides()


def ring_gather(block, axis, absolute=False):
    pieces = [block]
    for k in range(1, size_of(axis)):
        pieces.append(moved(block, axis, k))
    if absolute:
        whole = jnp.zeros((len(pieces),) + block.shape, block.dtype)
        for k, piece in enumerate(pieces):
            whole = lax.dynamic_update_index_in_dim(whole, piece, depth_of(k), 0)
        return whole
    return jnp.stack(pieces)


def depth_of(k):
    size = lax.axis_size("seq")
    return lax.rem(lax.axis_index("seq") + size - k, size)


def added(left, right):
    return (left.astype(F32) + right.astype(F32)).astype(BF16)


def ring_scatter(parts, axis, absolute=False):
    size = size_of(axis)
    if absolute:
        parts = [lax.dynamic_index_in_dim(parts, depth_of(k), 0, False) for k in range(size)]
    total = parts[0].astype(F32)
    for k in range(1, size):
        total = total + moved(parts[k], axis, -k).astype(F32)
    return total.astype(BF16)


def cut_of(columns):
    return (columns // LANE + 1) // 2 * LANE


def after(value, *others):
    mark = sum(other[(0,) * other.ndim].astype(F32) for other in others)
    return jnp.where(mark != mark, jnp.zeros_like(value), value)


def wide_gather(pieces):
    cut = cut_of(pieces.shape[-1])
    left = ring_gather(pieces[..., :cut], "x")
    right = ring_gather(pieces[..., cut:], "y")
    return left, right


def last_gather(left, right):
    return ring_gather(left, "y"), ring_gather(right, "x")


def first_scatter(left, right):
    return ring_scatter(left, "y"), ring_scatter(right, "x")


def second_scatter(left, right):
    return jnp.concatenate([ring_scatter(left, "x"), ring_scatter(right, "y")], -1)


def by_place(pieces, axis):
    size = size_of(axis)
    mine = lax.axis_index("dp") // {"core": 1, "x": 2, "y": 2 * sides()}[axis]
    order = []
    for j in range(size):
        piece = pieces[size - 1]
        for k in range(size - 1):
            piece = jnp.where(lax.rem(lax.rem(mine, size) - j + size, size) == k, pieces[k], piece)
        order.append(piece)
    return order


def unit_blocks(whole, inverse=False):
    side = sides()
    dp = lax.axis_index("dp")
    at_x, at_core = lax.rem(dp // 2, side), lax.rem(dp, 2)
    parts = whole.reshape((side // 2, side, 2, -1) + whole.shape[1:])
    if inverse:
        parts = whole.reshape((2, side // 2, side, -1) + whole.shape[1:]).transpose(1, 2, 0, 3, 4)
    rows = []
    for k in range(side):
        piece = lax.dynamic_index_in_dim(parts, lax.rem(at_x - k + side, side), 1, False)
        pair = [piece[:, 0], piece[:, 1]]
        rows.append([jnp.where(at_core == 0, pair[c], pair[1 - c]) for c in range(2)])
    if inverse:
        return jnp.stack([jnp.stack(r, 1) for r in rows], 1).reshape(whole.shape)
    return [jnp.stack([r[c] for r in rows], 1).reshape((-1,) + whole.shape[1:]) for c in range(2)]


def unit_pairs():
    side, depth = sides(), lax.axis_size("seq")
    half = max(side // 2, 1)
    pairs = []
    for unit in range(lax.axis_size("dp") * depth):
        k, b = unit // 2, unit % 2
        high, low = divmod(k, side * 2 * depth)
        pairs.append((unit, (high + b * half) * side * 2 * depth + low))
    return pairs


def units_in_order(near, far):
    side, depth = sides(), lax.axis_size("seq")
    cores = []
    for part in by_place([near, far], "core"):
        rows = by_place([part[k] for k in range(side)], "y")
        cores.append(jnp.stack([jnp.stack(by_place([r[k] for k in range(side)], "x")) for r in rows]))
    whole = jnp.stack(cores, 2)
    whole = whole.reshape(side, side, 2, depth, 2, -1, whole.shape[-1])
    whole = jnp.concatenate([whole[..., 0, :, :], whole[..., 1, :, :]], -1)
    return whole.reshape(-1, whole.shape[-1])


def units_from_order(whole):
    side, depth = sides(), lax.axis_size("seq")
    parts = whole.reshape(side, side, 2, depth, -1, 2, LANE)
    parts = jnp.concatenate([parts[..., 0, :], parts[..., 1, :]], 4)
    near, far = by_place([parts[:, :, k] for k in range(2)], "core")
    near = added(near, moved(far, "core"))
    rows = [jnp.stack(by_place([near[j, k] for k in range(side)], "x")) for j in range(side)]
    return jnp.stack(by_place(rows, "y"))


def plane_rows(plane):
    side, depth = sides(), lax.axis_size("seq")
    columns = plane.shape[1]
    parts = plane.reshape(side // 2, side, depth, 2, -1, columns)
    parts = jnp.stack(by_place([parts[:, k] for k in range(side)], "x"))
    return parts.transpose(3, 1, 0, 2, 4, 5).reshape(side * side * depth, -1, columns)


def everywhere(array):
    for axis in ("seq", "dp"):
        size = lax.axis_size(axis)
        bit = 1
        while bit < size:
            array = array + lax.ppermute(array, axis, [(i, i ^ bit) for i in range(size)])
            bit *= 2
    return array


def per_device(
    tokens,
    doc_ids,
    token_expert,
    out_grad,
    norm_gains,
    in_proj,
    conv_weight,
    conv_bias,
    select_proj,
    step_proj,
    step_bias,
    decay_log,
    skip_gain,
    out_proj,
    router,
    expert_up,
    expert_down,
):
    rows = tokens.shape[1]
    slots_per = 5 * rows // (4 * EXPERT_COUNT)
    slots = EXPERT_COUNT * slots_per
    half = DI // 2
    wide = half // 3
    core = lax.rem(lax.axis_index("dp"), 2)
    side, depth = sides(), lax.axis_size("seq")
    both = range(2)

    last_doc = jnp.broadcast_to(doc_ids[0, rows - REACH :, None].astype(BF16), (REACH, LANE))
    prior = passed_along(jnp.concatenate([tokens[0, rows - REACH :], last_doc], 1), "seq", 1)
    prior_tokens = prior[:, :MODEL_WIDTH]
    prior_doc = prior[:, MODEL_WIDTH].astype(jnp.int32)
    lines = lax.all_gather(jnp.concatenate([norm_gains, router.T]), "dp", axis=1, tiled=True)
    gains_all = lines[:2].astype(F32)
    router_all = lines[2:].astype(F32)

    small = jnp.concatenate(
        [
            select_proj,
            step_proj.T,
            decay_log,
            conv_weight.T,
            conv_bias[:, None],
            step_bias[:, None],
            skip_gain[:, None],
        ],
        1,
    )
    columns = small.shape[1]

    small = jnp.pad(small, ((0, 0), (0, 2 * LANE - columns)))
    small = jnp.concatenate([small[:, :LANE], small[:, LANE:]])
    in_z = ring_gather(jnp.concatenate([in_proj.T, small], 1), "z", True)
    in_wide = wide_gather(in_z)
    left, right = last_gather(*in_wide)
    right = right.swapaxes(0, 1)
    rest = MODEL_WIDTH - left.shape[-1]
    in_near = jnp.concatenate([left, right[..., :rest]], -1).reshape(DI, MODEL_WIDTH)
    in_full = (in_near, moved(in_near, "core"))
    small_near = right[..., rest:]
    small_full = unit_blocks(units_in_order(small_near, moved(small_near, "core")))
    out_full = unit_blocks(lax.all_gather(out_proj, BOTH, axis=0, tiled=True))
    experts = jnp.stack([expert_up.swapaxes(1, 2), expert_down], 1)
    experts = after(experts.reshape(-1, MODEL_WIDTH), in_z)
    experts = lax.all_gather(experts, BOTH, axis=0, tiled=True)
    experts = experts.reshape(lax.axis_size("dp") * depth, 4, -1, MODEL_WIDTH)

    at = R + 2 * NS
    select_full = [w[:, :at] for w in small_full]
    step_full = [w[:, at : at + R] for w in small_full]
    unit_lines = jnp.eye(columns - at - R, dtype=BF16)
    line_full = [dot(unit_lines, w[:, at + R : columns], ((1,), (1,))) for w in small_full]
    decay_rate = [-jnp.exp(w[:NS]) for w in line_full]
    conv_taps = [w[NS : NS + KC] for w in line_full]
    bias_conv, bias_step, skip_wide = (
        [w[NS + KC + k][None] for w in line_full] for k in range(3)
    )

    mine = interleave(tokens[0])
    doc_row = interleave(doc_ids[0])
    route = interleave(token_expert[0, :, 0])
    out_cot = interleave(out_grad[0]).astype(F32)

    extended = jnp.concatenate([mine, prior_tokens, jnp.zeros_like(mine[: SEG - REACH])])
    stream_ext = extended.astype(F32)
    inv_ext = lax.rsqrt(jnp.mean(stream_ext * stream_ext, -1, keepdims=True) + EPS)
    hat_ext = stream_ext * inv_ext
    normed_ext = (hat_ext * gains_all[0]).astype(BF16)
    stream, inv_first, hat_first, normed = (
        a[:rows] for a in (stream_ext, inv_ext, hat_ext, normed_ext)
    )
    ext_ids = with_earlier(doc_row, prior_doc)
    same = jnp.stack(
        [(ext_ids[k * SEG : k * SEG + rows] == doc_row).astype(F32) for k in range(REACH)]
    )
    same = jnp.broadcast_to(same[:, :, None], (REACH, rows, LANE))
    kept = same[REACH - 1]

    strip = DI // side
    front, gate, conv_sum, inner = [], [], [], []
    for h in both:
        proj = dot(normed_ext, in_full[h], ((1,), (1,))).astype(BF16)
        parts = by_place([proj[:, k * strip : (k + 1) * strip] for k in range(side)], "y")
        front.append(jnp.concatenate(parts[: side // 2], 1))
        gate.append(jnp.concatenate(parts[side // 2 :], 1)[:rows])
        made = convolved(front[h], same, conv_taps[h], bias_conv[h], wide)
        conv_sum.append(made[0])
        inner.append(made[1])
    select = sum(dot(inner[h], select_full[h], ((1,), (0,))) for h in both)
    steps_low = select[:, :R].astype(BF16)
    in_select = select[:, R : R + NS]
    out_select = select[:, R + NS :]
    step_pre = [dot(steps_low, step_full[h], ((1,), (1,))) + bias_step[h] for h in both]
    delta = [jax.nn.softplus(p) for p in step_pre]
    driven = [d * x.astype(F32) for d, x in zip(delta, inner)]
    rate = [r * math.log2(math.e) for r in decay_rate]

    ends = [
        segment_ends(delta[h], driven[h], kept, in_select, rate[h], False, wide) for h in both
    ]
    pre = [e[:2] for e in ends]
    state_in = entering([e[2] for e in ends], [e[3] for e in ends], False)
    scanned, gated = zip(
        *(
            scan_output(
                delta[h], driven[h], inner[h], gate[h], kept, in_select, out_select, rate[h],
                skip_wide[h], pre[h], state_in[h], wide,
            )
            for h in both
        )
    )
    mixed = sum(dot(gated[h], out_full[h], ((1,), (0,))) for h in both)
    resid = stream + mixed
    inv_second = lax.rsqrt(jnp.mean(resid * resid, -1, keepdims=True) + EPS)
    hat_second = resid * inv_second
    normed_moe = (hat_second * gains_all[1]).astype(BF16)
    normed_wide = normed_moe.astype(F32)
    logits = dot(normed_wide, router_all, ((1,), (1,)), HIGHEST)
    probs = jax.nn.softmax(logits, -1)
    route_hot = route[:, None] == jnp.arange(EXPERT_COUNT, dtype=jnp.int32)[None, :]
    hot_wide = route_hot.astype(F32)
    chosen = jnp.sum(probs * hot_wide, 1, keepdims=True)
    place = jnp.arange(rows, dtype=jnp.int32)
    lower = (place[:, None] >= place[None, :]).astype(BF16)
    rank_in = dot(lower, route_hot.astype(BF16), ((1,), (0,))) - 1.0
    slot = jnp.sum(rank_in * hot_wide, 1).astype(jnp.int32)
    target = jnp.where(route == core, 0, slots_per) + slot
    pick = (jnp.arange(slots, dtype=jnp.int32)[:, None] == target[None, :]).astype(BF16)
    returned_grad = (chosen * out_cot).astype(BF16)
    placed = dot(pick, jnp.concatenate([normed_moe, returned_grad], 1), ((1,), (0,))).astype(BF16)
    placed = jnp.concatenate([placed[:slots_per], moved(placed[slots_per:], "core")])
    buffer, grad_slots = placed[:, :MODEL_WIDTH], placed[:, MODEL_WIDTH:]

    def from_slots(parts):
        parts = jnp.concatenate([parts[:slots_per], moved(parts[slots_per:], "core")])
        return dot(pick.astype(F32), parts, ((0,), (0,)), HIGHEST)

    gated_other = moved(gated[1], "core")
    returned, buffer_grad, expert_grads = expert_pass(core, buffer, grad_slots, experts, depth)
    returned = from_slots(returned)
    buffer_grad = from_slots(buffer_grad)
    branch = chosen * returned
    layer_out = (resid + branch).astype(BF16)
    squared_values = jnp.stack(
        [jnp.sum(resid * resid), jnp.sum(mixed * mixed), jnp.sum(branch * branch)]
    )
    chosen_grad = jnp.sum(out_cot * returned, 1, keepdims=True)
    logit_grad = chosen_grad * chosen * (hot_wide - probs)
    grad_router = dot(logit_grad, normed_wide, ((0,), (0,)), HIGHEST)
    moe_grad = buffer_grad + dot(logit_grad, router_all, ((1,), (0,)), HIGHEST)
    second_gain_grad = jnp.sum(moe_grad * hat_second, 0)
    scaled_second = moe_grad * gains_all[1]
    resid_grad = out_cot + inv_second * (
        scaled_second - hat_second * jnp.mean(scaled_second * hat_second, -1, keepdims=True)
    )
    mixed_grad = resid_grad.astype(BF16)
    crossed = moved(jnp.concatenate([mixed_grad, normed]), "core")
    gated_near = jnp.concatenate([gated[0], gated_other])
    grad_out = dot(gated_near, jnp.concatenate([mixed_grad, crossed[:rows]]), ((0,), (0,)))
    gated_grad = [dot(mixed_grad, out_full[h], ((1,), (1,))) for h in both]
    gates = [g.astype(F32) for g in gate]
    scan_grad = [gated_grad[h] * jax.nn.silu(gates[h]) for h in both]
    gate_grad = [(gated_grad[h] * scanned[h] * silu_slope(gates[h])).astype(BF16) for h in both]
    ends = [
        segment_ends(delta[h], scan_grad[h], kept, out_select, rate[h], True, wide) for h in both
    ]
    post = [e[:2] for e in ends]
    adjoint_in = entering([e[2] for e in ends], [e[3] for e in ends], True)
    groups = [list(range(c, lax.axis_size("dp"), 2)) for c in range(2)]
    out_rows = plane_rows(grad_out.astype(BF16))
    unit = out_rows.shape[1]
    out_rows = jnp.pad(out_rows, ((0, 0), (0, expert_grads.shape[2] - unit), (0, 0)))
    both_sum = lax.dynamic_update_slice(expert_grads, out_rows[:, None], (0, 4, 0, 0))
    both_sum = lax.psum_scatter(
        both_sum, "dp", scatter_dimension=0, tiled=True, axis_index_groups=groups
    )
    both_sum = lax.psum_scatter(both_sum, "seq", scatter_dimension=0, tiled=True)[0]
    out_sum = lax.ppermute(both_sum[4, :unit], BOTH, [(b, a) for a, b in unit_pairs()])
    out_sum = out_sum.astype(F32)
    expert_sum = both_sum[:4].reshape(2, 2, -1, MODEL_WIDTH)
    mine_sum = jnp.where(core == 0, expert_sum[0], expert_sum[1])
    other_sum = moved(jnp.where(core == 0, expert_sum[1], expert_sum[0]), "core")
    expert_sum = jnp.stack(
        [jnp.where(core == e, mine_sum, other_sum) for e in range(EXPERT_COUNT)]
    ).astype(F32)
    made = [
        scan_adjoint(
            delta[h], driven[h], inner[h], scan_grad[h], step_pre[h], kept, in_select, out_select,
            rate[h], skip_wide[h], pre[h], state_in[h], post[h], adjoint_in[h], wide,
        )
        for h in both
    ]
    pre_low, inner_part, rate_sum, step_sum, skip_sum, in_grad, out_grads = map(list, zip(*made))
    steps_grad = sum(dot(pre_low[h], step_full[h], ((1,), (0,))) for h in both)
    select_low = jnp.concatenate(
        [steps_grad, in_grad[0] + in_grad[1], out_grads[0] + out_grads[1]], 1
    ).astype(BF16)
    front_grad, early, tap_sums = zip(
        *(
            convolved_back(
                front[h], same, conv_taps[h], conv_sum[h], inner_part[h], select_low,
                select_full[h], wide,
            )
            for h in both
        )
    )
    grad_small = []
    for h in both:
        lines = [rate_sum[h] * decay_rate[h], tap_sums[h][: KC + 1], step_sum[h], skip_sum[h]]
        grad_small.append(
            jnp.concatenate(
                [
                    dot(inner[h], select_low, ((0,), (0,))),
                    dot(pre_low[h], steps_low, ((0,), (0,))),
                    dot(jnp.concatenate(lines).astype(BF16), unit_lines, ((0,), (0,))),
                    jnp.zeros((half, -columns % LANE), F32),
                ],
                1,
            ).astype(BF16)
        )
    proj_grad = []
    for h in both:
        incoming = passed_along(early[h].reshape(REACH, SEG, half)[:, 0], "seq", -1)
        tail = jnp.pad(incoming[:, None], ((0, 0), (SEG - 1, 0), (0, 0)))
        tail = jnp.pad(tail.reshape(REACH * SEG, half), ((rows - REACH * SEG, 0), (0, 0)))
        whole = jnp.concatenate([(front_grad[h] + tail).astype(BF16), gate_grad[h]], 1)
        parts = [whole[:, k * strip : (k + 1) * strip] for k in range(side)]
        proj_grad.append(jnp.concatenate(by_place(parts, "y"), 1))
    proj_other = moved(proj_grad[1], "core")
    grad_in = dot(
        jnp.concatenate([proj_grad[0], proj_other]),
        jnp.concatenate([normed, crossed[rows:]]),
        ((0,), (0,)),
    ).astype(BF16)
    parts, width = lax.axis_size("dp"), MODEL_WIDTH // lax.axis_size("dp")
    unit = DI // (parts * depth)
    shared = jnp.concatenate([second_gain_grad[None], grad_router]).astype(BF16)
    shared = shared.reshape(3, parts, width).swapaxes(0, 1).reshape(parts, 1, 3 * width)
    extra = -(-3 * width // unit)
    shared = jnp.pad(shared, ((0, 0), (0, 0), (0, extra * unit - 3 * width)))
    shared = jnp.broadcast_to(shared, (parts, depth, extra * unit)).reshape(DI, extra)
    whole = unit_blocks(jnp.concatenate(grad_small), True)
    shared = jnp.pad(shared, ((0, 0), (columns, whole.shape[1] - columns - extra)))
    small_near = units_from_order(whole + shared)
    in_plane = grad_in.reshape(side, side, depth, -1, MODEL_WIDTH)
    cut = cut_of(MODEL_WIDTH + LANE)
    right = jnp.concatenate([in_plane[..., cut:], small_near], -1)
    in_plane = first_scatter(in_plane[..., :cut], right.swapaxes(0, 1))
    in_last = second_scatter(*in_plane)
    in_total = ring_scatter(in_last, "z", True).astype(F32)
    in_sum = in_total[:, :MODEL_WIDTH]
    small_sum = jnp.concatenate(jnp.split(in_total[:, MODEL_WIDTH:], 2), 1)
    line_sum = small_sum[:, at + R : columns]
    shared = small_sum[:, columns : columns + extra].reshape(-1)[: 3 * width].reshape(3, width)
    proj_grad = [after(p, grad_in) for p in proj_grad]
    normed_grad = sum(dot(proj_grad[h], in_full[h], ((1,), (0,))) for h in both)
    first_gain_grad = jnp.sum(normed_grad * hat_first, 0)
    scaled_first = normed_grad * gains_all[0]
    stream_grad = resid_grad + inv_first * (
        scaled_first - hat_first * jnp.mean(scaled_first * hat_first, -1, keepdims=True)
    )

    last = jnp.stack([first_gain_grad, jnp.pad(squared_values, (0, MODEL_WIDTH - 3))])
    last = everywhere(after(last, in_plane[0]))
    first_part = lax.dynamic_slice_in_dim(last[:1], lax.axis_index("dp") * width, width, 1)
    stats = jnp.sqrt(last[1, :3] / (rows * parts * depth * MODEL_WIDTH))
    return (
        in_order(layer_out)[None],
        in_order(stream_grad.astype(BF16))[None],
        jnp.concatenate([first_part, shared[:1]]),
        in_sum.T,
        line_sum[:, NS : NS + KC].T,
        line_sum[:, NS + KC],
        small_sum[:, :at],
        small_sum[:, at : at + R].T,
        line_sum[:, NS + KC + 1],
        line_sum[:, :NS],
        line_sum[:, NS + KC + 2],
        out_sum,
        shared[1:].T,
        expert_sum[:, 0].swapaxes(1, 2),
        expert_sum[:, 1],
        stats,
    )


def solution(mesh):
    return jax.shard_map(
        per_device,
        mesh=mesh,
        in_specs=(
            P("dp", "seq", None),
            P("dp", "seq"),
            P("dp", "seq", None),
            P("dp", "seq", None),
            P(None, "dp"),
            P(None, ("dp", "seq")),
            P(None, ("dp", "seq")),
            P(("dp", "seq")),
            P(("dp", "seq"), None),
            P(None, ("dp", "seq")),
            P(("dp", "seq")),
            P(("dp", "seq"), None),
            P(("dp", "seq")),
            P(("dp", "seq"), None),
            P("dp", None),
            P(None, None, ("dp", "seq")),
            P(None, ("dp", "seq"), None),
        ),
        out_specs=(
            P("dp", "seq", None),
            P("dp", "seq", None),
            P(None, "dp"),
            P(None, ("dp", "seq")),
            P(None, ("dp", "seq")),
            P(("dp", "seq")),
            P(("dp", "seq"), None),
            P(None, ("dp", "seq")),
            P(("dp", "seq")),
            P(("dp", "seq"), None),
            P(("dp", "seq")),
            P(("dp", "seq"), None),
            P("dp", None),
            P(None, None, ("dp", "seq")),
            P(None, ("dp", "seq"), None),
            P(),
        ),
        check_vma=False,
    )
```
